32 devices in a mesh: dp: 8 (over y, x, core), tensor: 4 (over z).
Axes of the slice: x: 2, y: 2, z: 4, core: 2. Of those that a mesh axis runs over, the one named last changes fastest.
Arguments:
- inputs: bfloat16 [1024, 16, 1024], P('tensor', 'dp'), may hold values from -6 to 6
- cotangent: bfloat16 [1024, 16, 1024], P('tensor', 'dp'), may hold values from -6 to 6
- lengths: int32 [16], replicated, may hold values from 128 to 1024, as said below
- dealing: int32 [16], replicated, may hold values from 0 to 15, as said below
- undealing: int32 [16], replicated, may hold values from 0 to 15, as said below
- query_weight: float32 [1024, 1024], P('dp', 'tensor'), may hold values from -0.1875 to 0.1875
- key_weight: float32 [1024, 1024], P('dp', 'tensor'), may hold values from -0.1875 to 0.1875
- value_weight: float32 [1024, 1024], P('dp', 'tensor'), may hold values from -0.1875 to 0.1875
- output_weight: float32 [1024, 1024], P('tensor', 'dp'), may hold values from -3 to 3
- up_weight: float32 [1024, 4096], P('dp', 'tensor'), may hold values from -0.1875 to 0.1875
- down_weight: float32 [4096, 1024], P('tensor', 'dp'), may hold values from -0.09375 to 0.09375
- query_bias: float32 [1024], P('tensor'), may hold values from -3 to 3
- value_bias: float32 [1024], P('tensor'), may hold values from -3 to 3
- output_bias: float32 [1024], replicated, may hold values from -3 to 3
- up_bias: float32 [4096], P('tensor'), may hold values from -3 to 3
- down_bias: float32 [1024], replicated, may hold values from -3 to 3
- first_gain: float32 [1024], replicated, may hold values from 0.25 to 1.75
- first_shift: float32 [1024], replicated, may hold values from -3 to 3
- second_gain: float32 [1024], replicated, may hold values from 0.25 to 1.75
- second_shift: float32 [1024], replicated, may hold values from -3 to 3
Outputs:
- layer_output: bfloat16 [1024, 16, 1024], P('tensor', 'dp')
- input_grad: bfloat16 [1024, 16, 1024], P('tensor', 'dp')
- query_weight_grad: float32 [1024, 1024], P('dp', 'tensor')
- key_weight_grad: float32 [1024, 1024], P('dp', 'tensor')
- value_weight_grad: float32 [1024, 1024], P('dp', 'tensor')
- output_weight_grad: float32 [1024, 1024], P('tensor', 'dp')
- up_weight_grad: float32 [1024, 4096], P('dp', 'tensor')
- down_weight_grad: float32 [4096, 1024], P('tensor', 'dp')
- query_bias_grad: float32 [1024], P('tensor')
- value_bias_grad: float32 [1024], P('tensor')
- output_bias_grad: float32 [1024], replicated
- up_bias_grad: float32 [4096], P('tensor')
- down_bias_grad: float32 [1024], replicated
- first_gain_grad: float32 [1024], replicated
- first_shift_grad: float32 [1024], replicated
- second_gain_grad: float32 [1024], replicated
- second_shift_grad: float32 [1024], replicated
The draws below stay inside these ranges and needn't reach their ends.
Inputs may be any that keep to these rules, and one draw needn't show every extreme that they name: `lengths`: 8 or more sequences have exactly 1024 tokens. `dealing`: a permutation of the sequences; dealt slot s belongs to dp index s // 2, and every dp index is dealt a sequence of 1024 tokens. undealing[dealing[s]] = s for every slot s.
All inputs are finite; a program needn't handle non-finite values.
Results may differ from the reference program's by a relative error of at most 0.022.
Values may be sent and summed in bfloat16 or wider, within the bound.
A program may use at most 192 MiB of HBM per device.

```python
import jax
import jax.numpy as jnp
from jax import lax

D = 1024
HEADS = 16
HEAD_DIM = 64
FF = 4096
SEQ_LEN = 1024
MIN_LEN = 128
SEQ_DEV = 2
SEQS = 16
N_TENSOR = 4


def dealt_lengths(key):
    first, second, third = jax.random.split(key, 3)
    devices = SEQS // SEQ_DEV
    seq_lengths = jax.random.randint(first, (SEQS,), MIN_LEN, SEQ_LEN + 1)
    chosen = jax.random.permutation(second, SEQS)[:devices]
    seq_lengths = seq_lengths.at[chosen].set(SEQ_LEN)
    tiebreak = jax.random.permutation(third, SEQS)
    ranking = jnp.argsort(-(seq_lengths * SEQS + tiebreak), stable=True)
    slot_index = jnp.arange(SEQS)
    holder = slot_index // SEQ_DEV
    rounds = slot_index % SEQ_DEV
    position = rounds * devices + jnp.where(rounds % 2 == 0, holder, devices - 1 - holder)
    dealing = jnp.take(ranking, position).astype(jnp.int32)
    undealing = jnp.zeros((SEQS,), jnp.int32).at[dealing].set(slot_index.astype(jnp.int32))
    return (seq_lengths.astype(jnp.int32), dealing, undealing)


def draw_lengths(key, part):
    shared = dealt_lengths(key)
    return shared[0]


def draw_dealing(key, part):
    shared = dealt_lengths(key)
    return shared[1]


def draw_undealing(key, part):
    shared = dealt_lengths(key)
    return shared[2]


def block_levels(rng, dims, shards, least, top_value):
    loudness, own = 1.0, jax.random.fold_in(rng, 6)
    for dim, parts in shards:
        steps = jnp.exp(jax.random.uniform(jax.random.fold_in(own, dim), (parts,), jnp.float32, least / len(shards), top_value / len(shards)))
        loudness = loudness * jnp.repeat(steps, dims[dim] // parts).reshape([-1 if axis == dim else 1 for axis in range(len(dims))])
    return loudness


def centred(key, extent, deviation, bound, cuts=(), held_as=jnp.bfloat16):
    values = jax.random.normal(key, extent, jnp.float32) * deviation
    if len(cuts) > 0:
        values = block_levels(key, extent, cuts, -0.22, 0.18) * values
    return jnp.clip(values, min=-bound, max=bound).astype(held_as)


def setup_inputs(seed: int = 0) -> dict:
    keys = jax.random.split(jax.random.key(seed), 21)
    inputs = centred(keys[0], (SEQ_LEN, SEQS, D), 1.0, 6.0, ((0, 4), (1, 8)))
    cotangent = centred(keys[1], (SEQ_LEN, SEQS, D), 1.0, 6.0, ((0, 4), (1, 8)))
    lengths = draw_lengths(jax.random.fold_in(keys[20], 71), 0)
    dealing = draw_dealing(jax.random.fold_in(keys[20], 71), 0)
    undealing = draw_undealing(jax.random.fold_in(keys[20], 71), 0)
    query_weight = centred(keys[5], (D, D), D ** -0.5, 0.1875, ((0, 8), (1, 4)), jnp.float32)
    key_weight = centred(keys[6], (D, D), D ** -0.5, 0.1875, ((0, 8), (1, 4)), jnp.float32)
    value_weight = centred(keys[7], (D, D), D ** -0.5, 0.1875, ((0, 8), (1, 4)), jnp.float32)
    output_weight = centred(keys[8], (D, D), (max(D // 256, 1)) ** -0.5, 3.0, ((0, 4), (1, 8)), jnp.float32)
    up_weight = centred(keys[9], (D, FF), D ** -0.5, 0.1875, ((0, 8), (1, 4)), jnp.float32)
    down_weight = centred(keys[10], (FF, D), FF ** -0.5, 0.09375, ((0, 4), (1, 8)), jnp.float32)
    query_bias = centred(keys[11], (D,), 0.5, 3.0, ((0, 4),), jnp.float32)
    value_bias = centred(keys[12], (D,), 0.5, 3.0, ((0, 4),), jnp.float32)
    output_bias = centred(keys[13], (D,), 0.5, 3.0, (), jnp.float32)
    up_bias = centred(keys[14], (FF,), 0.5, 3.0, ((0, 4),), jnp.float32)
    down_bias = centred(keys[15], (D,), 0.5, 3.0, (), jnp.float32)
    first_gain = jnp.clip(1.0 + 0.15 * jax.random.normal(keys[16], (D,), jnp.float32), 0.25, 1.75)
    first_shift = centred(keys[17], (D,), 0.5, 3.0, (), jnp.float32)
    second_gain = jnp.clip(1.0 + 0.15 * jax.random.normal(keys[18], (D,), jnp.float32), 0.25, 1.75)
    second_shift = centred(keys[19], (D,), 0.5, 3.0, (), jnp.float32)
    return dict(inputs=inputs, cotangent=cotangent, lengths=lengths, dealing=dealing, undealing=undealing, query_weight=query_weight, key_weight=key_weight, value_weight=value_weight, output_weight=output_weight, up_weight=up_weight, down_weight=down_weight, query_bias=query_bias, value_bias=value_bias, output_bias=output_bias, up_bias=up_bias, down_bias=down_bias, first_gain=first_gain, first_shift=first_shift, second_gain=second_gain, second_shift=second_shift)


@jax.custom_vjp
def low(v):
    return lax.optimization_barrier(v.astype(jnp.bfloat16)).astype(jnp.float32)

@jax.custom_vjp
def low_back(v):
    return v

def low_keep(v):
    return (low(v), None)

def low_pass(kept, grad):
    return (grad,)

def back_keep(v):
    return (v, None)

def back_low(kept, grad):
    return (low(grad),)
low.defvjp(low_keep, low_pass)
low_back.defvjp(back_keep, back_low)
highest = lax.Precision.HIGHEST

def matmul(left_side, right_side):
    return jnp.dot(left_side, right_side, precision=highest, preferred_element_type=jnp.float32)

def normalize(hidden, norm_gain, norm_shift):
    center = hidden - lax.optimization_barrier(jnp.mean(hidden, axis=-1, keepdims=True))
    spread = lax.optimization_barrier(jnp.mean(center * center, axis=-1, keepdims=True))
    return center * lax.rsqrt(spread + 1e-05) * norm_gain + norm_shift

def attend(pieces):
    query_seq, key_seq, value_seq, length = pieces
    scores = jnp.einsum('qhe,khe->hqk', query_seq, key_seq, precision=highest)
    scores = low_back(scores)
    visible = jnp.arange(query_seq.shape[0]) < length
    scores = jnp.where(visible[None, None, :], scores, -1000000000.0)
    summit = lax.optimization_barrier(jnp.max(scores, axis=-1, keepdims=True))
    raised = jnp.exp(scores - summit)
    prob_rows = low(raised / lax.optimization_barrier(jnp.sum(raised, axis=-1, keepdims=True)))
    return jnp.einsum('hqk,khe->qhe', prob_rows, value_seq, precision=highest)

def grouped_sum(left_side, right_side):
    width = left_side.shape[1] // N_TENSOR
    total = jnp.zeros((left_side.shape[0], right_side.shape[1]), jnp.float32)
    for group in range(N_TENSOR):
        total = total + low(matmul(left_side[:, group * width:(group + 1) * width], right_side[group * width:(group + 1) * width]))
    return total

def reference(inputs, cotangent, lengths, dealing, undealing, query_weight, key_weight, value_weight, output_weight, up_weight, down_weight, query_bias, value_bias, output_bias, up_bias, down_bias, first_gain, first_shift, second_gain, second_shift):
    full_span, seqs_all, model_width = inputs.shape
    seq_lengths = jnp.take(lengths, dealing)
    dealt_rows = jnp.take(inputs, dealing, axis=1).astype(jnp.float32)
    rows_valid = (jnp.arange(full_span)[:, None] < seq_lengths[None, :]).astype(jnp.float32)

    def heads_first(flat_rows):
        return jnp.transpose(flat_rows.reshape(full_span, seqs_all, HEADS, HEAD_DIM), (1, 0, 2, 3))

    def layer(source, params):
        w_query, w_key, w_value, w_out, w_up, w_down, b_query, b_value, b_out, b_up, b_down, gain_a, shift_a, gain_b, shift_b = params
        flat_rows = source.reshape(full_span * seqs_all, model_width)
        low_query, low_key, low_value = (low(w_query), low(w_key), low(w_value))
        head_width = model_width // N_TENSOR
        query_parts, key_parts, value_parts = ([], [], [])
        for group in range(N_TENSOR):
            group_rows = low_back(flat_rows)
            columns = slice(group * head_width, (group + 1) * head_width)
            query_parts.append(matmul(group_rows, low_query[:, columns]))
            key_parts.append(matmul(group_rows, low_key[:, columns]))
            value_parts.append(matmul(group_rows, low_value[:, columns]))
        query_rows = low(low_back((jnp.concatenate(query_parts, axis=1) + b_query) * 0.125))
        key_rows = low(low_back(jnp.concatenate(key_parts, axis=1)))
        value_rows = low(low_back(jnp.concatenate(value_parts, axis=1) + b_value))
        attended = lax.map(jax.checkpoint(attend), (heads_first(query_rows), heads_first(key_rows), heads_first(value_rows), seq_lengths))
        attn_mixed = jnp.transpose(attended, (1, 0, 2, 3)).reshape(full_span * seqs_all, model_width)
        attn_mixed = low(low_back(attn_mixed))
        branch = low_back(grouped_sum(attn_mixed, low(w_out)) + b_out)
        hidden_one = normalize(flat_rows + branch, gain_a, shift_a)
        hidden_low = low(hidden_one)
        low_up = low(w_up)
        unit_width = low_up.shape[1] // N_TENSOR
        up_parts = []
        for group in range(N_TENSOR):
            up_parts.append(matmul(low_back(hidden_low), low_up[:, group * unit_width:(group + 1) * unit_width]))
        expanded = low_back(jnp.concatenate(up_parts, axis=1) + b_up)
        activated = low(jax.nn.gelu(expanded, approximate=False))
        branch_two = low_back(grouped_sum(activated, low(w_down)) + b_down)
        result = normalize(hidden_one + branch_two, gain_b, shift_b)
        return result.reshape(full_span, seqs_all, model_width)
    params = (query_weight.astype(jnp.float32), key_weight.astype(jnp.float32), value_weight.astype(jnp.float32), output_weight.astype(jnp.float32), up_weight.astype(jnp.float32), down_weight.astype(jnp.float32), query_bias.astype(jnp.float32), value_bias.astype(jnp.float32), output_bias.astype(jnp.float32), up_bias.astype(jnp.float32), down_bias.astype(jnp.float32), first_gain.astype(jnp.float32), first_shift.astype(jnp.float32), second_gain.astype(jnp.float32), second_shift.astype(jnp.float32))
    result, pullback = jax.vjp(layer, dealt_rows, params)
    seed_grad = cotangent.astype(jnp.float32) * rows_valid[:, :, None]
    grad_input, grad_params = pullback(seed_grad)
    layer_output = jnp.take(result, undealing, axis=1).astype(jnp.bfloat16)
    input_grad = jnp.take(grad_input, undealing, axis=1).astype(jnp.bfloat16)
    return (layer_output, input_grad, grad_params[0], grad_params[1], grad_params[2], grad_params[3], grad_params[4], grad_params[5], grad_params[6], grad_params[7], grad_params[8], grad_params[9], grad_params[10], grad_params[11], grad_params[12], grad_params[13], grad_params[14])
```

```python
import functools

import jax
import jax.numpy as jnp
from jax import lax
from jax.experimental import pallas as pl
from jax.experimental.pallas import tpu as pltpu
from jax.sharding import PartitionSpec as P

HEAD_DIM = 64
KINDS = 3
MESH = pl.DeviceIdType.MESH
VMEM_LIMIT = 60 << 20
BF = jnp.bfloat16
F32 = jnp.float32


def flip(index, bit):
    unit = 1 << bit
    return index + unit * (1 - 2 * lax.rem(lax.div(index, unit), 2))


def orders(bits):
    return (tuple(range(bits)), tuple(reversed(range(bits))))


def relative(chip, order, code):
    for place, bit in enumerate(order):
        if code >> place & 1:
            chip = flip(chip, bit)
    return chip


def place():
    d, t = lax.axis_index("dp"), lax.axis_index("tensor")
    return d, t, lax.div(d, 2), lax.rem(d, 2)


def greet(n_dp, n_tensor):
    d, t, _, _ = place()
    barrier = pltpu.get_barrier_semaphore()
    me = d * n_tensor + t
    count = n_dp * n_tensor

    def one(step, carry):
        other = lax.rem(me + step, count)
        pl.semaphore_signal(
            barrier,
            inc=1,
            device_id=(lax.div(other, n_tensor), lax.rem(other, n_tensor)),
            device_id_type=MESH,
        )
        return carry

    lax.fori_loop(1, count, one, 0)
    pl.semaphore_wait(barrier, count - 1)


def remote(src, dst, ssem, rsem, device):
    return pltpu.make_async_remote_copy(
        src_ref=src,
        dst_ref=dst,
        send_sem=ssem,
        recv_sem=rsem,
        device_id=device,
        device_id_type=MESH,
    )


def landed(ref, sem):
    pltpu.make_async_copy(ref, ref, sem).wait()


def send_or_keep(mine, src, dst, ssem, rsem, device):
    @pl.when(mine)
    def _():
        pltpu.make_async_copy(src, dst, rsem).start()

    @pl.when(jnp.logical_not(mine))
    def _():
        remote(src, dst, ssem, rsem, device).start()


def sent(mine, src, ssem):
    @pl.when(jnp.logical_not(mine))
    def _():
        landed(src, ssem)


def gather_kernel(
    n_dp,
    n_tensor,
    undealing,
    x_ref,
    cot_ref,
    shard_ref,
    xl_ref,
    cl_ref,
    full_ref,
    c_one,
    c_two,
    x_s,
    x_r,
    c1_s,
    c1_r,
    c2_s,
    c2_r,
    own_sem,
    z_s,
    z_r,
    xy_s,
    xy_r,
    sib_s,
    sib_r,
):
    d, t, chip, core = place()
    chips = n_dp // 2
    bits = chips.bit_length() - 1
    half_t = n_tensor // 2
    rows, cols = shard_ref.shape[1:]
    half_cols = cols // 2
    prow, pcol = c_one.shape[2:]
    n_col = cot_ref.shape[2] // pcol
    greet(n_dp, n_tensor)

    def block(k, tt, who, half):
        return full_ref.at[k, tt, who, core, :, pl.ds(half * half_cols, half_cols)]

    for k in range(KINDS):
        pltpu.make_async_copy(shard_ref.at[k], full_ref.at[k, t, chip, core], own_sem.at[k]).start()
        for step in range(1, n_tensor):
            remote(
                shard_ref.at[k],
                full_ref.at[k, t, chip, core],
                z_s.at[k, step],
                z_r.at[k, t],
                (d, lax.rem(t + step, n_tensor)),
            ).start()
    for s in range(2):
        send_or_keep(
            (lax.div(t, half_t) == core) & (2 * core + s == t),
            x_ref.at[s],
            xl_ref.at[lax.rem(t, half_t)],
            x_s.at[s],
            x_r.at[lax.rem(t, half_t)],
            (2 * chip + lax.div(t, half_t), 2 * core + s),
        )

    def piece(who):
        return cot_ref.at[
            :,
            pl.ds(pl.multiple_of(lax.div(who, n_col) * prow, prow), prow),
            pl.ds(pl.multiple_of(lax.rem(who, n_col) * pcol, pcol), pcol),
        ]

    pltpu.make_async_copy(piece(d), c_one.at[d], c1_r.at[0]).start()
    for step in range(1, n_dp):
        who = lax.rem(d + step, n_dp)
        remote(piece(who), c_one.at[d], c1_s.at[step], c1_r.at[step], (who, t)).start()

    def forward(k, tt, half, code):
        order = orders(bits)[half]
        chip_here = relative(chip, order, code)
        ref = block(k, tt, chip_here, half)
        for s in range(code.bit_length(), bits):
            target = code | 1 << s
            remote(
                ref,
                ref,
                xy_s.at[k, tt, half, target],
                xy_r.at[k, tt, half, target],
                (2 * flip(chip, order[s]) + core, t),
            ).start()
        remote(
            ref, ref, sib_s.at[k, tt, half, code], sib_r.at[k, tt, half, code], (d + 1 - 2 * core, t)
        ).start()

    def cot_second():
        for step in range(n_dp):
            landed(c_one.at[0], c1_r.at[step])
        count = 2 * n_dp
        for step in range(count):
            seq = lax.rem(4 * chip + step, count)
            slot = undealing[seq]
            c_two[seq] = c_one[lax.div(slot, 2), lax.rem(slot, 2)]
            goal = 2 * lax.div(seq, 4) + lax.div(t, half_t)
            send_or_keep(
                (goal == d) & (lax.rem(seq, 4) == t),
                c_two.at[seq],
                cl_ref.at[lax.rem(t, half_t), d],
                c2_s.at[step],
                c2_r.at[lax.rem(t, half_t), d],
                (goal, lax.rem(seq, 4)),
            )

    for k in range(KINDS):
        landed(shard_ref.at[k], own_sem.at[k])
        for step in range(n_tensor):
            tt = lax.rem(t + step, n_tensor)
            if step:
                landed(shard_ref.at[k], z_r.at[k, tt])
            for half in range(2):
                forward(k, tt, half, 0)
        if k == 0:
            cot_second()
        for code in range(1, chips):
            for step in range(n_tensor):
                tt = lax.rem(t + step, n_tensor)
                for half in range(2):
                    landed(block(k, tt, chip, half), xy_r.at[k, tt, half, code])
                    forward(k, tt, half, code)

    for k in range(KINDS):
        for step in range(1, n_tensor):
            landed(shard_ref.at[k], z_s.at[k, step])
        for step in range(n_tensor):
            tt = lax.rem(t + step, n_tensor)
            for half in range(2):
                for code in range(chips):
                    ref = block(k, tt, chip, half)
                    landed(ref, sib_r.at[k, tt, half, code])
                    landed(ref, sib_s.at[k, tt, half, code])
                    if code:
                        landed(ref, xy_s.at[k, tt, half, code])
    for s in range(2):
        sent((lax.div(t, half_t) == core) & (2 * core + s == t), x_ref.at[s], x_s.at[s])
        landed(x_ref.at[s], x_r.at[s])
    for step in range(1, n_dp):
        landed(c_one.at[0], c1_s.at[step])
    for step in range(2 * n_dp):
        seq = lax.rem(4 * chip + step, 2 * n_dp)
        goal = 2 * lax.div(seq, 4) + lax.div(t, half_t)
        sent((goal == d) & (lax.rem(seq, 4) == t), c_two.at[0], c2_s.at[step])
    for q in range(half_t):
        for who in range(n_dp):
            landed(c_two.at[0], c2_r.at[q, who])


def gather(n_dp, n_tensor, undealing, x_in, cot_in, shard):
    slots, span, width = x_in.shape
    rows, cols = shard.shape[1:]
    chips = n_dp // 2
    n_pos = min(n_dp, span // 16)
    prow, pcol = span // n_pos, width // (n_dp // n_pos)
    dma = pltpu.SemaphoreType.DMA
    any_space = pl.BlockSpec(memory_space=pl.ANY)
    return pl.pallas_call(
        functools.partial(gather_kernel, n_dp, n_tensor),
        out_shape=(
            jax.ShapeDtypeStruct((2, span, width), BF),
            jax.ShapeDtypeStruct((2, n_dp, prow, pcol), BF),
            jax.ShapeDtypeStruct((KINDS, n_tensor, chips, 2, rows, cols), BF),
        ),
        in_specs=[pl.BlockSpec(memory_space=pltpu.SMEM), any_space, any_space, any_space],
        out_specs=(any_space, any_space, any_space),
        scratch_shapes=[
            pltpu.VMEM((n_dp, slots, prow, pcol), BF),
            pltpu.VMEM((2 * n_dp, prow, pcol), BF),
            dma((2,)),
            dma((2,)),
            dma((n_dp,)),
            dma((n_dp,)),
            dma((2 * n_dp,)),
            dma((n_tensor // 2, n_dp)),
            dma((KINDS,)),
            dma((KINDS, n_tensor)),
            dma((KINDS, n_tensor)),
            dma((KINDS, n_tensor, 2, chips)),
            dma((KINDS, n_tensor, 2, chips)),
            dma((KINDS, n_tensor, 2, chips)),
            dma((KINDS, n_tensor, 2, chips)),
        ],
        compiler_params=pltpu.CompilerParams(
            collective_id=0, has_side_effects=True, vmem_limit_bytes=VMEM_LIMIT
        ),
        name="gather_all",
    )(undealing, x_in, cot_in, shard)


def scatter_kernel(
    n_dp,
    n_tensor,
    grad_ref,
    bias_ref,
    y_ref,
    sum_ref,
    bias_out,
    y_out,
    from_core,
    held,
    from_chip,
    from_z,
    bias_in,
    y_s,
    y_r,
    b_s,
    b_r,
    bo_s,
    bo_r,
    own_sem,
    core_s,
    core_r,
    xy_s,
    xy_r,
    z_s,
    z_r,
    out_sem,
):
    d, t, chip, core = place()
    chips = n_dp // 2
    bits = chips.bit_length() - 1
    half_t = n_tensor // 2
    count = n_dp * n_tensor
    me = d * n_tensor + t
    rows, cols = grad_ref.shape[4:]
    half_cols = cols // 2
    pieces = KINDS * n_tensor
    greet(n_dp, n_tensor)

    def at(index):
        k = lax.div(index, n_tensor)
        return k, lax.rem(t + lax.rem(index, n_tensor), n_tensor)

    def begin(index, carry):
        k, tt = at(index)
        remote(
            grad_ref.at[k, tt, :, 1 - core],
            from_core.at[index],
            core_s.at[index],
            core_r.at[index],
            (d + 1 - 2 * core, t),
        ).start()
        pltpu.make_async_copy(grad_ref.at[k, tt, :, core], held.at[index], own_sem.at[index]).start()
        return carry

    lax.fori_loop(0, pieces, begin, 0)

    for a in range(y_ref.shape[0]):
        for q in range(2):
            send_or_keep(
                (lax.div(t, half_t) == core) & (2 * core + q == t),
                y_ref.at[a, q],
                y_out.at[a, lax.rem(t, half_t)],
                y_s.at[a, q],
                y_r.at[a, lax.rem(t, half_t)],
                (2 * chip + lax.div(t, half_t), 2 * core + q),
            )

    def device(index):
        return (lax.div(index, n_tensor), lax.rem(index, n_tensor))

    def bias_begin(step, carry):
        other = lax.rem(me + step, count)
        remote(
            bias_ref.at[other], bias_in.at[step], b_s.at[step], b_r.at[step], device(other)
        ).start()
        return carry

    lax.fori_loop(1, count, bias_begin, 0)
    pltpu.make_async_copy(bias_ref.at[me], bias_in.at[0], b_r.at[0]).start()

    def bias_middle():
        def arrive(step, total):
            landed(bias_in.at[0], b_r.at[step])
            return total + bias_in[step]

        total = lax.fori_loop(0, count, arrive, jnp.zeros(bias_in.shape[1:], F32))

        def leave(step, carry):
            landed(bias_in.at[0], b_s.at[step])
            return carry

        lax.fori_loop(1, count, leave, 0)
        bias_in[0] = total
        pltpu.make_async_copy(bias_in.at[0], bias_out.at[me], bo_r.at[0]).start()

        def spread(step, carry):
            other = lax.rem(me + step, count)
            remote(
                bias_in.at[0], bias_out.at[me], bo_s.at[step], bo_r.at[step], device(other)
            ).start()
            return carry

        lax.fori_loop(1, count, spread, 0)

    def bias_end():
        def last(step, carry):
            landed(bias_in.at[0], bo_r.at[step])
            return carry

        lax.fori_loop(0, count, last, 0)

        def gone(step, carry):
            landed(bias_in.at[0], bo_s.at[step])
            return carry

        lax.fori_loop(1, count, gone, 0)

    def pass_on(index, s):
        for half in range(2):
            order = orders(bits)[half]
            for code in range(1 << s, 2 << s):
                remote(
                    held.at[index, relative(chip, order, code), :, pl.ds(half * half_cols, half_cols)],
                    from_chip.at[index, half, code - 1],
                    xy_s.at[index, half, code],
                    xy_r.at[index, half, code],
                    (2 * flip(chip, order[s]) + core, t),
                ).start()

    def take_in(index, s):
        for half in range(2):
            order = orders(bits)[half]
            for code in range(1 << s, 2 << s):
                landed(from_chip.at[0, 0, 0], xy_r.at[index, half, code])
                spot = held.at[
                    index,
                    relative(chip, order, code - (1 << s)),
                    :,
                    pl.ds(half * half_cols, half_cols),
                ]
                spot[...] = (
                    spot[...].astype(F32) + from_chip[index, half, code - 1].astype(F32)
                ).astype(BF)

    def first(index):
        landed(held.at[0], own_sem.at[index])
        landed(held.at[0], core_r.at[index])

        def add(c, carry):
            held[index, c] = (held[index, c].astype(F32) + from_core[index, c].astype(F32)).astype(BF)
            return carry

        lax.fori_loop(0, chips, add, 0)
        if bits:
            pass_on(index, bits - 1)

    def finish(index):
        k, tt = at(index)
        step = lax.rem(index, n_tensor)

        @pl.when(step > 0)
        def _():
            remote(
                held.at[index, chip],
                from_z.at[k, step],
                z_s.at[k, step],
                z_r.at[k, step],
                (d, tt),
            ).start()

    def turn(it, carry):
        for stage in range(bits + 1):
            index = it - stage

            @pl.when((index >= 0) & (index < pieces))
            def _(stage=stage, index=index):
                if stage == 0:
                    first(index)
                else:
                    take_in(index, bits - stage)
                    if stage < bits:
                        pass_on(index, bits - stage - 1)
                if stage == bits:
                    finish(index)

        return carry

    lax.fori_loop(0, pieces + bits, turn, 0)
    bias_middle()

    for k in range(KINDS):
        total = held[k * n_tensor, chip].astype(F32)
        for step in range(1, n_tensor):
            landed(from_z.at[0, 0], z_r.at[k, step])
            total = total + from_z[k, step].astype(F32)
        sum_ref[k] = total

    def close(index, carry):
        landed(held.at[0], core_s.at[index])
        for half in range(2):
            for code in range(1, chips):
                landed(from_chip.at[0, 0, 0], xy_s.at[index, half, code])
        return carry

    lax.fori_loop(0, pieces, close, 0)
    for k in range(KINDS):
        for step in range(1, n_tensor):
            landed(from_z.at[0, 0], z_s.at[k, step])
    for a in range(y_ref.shape[0]):
        for q in range(2):
            sent((lax.div(t, half_t) == core) & (2 * core + q == t), y_ref.at[a, q], y_s.at[a, q])
            landed(y_ref.at[a, q], y_r.at[a, q])
    bias_end()


def scatter(n_dp, n_tensor, grads, bias, outs):
    rows, cols = grads.shape[4:]
    chips = n_dp // 2
    pieces = KINDS * n_tensor
    count = n_dp * n_tensor
    dma = pltpu.SemaphoreType.DMA
    any_space = pl.BlockSpec(memory_space=pl.ANY)
    return pl.pallas_call(
        functools.partial(scatter_kernel, n_dp, n_tensor),
        out_shape=(
            jax.ShapeDtypeStruct((KINDS, rows, cols), F32),
            jax.ShapeDtypeStruct(bias.shape, F32),
            jax.ShapeDtypeStruct(outs.shape, BF),
        ),
        in_specs=[any_space] * 3,
        out_specs=(pl.BlockSpec(memory_space=pltpu.VMEM), any_space, any_space),
        scratch_shapes=[
            pltpu.VMEM((pieces, chips, rows, cols), BF),
            pltpu.VMEM((pieces, chips, rows, cols), BF),
            pltpu.VMEM((pieces, 2, chips - 1, rows, cols // 2), BF),
            pltpu.VMEM((KINDS, n_tensor, rows, cols), BF),
            pltpu.VMEM(bias.shape, F32),
            dma((outs.shape[0], 2)),
            dma((outs.shape[0], 2)),
            dma((count,)),
            dma((count,)),
            dma((count,)),
            dma((count,)),
            dma((pieces,)),
            dma((pieces,)),
            dma((pieces,)),
            dma((pieces, 2, chips)),
            dma((pieces, 2, chips)),
            dma((KINDS, n_tensor)),
            dma((KINDS, n_tensor)),
            dma((1,)),
        ],
        compiler_params=pltpu.CompilerParams(
            collective_id=1, has_side_effects=True, vmem_limit_bytes=VMEM_LIMIT
        ),
        name="scatter_all",
    )(grads, bias, outs)


def normalize(hidden, norm_gain, norm_shift):
    center = hidden - jnp.mean(hidden, axis=-1, keepdims=True)
    spread = jnp.mean(center * center, axis=-1, keepdims=True)
    return center * lax.rsqrt(spread + 1e-05) * norm_gain + norm_shift


def gelu_exact(values):
    return jax.nn.gelu(values, approximate=False)


def mm(spec, left, right):
    return jnp.einsum(spec, left, right, preferred_element_type=F32)


def shards(
    n_dp,
    n_tensor,
    inputs,
    cotangent,
    lengths,
    dealing,
    undealing,
    query_weight,
    key_weight,
    value_weight,
    output_weight,
    up_weight,
    down_weight,
    query_bias,
    value_bias,
    output_bias,
    up_bias,
    down_bias,
    first_gain,
    first_shift,
    second_gain,
    second_shift,
):
    span, slots, width = inputs.shape
    group = query_weight.shape[1]
    units = up_weight.shape[1]
    half = span * n_tensor // 2
    d, t, chip, core = place()
    length = lengths[2 * slots * chip + t]
    positions = core * half + jnp.arange(half)
    valid = (positions < length).astype(F32)

    shard = jnp.stack(
        [
            jnp.concatenate([query_weight, key_weight, value_weight, output_weight.T], axis=1),
            up_weight,
            down_weight.T,
        ]
    ).astype(BF)
    x_loc, cot_loc, full = gather(
        n_dp,
        n_tensor,
        undealing,
        jnp.transpose(inputs, (1, 0, 2)),
        jnp.transpose(cotangent, (1, 0, 2)),
        shard,
    )
    n_col = width // cot_loc.shape[3]
    cot = cot_loc.reshape(2, n_dp // n_col, n_col, *cot_loc.shape[2:])
    cot = jnp.transpose(cot, (0, 1, 3, 2, 4)).reshape(half, width)
    x = x_loc.reshape(half, width)
    full = full.reshape(KINDS, n_tensor, width, 4 * group)
    w_qkv = full[0][:, :, : 3 * group].reshape(n_tensor, width, 3, group)
    w_out = full[0][:, :, 3 * group :]
    w_up, w_down = full[1], full[2]

    bias_q = lax.all_gather(query_bias, "tensor", axis=0)
    bias_v = lax.all_gather(value_bias, "tensor", axis=0)
    bias_u = lax.all_gather(up_bias, "tensor", axis=0)

    def swap(values):
        other = lax.ppermute(values, "dp", [(i, i ^ 1) for i in range(n_dp)])
        return other

    def whole(values):
        other = swap(values)
        return jnp.concatenate(
            [jnp.where(core == 0, values, other), jnp.where(core == 0, other, values)], axis=0
        )

    qkv = mm("nm,tmjc->jntc", x, w_qkv)
    query = ((qkv[0] + bias_q) * 0.125).astype(BF)
    key = qkv[1].astype(BF)
    value = (qkv[2] + bias_v).astype(BF)
    heads = n_tensor * group // HEAD_DIM

    def split(values):
        return jnp.transpose(values.reshape(-1, heads, HEAD_DIM), (1, 0, 2))

    def join(values):
        return jnp.transpose(values, (1, 0, 2)).reshape(-1, n_tensor, group)

    q_h, k_h, v_h = split(query), split(whole(key)), split(whole(value))
    visible = jnp.arange(2 * half) < length

    def attend(one):
        q_one, k_one, v_one = one
        scores = jnp.where(visible, mm("qe,ke->qk", q_one, k_one), -1000000000.0)
        summit = jnp.max(scores, axis=-1, keepdims=True)
        raised = jnp.exp(scores - summit)
        total = jnp.sum(raised, axis=-1, keepdims=True)
        out = mm("qk,ke->qe", (raised / total).astype(BF), v_one)
        return out.astype(BF), (summit + jnp.log(total))[:, 0]

    attended, log_total = lax.map(attend, (q_h, k_h, v_h))
    mixed = join(attended)
    branch = mm("ntc,tmc->nm", mixed, w_out) + output_bias
    residual = x.astype(F32) + branch
    hidden_one, back_one = jax.vjp(normalize, residual, first_gain, first_shift)
    hidden_low = hidden_one.astype(BF)
    expanded = mm("nm,tmf->ntf", hidden_low, w_up) + bias_u
    activated = gelu_exact(expanded).astype(BF)
    branch_two = mm("ntf,tmf->nm", activated, w_down) + down_bias
    result, back_two = jax.vjp(normalize, hidden_one + branch_two, second_gain, second_shift)

    seed = cot.astype(F32) * valid[:, None]
    grad_two, gain_two, shift_two = back_two(seed)
    mlp_grad = grad_two.astype(BF)
    down_bias_grad = jnp.sum(mlp_grad, axis=0, dtype=F32)
    down_grad = mm("nm,ntf->tmf", mlp_grad, activated).astype(BF)
    act_grad = mm("nm,tmf->ntf", mlp_grad, w_down)
    expand_grad = jax.vjp(gelu_exact, expanded)[1](act_grad)[0].astype(BF)
    up_bias_grad = jnp.sum(expand_grad, axis=0, dtype=F32)
    up_grad = mm("nm,ntf->tmf", hidden_low, expand_grad).astype(BF)
    hidden_grad = grad_two + mm("ntf,tmf->nm", expand_grad, w_up)
    grad_one, gain_one, shift_one = back_one(hidden_grad)
    attn_grad = grad_one.astype(BF)
    output_bias_grad = jnp.sum(attn_grad, axis=0, dtype=F32)
    out_grad = mm("nm,ntc->tmc", attn_grad, mixed).astype(BF)
    mixed_grad = split(mm("nm,tmc->ntc", attn_grad, w_out).astype(BF))

    def attend_back(one):
        q_one, k_one, v_one, total, o_one = one
        scores = jnp.where(visible, mm("qe,ke->qk", q_one, k_one), -1000000000.0)
        probs = jnp.exp(scores - total[:, None])
        prob_grad = mm("qe,ke->qk", o_one, v_one)
        value_g = mm("qk,qe->ke", probs.astype(BF), o_one)
        inner = jnp.sum(probs * prob_grad, axis=-1, keepdims=True)
        score_grad = (probs * (prob_grad - inner)).astype(BF)
        query_g = mm("qk,ke->qe", score_grad, k_one)
        key_g = mm("qk,qe->ke", score_grad, q_one)
        return query_g.astype(BF), key_g.astype(BF), value_g.astype(BF)

    query_g, key_g, value_g = lax.map(attend_back, (q_h, k_h, v_h, log_total, mixed_grad))

    def collect(values):
        parts = join(values).reshape(2, half, n_tensor, group)
        own = jnp.where(core == 0, parts[0], parts[1])
        other = jnp.where(core == 0, parts[1], parts[0])
        return (own.astype(F32) + swap(other).astype(F32)).astype(BF)

    query_grad = join(query_g) * jnp.asarray(0.125, BF)
    qkv_grad = jnp.stack([query_grad, collect(key_g), collect(value_g)])
    query_bias_grad = jnp.sum(qkv_grad[0], axis=0, dtype=F32)
    value_bias_grad = jnp.sum(qkv_grad[2], axis=0, dtype=F32)
    qkv_w_grad = mm("nm,jntc->tmjc", x, qkv_grad).astype(BF)
    dealt = grad_one + mm("jntc,tmjc->nm", qkv_grad, w_qkv)

    grads = jnp.stack(
        [
            jnp.concatenate([qkv_w_grad.reshape(n_tensor, width, 3 * group), out_grad], axis=2),
            up_grad,
            down_grad,
        ]
    ).reshape(KINDS, n_tensor, n_dp // 2, 2, width // n_dp, 4 * group)
    parts = (
        query_bias_grad,
        value_bias_grad,
        output_bias_grad,
        up_bias_grad,
        down_bias_grad,
        gain_one,
        shift_one,
        gain_two,
        shift_two,
    )
    count = n_dp * n_tensor
    flat = jnp.concatenate([part.reshape(-1) for part in parts])
    flat = jnp.pad(flat.reshape(count, -1), ((0, 0), (0, 1024 - flat.shape[0] // count)))
    outs = jnp.stack([result.astype(BF), dealt.astype(BF)]).reshape(2, 2, span, width)
    sums, bias_sum, returned = scatter(n_dp, n_tensor, grads, flat.reshape(count, 8, 128), outs)

    returned = jnp.transpose(returned, (0, 2, 1, 3))
    used = sum(part.size for part in parts) // count
    bias_sum = bias_sum.reshape(count, 1024)[:, :used].reshape(-1)
    sizes = [part.size for part in parts]
    ends = [sum(sizes[: i + 1]) for i in range(len(sizes))]
    pieces = [bias_sum[end - size : end] for end, size in zip(ends, sizes)]

    def mine(values, size):
        return lax.dynamic_slice(values, (t * size,), (size,))

    return (
        returned[0],
        returned[1],
        sums[0][:, :group],
        sums[0][:, group : 2 * group],
        sums[0][:, 2 * group : 3 * group],
        sums[0][:, 3 * group :].T,
        sums[1],
        sums[2].T,
        mine(pieces[0], group),
        mine(pieces[1], group),
        pieces[2],
        mine(pieces[3], units),
        pieces[4],
        pieces[5],
        pieces[6],
        pieces[7],
        pieces[8],
    )


def solution(mesh):
    tokens = P("tensor", "dp", None)
    rows, columns = P("dp", "tensor"), P("tensor", "dp")
    split, copied = P("tensor"), P()
    return jax.shard_map(
        functools.partial(shards, mesh.shape["dp"], mesh.shape["tensor"]),
        mesh=mesh,
        in_specs=(
            (tokens, tokens, copied, copied, copied)
            + (rows, rows, rows, columns, rows, columns)
            + (split, split, copied, split, copied, copied, copied, copied, copied)
        ),
        out_specs=(
            (tokens, tokens, rows, rows, rows, columns, rows, columns)
            + (split, split, copied, split, copied, copied, copied, copied, copied)
        ),
        check_vma=False,
    )
```

```python
import functools

import jax
import jax.numpy as jnp
from jax import lax
from jax.experimental import pallas as pl
from jax.experimental.pallas import tpu as pltpu
from jax.sharding import PartitionSpec as P

HEAD_DIM = 64
KINDS = 3
MESH = pl.DeviceIdType.MESH
VMEM_LIMIT = 60 << 20
BF = jnp.bfloat16
F32 = jnp.float32


def flip(index, bit):
    unit = 1 << bit
    return index + unit * (1 - 2 * lax.rem(lax.div(index, unit), 2))


def orders(bits):
    return (tuple(range(bits)), tuple(reversed(range(bits))))


def relative(chip, order, code):
    for place, bit in enumerate(order):
        if code >> place & 1:
            chip = flip(chip, bit)
    return chip


def place():
    d, t = lax.axis_index("dp"), lax.axis_index("tensor")
    return d, t, lax.div(d, 2), lax.rem(d, 2)


def greet(n_dp, n_tensor):
    d, t, _, _ = place()
    barrier = pltpu.get_barrier_semaphore()
    me = d * n_tensor + t
    count = n_dp * n_tensor

    def one(step, carry):
        other = lax.rem(me + step, count)
        pl.semaphore_signal(
            barrier,
            inc=1,
            device_id=(lax.div(other, n_tensor), lax.rem(other, n_tensor)),
            device_id_type=MESH,
        )
        return carry

    lax.fori_loop(1, count, one, 0)
    pl.semaphore_wait(barrier, count - 1)


def remote(src, dst, ssem, rsem, device):
    return pltpu.make_async_remote_copy(
        src_ref=src,
        dst_ref=dst,
        send_sem=ssem,
        recv_sem=rsem,
        device_id=device,
        device_id_type=MESH,
    )


def landed(ref, sem):
    pltpu.make_async_copy(ref, ref, sem).wait()


def send_or_keep(mine, src, dst, ssem, rsem, device):
    @pl.when(mine)
    def _():
        pltpu.make_async_copy(src, dst, rsem).start()

    @pl.when(jnp.logical_not(mine))
    def _():
        remote(src, dst, ssem, rsem, device).start()


def sent(mine, src, ssem):
    @pl.when(jnp.logical_not(mine))
    def _():
        landed(src, ssem)


def forward_kernel(
    n_dp,
    n_tensor,
    undealing,
    lengths,
    vec_ref,
    x_ref,
    cot_ref,
    shard_ref,
    bias_ref,
    cl_ref,
    full_ref,
    q_out,
    k_out,
    v_out,
    mixed_out,
    act_out,
    slope_out,
    xt_out,
    ht_out,
    n1_out,
    n2_out,
    y_out,
    lse_out,
    rstd_out,
    c_one,
    c_two,
    xv,
    bias_v,
    wbuf,
    q_v,
    k_v,
    v_v,
    mixed_v,
    act_v,
    slope_v,
    turned,
    low_v,
    n1_v,
    n2_v,
    y_v,
    acc,
    lse_v,
    x_s,
    x_r,
    c1_s,
    c1_r,
    c2_s,
    c2_r,
    own_sem,
    z_s,
    z_r,
    xy_s,
    xy_r,
    sib_s,
    sib_r,
    kv_s,
    kv_r,
    bz_s,
    bz_r,
    w_sem,
    save_sem,
):
    d, t, chip, core = place()
    chips = n_dp // 2
    bits = chips.bit_length() - 1
    half_t = n_tensor // 2
    rows, cols = shard_ref.shape[1:]
    half_cols = cols // 2
    group = q_v.shape[2]
    span, width = x_ref.shape[1:]
    tokens = 2 * span
    units = cols
    prow, pcol = c_one.shape[2:]
    n_col = cot_ref.shape[2] // pcol
    pieces = KINDS * n_tensor
    sibling = (d + 1 - 2 * core, t)
    length = lengths[4 * chip + t]
    greet(n_dp, n_tensor)

    def block(k, tt, who, half):
        return full_ref.at[
            k,
            tt,
            pl.ds(pl.multiple_of((2 * who + core) * rows, rows), rows),
            pl.ds(half * half_cols, half_cols),
        ]

    def stripe(k, tt):
        return full_ref.at[k, tt, pl.ds(pl.multiple_of(d * rows, rows), rows)]

    def at(index):
        return lax.div(index, n_tensor), lax.rem(t + lax.rem(index, n_tensor), n_tensor)

    for s in range(2):
        send_or_keep(
            (lax.div(t, half_t) == core) & (2 * core + s == t),
            x_ref.at[s],
            xv.at[lax.rem(t, half_t)],
            x_s.at[s],
            x_r.at[lax.rem(t, half_t)],
            (2 * chip + lax.div(t, half_t), 2 * core + s),
        )
    for k in range(KINDS):
        pltpu.make_async_copy(shard_ref.at[k], stripe(k, t), own_sem.at[k]).start()
        for step in range(1, n_tensor):
            remote(
                shard_ref.at[k],
                stripe(k, t),
                z_s.at[k, step],
                z_r.at[k, t],
                (d, lax.rem(t + step, n_tensor)),
            ).start()
        if k == 0:
            pltpu.make_async_copy(bias_ref, bias_v.at[t], bz_r.at[0]).start()
            for step in range(1, n_tensor):
                remote(
                    bias_ref,
                    bias_v.at[t],
                    bz_s.at[step],
                    bz_r.at[step],
                    (d, lax.rem(t + step, n_tensor)),
                ).start()

    def piece(who):
        return cot_ref.at[
            :,
            pl.ds(pl.multiple_of(lax.div(who, n_col) * prow, prow), prow),
            pl.ds(pl.multiple_of(lax.rem(who, n_col) * pcol, pcol), pcol),
        ]

    pltpu.make_async_copy(piece(d), c_one.at[d], c1_r.at[0]).start()
    for step in range(1, n_dp):
        who = lax.rem(d + step, n_dp)
        remote(piece(who), c_one.at[d], c1_s.at[step], c1_r.at[step], (who, t)).start()

    def cot_second():
        for step in range(n_dp):
            landed(c_one.at[0], c1_r.at[step])
        count = 2 * n_dp
        for step in range(count):
            seq = lax.rem(4 * chip + step, count)
            slot = undealing[seq]
            c_two[seq] = c_one[lax.div(slot, 2), lax.rem(slot, 2)]
            goal = 2 * lax.div(seq, 4) + lax.div(t, half_t)
            send_or_keep(
                (goal == d) & (lax.rem(seq, 4) == t),
                c_two.at[seq],
                cl_ref.at[lax.rem(t, half_t), d],
                c2_s.at[step],
                c2_r.at[lax.rem(t, half_t), d],
                (goal, lax.rem(seq, 4)),
            )

    def forward(k, tt, half, code):
        order = orders(bits)[half]
        ref = block(k, tt, relative(chip, order, code), half)
        for s in range(code.bit_length(), bits):
            target = code | 1 << s
            remote(
                ref,
                ref,
                xy_s.at[k, tt, half, target],
                xy_r.at[k, tt, half, target],
                (2 * flip(chip, order[s]) + core, t),
            ).start()
        remote(
            ref, ref, sib_s.at[k, tt, half, code], sib_r.at[k, tt, half, code], sibling
        ).start()

    def receive(index, codes):
        k, tt = at(index)
        for code in codes:
            for half in range(2):
                landed(block(k, tt, chip, half), xy_r.at[k, tt, half, code])
                forward(k, tt, half, code)

    early, late = range(1, max(chips // 2, 1)), range(max(chips // 2, 1), chips)

    def comm_step(index):
        @pl.when(index + 1 < pieces)
        def _():
            k, tt = at(index + 1)

            @pl.when(tt == t)
            def _():
                landed(shard_ref.at[0], own_sem.at[k])

            @pl.when(tt != t)
            def _():
                landed(shard_ref.at[0], z_r.at[k, tt])

            for half in range(2):
                forward(k, tt, half, 0)

        @pl.when((index >= 0) & (index < pieces))
        def _():
            receive(index, early)

        @pl.when((index >= 1) & (index <= pieces))
        def _():
            receive(index - 1, late)

    def load(index):
        k, tt = at(index)
        slot = lax.rem(index, 2)
        for half in range(2):
            for code in range(chips):
                landed(block(k, tt, chip, half), sib_r.at[k, tt, half, code])
        copy = pltpu.make_async_copy(full_ref.at[k, tt], wbuf.at[slot], w_sem.at[slot])
        copy.start()
        copy.wait()

    def project(index):
        _, tt = at(index)
        slot = lax.rem(index, 2)
        x = xv[...].reshape(tokens, width)
        mine = pl.ds(pl.multiple_of(core * tokens, tokens), tokens)
        for c in range(3):
            out = jnp.dot(
                x, wbuf[slot, :, c * group : (c + 1) * group], preferred_element_type=F32
            )
            if c == 0:
                q_v[tt] = ((out + bias_v[tt, 0:1]) * 0.125).astype(BF)
            elif c == 1:
                k_v[tt, mine] = out.astype(BF)
            else:
                v_v[tt, mine] = (out + bias_v[tt, 1:2]).astype(BF)
        for j, ref in enumerate((k_v, v_v)):
            remote(
                ref.at[tt, mine], ref.at[tt, mine], kv_s.at[tt, j], kv_r.at[tt, j], sibling
            ).start()

    def attend(index):
        _, tt = at(index)
        slot = lax.rem(index, 2)
        mine = pl.ds(pl.multiple_of(core * tokens, tokens), tokens)
        for j, ref in enumerate((k_v, v_v)):
            landed(ref.at[tt, mine], kv_r.at[tt, j])
        block_rows = min(256, tokens)
        low = lax.broadcasted_iota(jnp.int32, (block_rows, 2 * HEAD_DIM), 1) < HEAD_DIM
        lanes = lax.broadcasted_iota(jnp.int32, (block_rows, lse_v.shape[1]), 1)
        live = lax.broadcasted_iota(jnp.int32, (1, 2 * tokens), 1) < length

        def pair_step(step, carry):
            pair, part = lax.div(step, tokens // block_rows), lax.rem(step, tokens // block_rows)
            wide = pl.ds(pl.multiple_of(pair * 2 * HEAD_DIM, 2 * HEAD_DIM), 2 * HEAD_DIM)
            spot = pl.ds(pl.multiple_of(part * block_rows, block_rows), block_rows)
            k_pair, v_pair = k_v[tt, :, wide], v_v[tt, :, wide]
            q_pair = q_v[tt, spot, wide]
            outs = []
            for head in range(2):
                q_one = jnp.where(low if head == 0 else jnp.logical_not(low), q_pair, 0).astype(BF)
                scores = lax.dot_general(
                    q_one, k_pair, (((1,), (1,)), ((), ())), preferred_element_type=F32
                )
                scores = jnp.where(live, scores, -1000000000.0)
                summit = jnp.max(scores, axis=-1, keepdims=True)
                raised = jnp.exp(scores - summit)
                total = jnp.sum(raised, axis=-1, keepdims=True)
                out = jnp.dot(raised.astype(BF), v_pair, preferred_element_type=F32)
                outs.append(out / total)
                number = tt * (group // HEAD_DIM) + pair * 2 + head
                lse_v[spot] = jnp.where(lanes == number, summit + jnp.log(total), lse_v[spot])
            mixed_v[tt, spot, wide] = jnp.where(low, outs[0], outs[1]).astype(BF)
            return carry

        lax.fori_loop(0, (group // (2 * HEAD_DIM)) * (tokens // block_rows), pair_step, 0)
        for n in range(width // 256):
            acc[:, n * 256 : (n + 1) * 256] += lax.dot_general(
                mixed_v[tt],
                wbuf[slot, n * 256 : (n + 1) * 256, 3 * group :],
                (((1,), (1,)), ((), ())),
                preferred_element_type=F32,
            )

    chunk = 64

    def norm(which, keep):
        gain, shift = vec_ref[2 + 2 * which : 3 + 2 * which], vec_ref[3 + 2 * which : 4 + 2 * which]

        def one(step, carry):
            spot = pl.ds(pl.multiple_of(step * chunk, chunk), chunk)
            value = acc[spot]
            center = value - jnp.mean(value, axis=-1, keepdims=True)
            spread = jnp.mean(center * center, axis=-1, keepdims=True)
            inverse = lax.rsqrt(spread + 1e-05)
            unit = center * inverse
            rstd_out[which, spot] = jnp.broadcast_to(inverse, (chunk, rstd_out.shape[2]))
            keep(spot, unit, unit * gain + shift)
            return carry

        lax.fori_loop(0, tokens // chunk, one, 0)

    def keep_one(spot, unit, hidden):
        n1_v[spot] = unit.astype(BF)
        low_v[spot] = hidden.astype(BF)
        acc[spot] = hidden + vec_ref[1:2]

    def keep_two(spot, unit, hidden):
        n2_v[spot] = unit.astype(BF)
        y_v[spot] = hidden.astype(BF)

    def turn_rows(source, which):
        flat = jnp.transpose(source)
        for dev in range(n_dp):
            turned[which, dev % 2, (dev // 2) * rows : (dev // 2 + 1) * rows] = flat[
                dev * rows : (dev + 1) * rows
            ]

    def expand(index):
        _, tt = at(index)
        slot = lax.rem(index, 2)

        def one(n, carry):
            wide = pl.ds(pl.multiple_of(n * 256, 256), 256)
            u = jnp.dot(low_v[...], wbuf[slot, :, wide], preferred_element_type=F32)
            u = u + bias_v[tt, pl.ds(2 + n, 1)]
            bell, below = gauss(u)
            act_v[tt, :, wide] = (u * below).astype(BF)
            slope_v[tt, :, wide] = (below + u * bell).astype(BF)
            return carry

        lax.fori_loop(0, units // 256, one, 0)

    def contract(index):
        _, tt = at(index)
        slot = lax.rem(index, 2)

        def one(n, carry):
            wide = pl.ds(pl.multiple_of(n * 256, 256), 256)
            acc[:, wide] += lax.dot_general(
                act_v[tt], wbuf[slot, wide, :], (((1,), (1,)), ((), ())), preferred_element_type=F32
            )
            return carry

        lax.fori_loop(0, width // 256, one, 0)

    comm_step(jnp.int32(-1))
    comm_step(jnp.int32(0))
    for s in range(2):
        landed(x_ref.at[s], x_r.at[s])
    for step in range(n_tensor):
        landed(bias_ref, bz_r.at[step])
    acc[...] = xv[...].reshape(tokens, width).astype(F32) + vec_ref[0:1]
    turn_rows(xv[...].reshape(tokens, width), 0)
    lse_v[...] = jnp.zeros_like(lse_v)

    def turn(index, carry):
        comm_step(index + 1)
        load(index)

        @pl.when(index < n_tensor)
        def _():
            project(index)

        @pl.when((index >= 1) & (index <= n_tensor))
        def _():
            attend(index - 1)

        @pl.when(index == n_tensor)
        def _():
            cot_second()
            norm(0, keep_one)
            turn_rows(low_v[...], 1)

        @pl.when((index >= n_tensor) & (index < 2 * n_tensor))
        def _():
            expand(index)

        @pl.when(index >= 2 * n_tensor)
        def _():
            contract(index)

        return carry

    lax.fori_loop(0, pieces, turn, 0)
    norm(1, keep_two)
    lse_out[...] = jnp.transpose(lse_v[...])

    saves = [
        pltpu.make_async_copy(src, dst, save_sem.at[i])
        for i, (src, dst) in enumerate(
            (
                (q_v, q_out),
                (k_v, k_out),
                (v_v, v_out),
                (mixed_v, mixed_out),
                (act_v, act_out),
                (slope_v, slope_out),
                (turned.at[0], xt_out),
                (turned.at[1], ht_out),
                (n1_v, n1_out),
                (n2_v, n2_out),
                (y_v, y_out),
            )
        )
    ]
    for copy in saves:
        copy.start()

    for k in range(KINDS):
        for step in range(1, n_tensor):
            landed(shard_ref.at[k], z_s.at[k, step])
        for step in range(n_tensor):
            tt = lax.rem(t + step, n_tensor)
            for half in range(2):
                for code in range(chips):
                    ref = block(k, tt, chip, half)
                    landed(ref, sib_s.at[k, tt, half, code])
                    if code:
                        landed(ref, xy_s.at[k, tt, half, code])
    for s in range(2):
        sent((lax.div(t, half_t) == core) & (2 * core + s == t), x_ref.at[s], x_s.at[s])
    for step in range(1, n_tensor):
        landed(bias_ref, bz_s.at[step])
    for tt in range(n_tensor):
        for j in range(2):
            landed(q_v.at[tt], kv_s.at[tt, j])
    for step in range(1, n_dp):
        landed(c_one.at[0], c1_s.at[step])
    for step in range(2 * n_dp):
        seq = lax.rem(4 * chip + step, 2 * n_dp)
        goal = 2 * lax.div(seq, 4) + lax.div(t, half_t)
        sent((goal == d) & (lax.rem(seq, 4) == t), c_two.at[0], c2_s.at[step])
    for q in range(half_t):
        for who in range(n_dp):
            landed(c_two.at[0], c2_r.at[q, who])
    for copy in saves:
        copy.wait()


def gauss(u):
    size = jnp.abs(u)
    bell = 0.3989422804014327 * jnp.exp(-0.5 * (u * u))
    s = 1.0 / (1.0 + 0.23164190 * size)
    tail = bell * s * (
        0.319381530 + s * (-0.356563782 + s * (1.781477937 + s * (-1.821255978 + s * 1.330274429)))
    )
    return bell, jnp.where(u < 0, tail, 1.0 - tail)


def run_forward(n_dp, n_tensor, undealing, lengths, vecs, x_in, cot_in, shard, biases):
    slots, span, width = x_in.shape
    rows, cols = shard.shape[1:]
    chips = n_dp // 2
    tokens = 2 * span
    group = cols // 4
    n_pos = min(n_dp, span // 16)
    prow, pcol = span // n_pos, width // (n_dp // n_pos)
    dma = pltpu.SemaphoreType.DMA
    any_space = pl.BlockSpec(memory_space=pl.ANY)
    smem = pl.BlockSpec(memory_space=pltpu.SMEM)
    vmem = pl.BlockSpec(memory_space=pltpu.VMEM)
    shapes = (
        ((2, n_dp, prow, pcol), BF),
        ((KINDS, n_tensor, width, cols), BF),
        ((n_tensor, tokens, group), BF),
        ((n_tensor, 2 * tokens, group), BF),
        ((n_tensor, 2 * tokens, group), BF),
        ((n_tensor, tokens, group), BF),
        ((n_tensor, tokens, cols), BF),
        ((n_tensor, tokens, cols), BF),
        ((2, width // 2, tokens), BF),
        ((2, width // 2, tokens), BF),
        ((tokens, width), BF),
        ((tokens, width), BF),
        ((tokens, width), BF),
        ((128, tokens), F32),
        ((2, tokens, 128), F32),
    )
    return pl.pallas_call(
        functools.partial(forward_kernel, n_dp, n_tensor),
        out_shape=tuple(jax.ShapeDtypeStruct(*shape) for shape in shapes),
        in_specs=[smem, smem, vmem, any_space, any_space, any_space, any_space],
        out_specs=(any_space,) * 13 + (vmem, vmem),
        scratch_shapes=[
            pltpu.VMEM((n_dp, slots, prow, pcol), BF),
            pltpu.VMEM((2 * n_dp, prow, pcol), BF),
            pltpu.VMEM((2, span, width), BF),
            pltpu.VMEM((n_tensor,) + biases.shape, F32),
            pltpu.VMEM((2, width, cols), BF),
            pltpu.VMEM((n_tensor, tokens, group), BF),
            pltpu.VMEM((n_tensor, 2 * tokens, group), BF),
            pltpu.VMEM((n_tensor, 2 * tokens, group), BF),
            pltpu.VMEM((n_tensor, tokens, group), BF),
            pltpu.VMEM((n_tensor, tokens, cols), BF),
            pltpu.VMEM((n_tensor, tokens, cols), BF),
            pltpu.VMEM((2, 2, width // 2, tokens), BF),
            pltpu.VMEM((tokens, width), BF),
            pltpu.VMEM((tokens, width), BF),
            pltpu.VMEM((tokens, width), BF),
            pltpu.VMEM((tokens, width), BF),
            pltpu.VMEM((tokens, width), F32),
            pltpu.VMEM((tokens, 128), F32),
            dma((2,)),
            dma((2,)),
            dma((n_dp,)),
            dma((n_dp,)),
            dma((2 * n_dp,)),
            dma((n_tensor // 2, n_dp)),
            dma((KINDS,)),
            dma((KINDS, n_tensor)),
            dma((KINDS, n_tensor)),
            dma((KINDS, n_tensor, 2, chips)),
            dma((KINDS, n_tensor, 2, chips)),
            dma((KINDS, n_tensor, 2, chips)),
            dma((KINDS, n_tensor, 2, chips)),
            dma((n_tensor, 2)),
            dma((n_tensor, 2)),
            dma((n_tensor,)),
            dma((n_tensor,)),
            dma((2,)),
            dma((11,)),
        ],
        compiler_params=pltpu.CompilerParams(
            collective_id=0, has_side_effects=True, vmem_limit_bytes=VMEM_LIMIT
        ),
        name="forward_layer",
    )(undealing, lengths, vecs, x_in, cot_in, shard, biases)


def scatter_kernel(
    n_dp,
    n_tensor,
    grad_ref,
    bias_ref,
    y_ref,
    sum_ref,
    bias_out,
    y_out,
    from_core,
    held,
    from_chip,
    from_z,
    bias_in,
    y_s,
    y_r,
    b_s,
    b_r,
    bo_s,
    bo_r,
    own_sem,
    core_s,
    core_r,
    xy_s,
    xy_r,
    z_s,
    z_r,
    out_sem,
):
    d, t, chip, core = place()
    chips = n_dp // 2
    bits = chips.bit_length() - 1
    half_t = n_tensor // 2
    count = n_dp * n_tensor
    me = d * n_tensor + t
    rows, cols = grad_ref.shape[4:]
    half_cols = cols // 2
    pieces = KINDS * n_tensor
    greet(n_dp, n_tensor)

    def at(index):
        k = lax.div(index, n_tensor)
        return k, lax.rem(t + lax.rem(index, n_tensor), n_tensor)

    def begin(index, carry):
        k, tt = at(index)
        remote(
            grad_ref.at[k, tt, :, 1 - core],
            from_core.at[index],
            core_s.at[index],
            core_r.at[index],
            (d + 1 - 2 * core, t),
        ).start()
        pltpu.make_async_copy(grad_ref.at[k, tt, :, core], held.at[index], own_sem.at[index]).start()
        return carry

    lax.fori_loop(0, pieces, begin, 0)

    for a in range(y_ref.shape[0]):
        for q in range(2):
            send_or_keep(
                (lax.div(t, half_t) == core) & (2 * core + q == t),
                y_ref.at[a, q],
                y_out.at[a, lax.rem(t, half_t)],
                y_s.at[a, q],
                y_r.at[a, lax.rem(t, half_t)],
                (2 * chip + lax.div(t, half_t), 2 * core + q),
            )

    def device(index):
        return (lax.div(index, n_tensor), lax.rem(index, n_tensor))

    def bias_begin(step, carry):
        other = lax.rem(me + step, count)
        remote(
            bias_ref.at[other], bias_in.at[step], b_s.at[step], b_r.at[step], device(other)
        ).start()
        return carry

    lax.fori_loop(1, count, bias_begin, 0)
    pltpu.make_async_copy(bias_ref.at[me], bias_in.at[0], b_r.at[0]).start()

    def bias_middle():
        def arrive(step, total):
            landed(bias_in.at[0], b_r.at[step])
            return total + bias_in[step]

        total = lax.fori_loop(0, count, arrive, jnp.zeros(bias_in.shape[1:], F32))

        def leave(step, carry):
            landed(bias_in.at[0], b_s.at[step])
            return carry

        lax.fori_loop(1, count, leave, 0)
        bias_in[0] = total
        pltpu.make_async_copy(bias_in.at[0], bias_out.at[me], bo_r.at[0]).start()

        def spread(step, carry):
            other = lax.rem(me + step, count)
            remote(
                bias_in.at[0], bias_out.at[me], bo_s.at[step], bo_r.at[step], device(other)
            ).start()
            return carry

        lax.fori_loop(1, count, spread, 0)

    def bias_end():
        def last(step, carry):
            landed(bias_in.at[0], bo_r.at[step])
            return carry

        lax.fori_loop(0, count, last, 0)

        def gone(step, carry):
            landed(bias_in.at[0], bo_s.at[step])
            return carry

        lax.fori_loop(1, count, gone, 0)

    def pass_on(index, s):
        for half in range(2):
            order = orders(bits)[half]
            for code in range(1 << s, 2 << s):
                remote(
                    held.at[index, relative(chip, order, code), :, pl.ds(half * half_cols, half_cols)],
                    from_chip.at[index, half, code - 1],
                    xy_s.at[index, half, code],
                    xy_r.at[index, half, code],
                    (2 * flip(chip, order[s]) + core, t),
                ).start()

    def take_in(index, s):
        for half in range(2):
            order = orders(bits)[half]
            for code in range(1 << s, 2 << s):
                landed(from_chip.at[0, 0, 0], xy_r.at[index, half, code])
                spot = held.at[
                    index,
                    relative(chip, order, code - (1 << s)),
                    :,
                    pl.ds(half * half_cols, half_cols),
                ]
                spot[...] = (
                    spot[...].astype(F32) + from_chip[index, half, code - 1].astype(F32)
                ).astype(BF)

    def first(index):
        landed(held.at[0], own_sem.at[index])
        landed(held.at[0], core_r.at[index])

        def add(c, carry):
            held[index, c] = (held[index, c].astype(F32) + from_core[index, c].astype(F32)).astype(BF)
            return carry

        lax.fori_loop(0, chips, add, 0)
        if bits:
            pass_on(index, bits - 1)

    def finish(index):
        k, tt = at(index)
        step = lax.rem(index, n_tensor)

        @pl.when(step > 0)
        def _():
            remote(
                held.at[index, chip],
                from_z.at[k, step],
                z_s.at[k, step],
                z_r.at[k, step],
                (d, tt),
            ).start()

    def turn(it, carry):
        for stage in range(bits + 1):
            index = it - stage

            @pl.when((index >= 0) & (index < pieces))
            def _(stage=stage, index=index):
                if stage == 0:
                    first(index)
                else:
                    take_in(index, bits - stage)
                    if stage < bits:
                        pass_on(index, bits - stage - 1)
                if stage == bits:
                    finish(index)

        return carry

    lax.fori_loop(0, pieces + bits, turn, 0)
    bias_middle()

    for k in range(KINDS):
        total = held[k * n_tensor, chip].astype(F32)
        for step in range(1, n_tensor):
            landed(from_z.at[0, 0], z_r.at[k, step])
            total = total + from_z[k, step].astype(F32)
        sum_ref[k] = total

    def close(index, carry):
        landed(held.at[0], core_s.at[index])
        for half in range(2):
            for code in range(1, chips):
                landed(from_chip.at[0, 0, 0], xy_s.at[index, half, code])
        return carry

    lax.fori_loop(0, pieces, close, 0)
    for k in range(KINDS):
        for step in range(1, n_tensor):
            landed(from_z.at[0, 0], z_s.at[k, step])
    for a in range(y_ref.shape[0]):
        for q in range(2):
            sent((lax.div(t, half_t) == core) & (2 * core + q == t), y_ref.at[a, q], y_s.at[a, q])
            landed(y_ref.at[a, q], y_r.at[a, q])
    bias_end()


def scatter(n_dp, n_tensor, grads, bias, outs):
    rows, cols = grads.shape[4:]
    chips = n_dp // 2
    pieces = KINDS * n_tensor
    count = n_dp * n_tensor
    dma = pltpu.SemaphoreType.DMA
    any_space = pl.BlockSpec(memory_space=pl.ANY)
    return pl.pallas_call(
        functools.partial(scatter_kernel, n_dp, n_tensor),
        out_shape=(
            jax.ShapeDtypeStruct((KINDS, rows, cols), F32),
            jax.ShapeDtypeStruct(bias.shape, F32),
            jax.ShapeDtypeStruct(outs.shape, BF),
        ),
        in_specs=[any_space] * 3,
        out_specs=(pl.BlockSpec(memory_space=pltpu.VMEM), any_space, any_space),
        scratch_shapes=[
            pltpu.VMEM((pieces, chips, rows, cols), BF),
            pltpu.VMEM((pieces, chips, rows, cols), BF),
            pltpu.VMEM((pieces, 2, chips - 1, rows, cols // 2), BF),
            pltpu.VMEM((KINDS, n_tensor, rows, cols), BF),
            pltpu.VMEM(bias.shape, F32),
            dma((outs.shape[0], 2)),
            dma((outs.shape[0], 2)),
            dma((count,)),
            dma((count,)),
            dma((count,)),
            dma((count,)),
            dma((pieces,)),
            dma((pieces,)),
            dma((pieces,)),
            dma((pieces, 2, chips)),
            dma((pieces, 2, chips)),
            dma((KINDS, n_tensor)),
            dma((KINDS, n_tensor)),
            dma((1,)),
        ],
        compiler_params=pltpu.CompilerParams(
            collective_id=1, has_side_effects=True, vmem_limit_bytes=VMEM_LIMIT
        ),
        name="scatter_all",
    )(grads, bias, outs)


def mm(spec, left, right):
    return jnp.einsum(spec, left, right, preferred_element_type=F32)


def shards(
    n_dp,
    n_tensor,
    inputs,
    cotangent,
    lengths,
    dealing,
    undealing,
    query_weight,
    key_weight,
    value_weight,
    output_weight,
    up_weight,
    down_weight,
    query_bias,
    value_bias,
    output_bias,
    up_bias,
    down_bias,
    first_gain,
    first_shift,
    second_gain,
    second_shift,
):
    span, slots, width = inputs.shape
    group = query_weight.shape[1]
    units = up_weight.shape[1]
    half = span * n_tensor // 2
    d, t, chip, core = place()
    length = lengths[2 * slots * chip + t]
    positions = core * half + jnp.arange(half)
    valid = (positions < length).astype(F32)

    shard = jnp.stack(
        [
            jnp.concatenate([query_weight, key_weight, value_weight, output_weight.T], axis=1),
            up_weight,
            down_weight.T,
        ]
    ).astype(BF)
    blank = jnp.zeros((group,), F32)
    biases = jnp.concatenate([query_bias, value_bias, up_bias, blank, blank]).reshape(8, group)
    vecs = jnp.stack([output_bias, down_bias, first_gain, first_shift, second_gain, second_shift])
    (
        cot_loc, full, query, key, value, mixed, activated, slope, x_t, h_t, n1, n2, y, lse, rstd
    ) = run_forward(
        n_dp,
        n_tensor,
        undealing,
        lengths,
        jnp.pad(vecs, ((0, 2), (0, 0))),
        jnp.transpose(inputs, (1, 0, 2)),
        jnp.transpose(cotangent, (1, 0, 2)),
        shard,
        biases,
    )
    n_col = width // cot_loc.shape[3]
    cot = cot_loc.reshape(2, n_dp // n_col, n_col, *cot_loc.shape[2:])
    cot = jnp.transpose(cot, (0, 1, 3, 2, 4)).reshape(half, width)
    w_qkv = full[0][:, :, : 3 * group].reshape(n_tensor, width, 3, group)
    w_out = full[0][:, :, 3 * group :]
    w_up, w_down = full[1], full[2]

    def unturn(values):
        return jnp.transpose(values.reshape(2, n_dp // 2, width // n_dp, half), (3, 1, 0, 2)).reshape(half, width)

    x, hidden_low = unturn(x_t), unturn(h_t)

    def swap(values):
        return lax.ppermute(values, "dp", [(i, i ^ 1) for i in range(n_dp)])

    heads = n_tensor * group // HEAD_DIM

    def split(values):
        values = values.reshape(n_tensor, -1, group // HEAD_DIM, HEAD_DIM)
        return jnp.transpose(values, (0, 2, 1, 3)).reshape(heads, -1, HEAD_DIM)

    def join(values):
        return jnp.transpose(values, (1, 0, 2)).reshape(-1, n_tensor, group)

    q_h, k_h, v_h = split(query), split(key), split(value)
    log_total = lse[:heads]
    visible = jnp.arange(2 * half) < length
    mixed = jnp.transpose(mixed, (1, 0, 2))
    activated = jnp.transpose(activated, (1, 0, 2))
    slope = jnp.transpose(slope, (1, 0, 2))
    result = y

    def norm_back(e, unit, gain, inverse):
        unit = unit.astype(F32)
        ge = e * gain
        grad = ge - jnp.mean(ge, -1, keepdims=True) - unit * jnp.mean(ge * unit, -1, keepdims=True)
        return grad * inverse[:, :1], jnp.sum(e * unit, 0), jnp.sum(e, 0)

    seed = cot.astype(F32) * valid[:, None]
    grad_two, gain_two, shift_two = norm_back(seed, n2, second_gain, rstd[1])
    mlp_grad = grad_two.astype(BF)
    down_bias_grad = jnp.sum(mlp_grad, axis=0, dtype=F32)
    down_grad = mm("nm,ntf->tmf", mlp_grad, activated).astype(BF)
    act_grad = mm("nm,tmf->ntf", mlp_grad, w_down)
    expand_grad = (slope.astype(F32) * act_grad).astype(BF)
    up_bias_grad = jnp.sum(expand_grad, axis=0, dtype=F32)
    up_grad = mm("nm,ntf->tmf", hidden_low, expand_grad).astype(BF)
    hidden_grad = grad_two + mm("ntf,tmf->nm", expand_grad, w_up)
    grad_one, gain_one, shift_one = norm_back(hidden_grad, n1, first_gain, rstd[0])
    attn_grad = grad_one.astype(BF)
    output_bias_grad = jnp.sum(attn_grad, axis=0, dtype=F32)
    out_grad = mm("nm,ntc->tmc", attn_grad, mixed).astype(BF)
    mixed_grad = split(mm("nm,tmc->tnc", attn_grad, w_out).astype(BF))

    def attend_back(one):
        q_one, k_one, v_one, total, o_one = one
        scores = jnp.where(visible, mm("qe,ke->qk", q_one, k_one), -1000000000.0)
        probs = jnp.exp(scores - total[:, None])
        prob_grad = mm("qe,ke->qk", o_one, v_one)
        value_g = mm("qk,qe->ke", probs.astype(BF), o_one)
        inner = jnp.sum(probs * prob_grad, axis=-1, keepdims=True)
        score_grad = (probs * (prob_grad - inner)).astype(BF)
        query_g = mm("qk,ke->qe", score_grad, k_one)
        key_g = mm("qk,qe->ke", score_grad, q_one)
        return query_g.astype(BF), key_g.astype(BF), value_g.astype(BF)

    query_g, key_g, value_g = lax.map(attend_back, (q_h, k_h, v_h, log_total, mixed_grad))

    def collect(values):
        parts = join(values).reshape(2, half, n_tensor, group)
        own = jnp.where(core == 0, parts[0], parts[1])
        other = jnp.where(core == 0, parts[1], parts[0])
        return (own.astype(F32) + swap(other).astype(F32)).astype(BF)

    query_grad = join(query_g) * jnp.asarray(0.125, BF)
    qkv_grad = jnp.stack([query_grad, collect(key_g), collect(value_g)])
    query_bias_grad = jnp.sum(qkv_grad[0], axis=0, dtype=F32)
    value_bias_grad = jnp.sum(qkv_grad[2], axis=0, dtype=F32)
    qkv_w_grad = mm("nm,jntc->tmjc", x, qkv_grad).astype(BF)
    dealt = grad_one + mm("jntc,tmjc->nm", qkv_grad, w_qkv)

    grads = jnp.stack(
        [
            jnp.concatenate([qkv_w_grad.reshape(n_tensor, width, 3 * group), out_grad], axis=2),
            up_grad,
            down_grad,
        ]
    ).reshape(KINDS, n_tensor, n_dp // 2, 2, width // n_dp, 4 * group)
    parts = (
        query_bias_grad,
        value_bias_grad,
        output_bias_grad,
        up_bias_grad,
        down_bias_grad,
        gain_one,
        shift_one,
        gain_two,
        shift_two,
    )
    count = n_dp * n_tensor
    flat = jnp.concatenate([part.reshape(-1) for part in parts])
    flat = jnp.pad(flat.reshape(count, -1), ((0, 0), (0, 1024 - flat.shape[0] // count)))
    outs = jnp.stack([result.astype(BF), dealt.astype(BF)]).reshape(2, 2, span, width)
    sums, bias_sum, returned = scatter(n_dp, n_tensor, grads, flat.reshape(count, 8, 128), outs)

    returned = jnp.transpose(returned, (0, 2, 1, 3))
    used = sum(part.size for part in parts) // count
    bias_sum = bias_sum.reshape(count, 1024)[:, :used].reshape(-1)
    sizes = [part.size for part in parts]
    ends = [sum(sizes[: i + 1]) for i in range(len(sizes))]
    pieces = [bias_sum[end - size : end] for end, size in zip(ends, sizes)]

    def mine(values, size):
        return lax.dynamic_slice(values, (t * size,), (size,))

    return (
        returned[0],
        returned[1],
        sums[0][:, :group],
        sums[0][:, group : 2 * group],
        sums[0][:, 2 * group : 3 * group],
        sums[0][:, 3 * group :].T,
        sums[1],
        sums[2].T,
        mine(pieces[0], group),
        mine(pieces[1], group),
        pieces[2],
        mine(pieces[3], units),
        pieces[4],
        pieces[5],
        pieces[6],
        pieces[7],
        pieces[8],
    )


def solution(mesh):
    tokens = P("tensor", "dp", None)
    rows, columns = P("dp", "tensor"), P("tensor", "dp")
    split, copied = P("tensor"), P()
    return jax.shard_map(
        functools.partial(shards, mesh.shape["dp"], mesh.shape["tensor"]),
        mesh=mesh,
        in_specs=(
            (tokens, tokens, copied, copied, copied)
            + (rows, rows, rows, columns, rows, columns)
            + (split, split, copied, split, copied, copied, copied, copied, copied)
        ),
        out_specs=(
            (tokens, tokens, rows, rows, rows, columns, rows, columns)
            + (split, split, copied, split, copied, copied, copied, copied, copied)
        ),
        check_vma=False,
    )
```

```python
import functools

import jax
import jax.numpy as jnp
from jax import lax
from jax.experimental import pallas as pl
from jax.experimental.pallas import tpu as pltpu
from jax.sharding import PartitionSpec as P

HEAD_DIM = 64
KINDS = 3
MESH = pl.DeviceIdType.MESH
VMEM_LIMIT = 60 << 20
BF = jnp.bfloat16
F32 = jnp.float32


def flip(index, bit):
    unit = 1 << bit
    return index + unit * (1 - 2 * lax.rem(lax.div(index, unit), 2))


def orders(bits):
    return (tuple(range(bits)), tuple(reversed(range(bits))))


def relative(chip, order, code):
    for place, bit in enumerate(order):
        if code >> place & 1:
            chip = flip(chip, bit)
    return chip


def place():
    d, t = lax.axis_index("dp"), lax.axis_index("tensor")
    return d, t, lax.div(d, 2), lax.rem(d, 2)


def greet(n_dp, n_tensor):
    d, t, _, _ = place()
    barrier = pltpu.get_barrier_semaphore()
    me = d * n_tensor + t
    count = n_dp * n_tensor

    def one(step, carry):
        other = lax.rem(me + step, count)
        pl.semaphore_signal(
            barrier,
            inc=1,
            device_id=(lax.div(other, n_tensor), lax.rem(other, n_tensor)),
            device_id_type=MESH,
        )
        return carry

    lax.fori_loop(1, count, one, 0)
    pl.semaphore_wait(barrier, count - 1)


def remote(src, dst, ssem, rsem, device):
    return pltpu.make_async_remote_copy(
        src_ref=src,
        dst_ref=dst,
        send_sem=ssem,
        recv_sem=rsem,
        device_id=device,
        device_id_type=MESH,
    )


def landed(ref, sem):
    pltpu.make_async_copy(ref, ref, sem).wait()


def send_or_keep(mine, src, dst, ssem, rsem, device):
    @pl.when(mine)
    def _():
        pltpu.make_async_copy(src, dst, rsem).start()

    @pl.when(jnp.logical_not(mine))
    def _():
        remote(src, dst, ssem, rsem, device).start()


def sent(mine, src, ssem):
    @pl.when(jnp.logical_not(mine))
    def _():
        landed(src, ssem)


def forward_kernel(
    n_dp,
    n_tensor,
    undealing,
    lengths,
    vec_ref,
    x_ref,
    cot_ref,
    shard_ref,
    bias_ref,
    cl_ref,
    full_ref,
    q_out,
    k_out,
    v_out,
    mixed_out,
    act_out,
    slope_out,
    xt_out,
    ht_out,
    n1_out,
    n2_out,
    y_out,
    lse_out,
    rstd_out,
    c_one,
    c_two,
    xv,
    bias_v,
    wbuf,
    q_v,
    k_v,
    v_v,
    mixed_v,
    act_v,
    slope_v,
    turned,
    low_v,
    n1_v,
    n2_v,
    y_v,
    acc,
    lse_v,
    x_s,
    x_r,
    c1_s,
    c1_r,
    c2_s,
    c2_r,
    own_sem,
    z_s,
    z_r,
    xy_s,
    xy_r,
    sib_s,
    sib_r,
    kv_s,
    kv_r,
    bz_s,
    bz_r,
    w_sem,
    save_sem,
):
    d, t, chip, core = place()
    chips = n_dp // 2
    bits = chips.bit_length() - 1
    half_t = n_tensor // 2
    rows, cols = shard_ref.shape[1:]
    half_cols = cols // 2
    group = q_v.shape[2]
    span, width = x_ref.shape[1:]
    tokens = 2 * span
    units = cols
    prow, pcol = c_one.shape[2:]
    n_col = cot_ref.shape[2] // pcol
    pieces = KINDS * n_tensor
    sibling = (d + 1 - 2 * core, t)
    length = lengths[4 * chip + t]
    greet(n_dp, n_tensor)

    def block(k, tt, who, half):
        return full_ref.at[
            k,
            tt,
            pl.ds(pl.multiple_of((2 * who + core) * rows, rows), rows),
            pl.ds(half * half_cols, half_cols),
        ]

    def stripe(k, tt):
        return full_ref.at[k, tt, pl.ds(pl.multiple_of(d * rows, rows), rows)]

    def at(index):
        return lax.div(index, n_tensor), lax.rem(t + lax.rem(index, n_tensor), n_tensor)

    for s in range(2):
        send_or_keep(
            (lax.div(t, half_t) == core) & (2 * core + s == t),
            x_ref.at[s],
            xv.at[lax.rem(t, half_t)],
            x_s.at[s],
            x_r.at[lax.rem(t, half_t)],
            (2 * chip + lax.div(t, half_t), 2 * core + s),
        )
    for k in range(KINDS):
        pltpu.make_async_copy(shard_ref.at[k], stripe(k, t), own_sem.at[k]).start()
        for step in range(1, n_tensor):
            remote(
                shard_ref.at[k],
                stripe(k, t),
                z_s.at[k, step],
                z_r.at[k, t],
                (d, lax.rem(t + step, n_tensor)),
            ).start()
        if k == 0:
            pltpu.make_async_copy(bias_ref, bias_v.at[t], bz_r.at[0]).start()
            for step in range(1, n_tensor):
                remote(
                    bias_ref,
                    bias_v.at[t],
                    bz_s.at[step],
                    bz_r.at[step],
                    (d, lax.rem(t + step, n_tensor)),
                ).start()

    def piece(who):
        return cot_ref.at[
            :,
            pl.ds(pl.multiple_of(lax.div(who, n_col) * prow, prow), prow),
            pl.ds(pl.multiple_of(lax.rem(who, n_col) * pcol, pcol), pcol),
        ]

    pltpu.make_async_copy(piece(d), c_one.at[d], c1_r.at[0]).start()
    for step in range(1, n_dp):
        who = lax.rem(d + step, n_dp)
        remote(piece(who), c_one.at[d], c1_s.at[step], c1_r.at[step], (who, t)).start()

    def cot_second():
        for step in range(n_dp):
            landed(c_one.at[0], c1_r.at[step])
        count = 2 * n_dp
        for step in range(count):
            seq = lax.rem(4 * chip + step, count)
            slot = undealing[seq]
            c_two[seq] = c_one[lax.div(slot, 2), lax.rem(slot, 2)]
            goal = 2 * lax.div(seq, 4) + lax.div(t, half_t)
            send_or_keep(
                (goal == d) & (lax.rem(seq, 4) == t),
                c_two.at[seq],
                cl_ref.at[lax.rem(t, half_t), d],
                c2_s.at[step],
                c2_r.at[lax.rem(t, half_t), d],
                (goal, lax.rem(seq, 4)),
            )

    def forward(k, tt, half, code):
        order = orders(bits)[half]
        ref = block(k, tt, relative(chip, order, code), half)
        for s in range(code.bit_length(), bits):
            target = code | 1 << s
            remote(
                ref,
                ref,
                xy_s.at[k, tt, half, target],
                xy_r.at[k, tt, half, target],
                (2 * flip(chip, order[s]) + core, t),
            ).start()
        remote(
            ref, ref, sib_s.at[k, tt, half, code], sib_r.at[k, tt, half, code], sibling
        ).start()

    def receive(index, codes):
        k, tt = at(index)
        for code in codes:
            for half in range(2):
                landed(block(k, tt, chip, half), xy_r.at[k, tt, half, code])
                forward(k, tt, half, code)

    early, late = range(1, max(chips // 2, 1)), range(max(chips // 2, 1), chips)

    def comm_step(index):
        @pl.when(index + 1 < pieces)
        def _():
            k, tt = at(index + 1)

            @pl.when(tt == t)
            def _():
                landed(shard_ref.at[0], own_sem.at[k])

            @pl.when(tt != t)
            def _():
                landed(shard_ref.at[0], z_r.at[k, tt])

            for half in range(2):
                forward(k, tt, half, 0)

        @pl.when((index >= 0) & (index < pieces))
        def _():
            receive(index, early)

        @pl.when((index >= 1) & (index <= pieces))
        def _():
            receive(index - 1, late)

    def load(index):
        k, tt = at(index)
        slot = lax.rem(index, 2)
        for half in range(2):
            for code in range(chips):
                landed(block(k, tt, chip, half), sib_r.at[k, tt, half, code])
        copy = pltpu.make_async_copy(full_ref.at[k, tt], wbuf.at[slot], w_sem.at[slot])
        copy.start()
        copy.wait()

    def project(index):
        _, tt = at(index)
        slot = lax.rem(index, 2)
        x = xv[...].reshape(tokens, width)
        mine = pl.ds(pl.multiple_of(core * tokens, tokens), tokens)
        for c in range(3):
            out = jnp.dot(
                x, wbuf[slot, :, c * group : (c + 1) * group], preferred_element_type=F32
            )
            if c == 0:
                q_v[tt] = ((out + bias_v[tt, 0:1]) * 0.125).astype(BF)
            elif c == 1:
                k_v[tt, mine] = out.astype(BF)
            else:
                v_v[tt, mine] = (out + bias_v[tt, 1:2]).astype(BF)
        for j, ref in enumerate((k_v, v_v)):
            remote(
                ref.at[tt, mine], ref.at[tt, mine], kv_s.at[tt, j], kv_r.at[tt, j], sibling
            ).start()

    def attend(index):
        _, tt = at(index)
        slot = lax.rem(index, 2)
        mine = pl.ds(pl.multiple_of(core * tokens, tokens), tokens)
        for j, ref in enumerate((k_v, v_v)):
            landed(ref.at[tt, mine], kv_r.at[tt, j])
        block_rows = min(256, tokens)
        low = lax.broadcasted_iota(jnp.int32, (block_rows, 2 * HEAD_DIM), 1) < HEAD_DIM
        lanes = lax.broadcasted_iota(jnp.int32, (block_rows, lse_v.shape[1]), 1)
        live = lax.broadcasted_iota(jnp.int32, (1, 2 * tokens), 1) < length

        def pair_step(step, carry):
            pair, part = lax.div(step, tokens // block_rows), lax.rem(step, tokens // block_rows)
            wide = pl.ds(pl.multiple_of(pair * 2 * HEAD_DIM, 2 * HEAD_DIM), 2 * HEAD_DIM)
            spot = pl.ds(pl.multiple_of(part * block_rows, block_rows), block_rows)
            k_pair, v_pair = k_v[tt, :, wide], v_v[tt, :, wide]
            q_pair = q_v[tt, spot, wide]
            outs = []
            for head in range(2):
                q_one = jnp.where(low if head == 0 else jnp.logical_not(low), q_pair, 0).astype(BF)
                scores = lax.dot_general(
                    q_one, k_pair, (((1,), (1,)), ((), ())), preferred_element_type=F32
                )
                scores = jnp.where(live, scores, -1000000000.0)
                summit = jnp.max(scores, axis=-1, keepdims=True)
                raised = jnp.exp(scores - summit)
                total = jnp.sum(raised, axis=-1, keepdims=True)
                out = jnp.dot(raised.astype(BF), v_pair, preferred_element_type=F32)
                outs.append(out / total)
                number = tt * (group // HEAD_DIM) + pair * 2 + head
                lse_v[spot] = jnp.where(lanes == number, summit + jnp.log(total), lse_v[spot])
            mixed_v[tt, spot, wide] = jnp.where(low, outs[0], outs[1]).astype(BF)
            return carry

        lax.fori_loop(0, (group // (2 * HEAD_DIM)) * (tokens // block_rows), pair_step, 0)
        for n in range(width // 256):
            acc[:, n * 256 : (n + 1) * 256] += lax.dot_general(
                mixed_v[tt],
                wbuf[slot, n * 256 : (n + 1) * 256, 3 * group :],
                (((1,), (1,)), ((), ())),
                preferred_element_type=F32,
            )

    chunk = 64

    def norm(which, keep):
        gain, shift = vec_ref[2 + 2 * which : 3 + 2 * which], vec_ref[3 + 2 * which : 4 + 2 * which]

        def one(step, carry):
            spot = pl.ds(pl.multiple_of(step * chunk, chunk), chunk)
            value = acc[spot]
            center = value - jnp.mean(value, axis=-1, keepdims=True)
            spread = jnp.mean(center * center, axis=-1, keepdims=True)
            inverse = lax.rsqrt(spread + 1e-05)
            unit = center * inverse
            rstd_out[which, spot] = jnp.broadcast_to(inverse, (chunk, rstd_out.shape[2]))
            keep(spot, unit, unit * gain + shift)
            return carry

        lax.fori_loop(0, tokens // chunk, one, 0)

    def keep_one(spot, unit, hidden):
        n1_v[spot] = unit.astype(BF)
        low_v[spot] = hidden.astype(BF)
        acc[spot] = hidden + vec_ref[1:2]

    def keep_two(spot, unit, hidden):
        n2_v[spot] = unit.astype(BF)
        y_v[spot] = hidden.astype(BF)

    def turn_rows(source, which):
        flat = jnp.transpose(source)
        for dev in range(n_dp):
            turned[which, dev % 2, (dev // 2) * rows : (dev // 2 + 1) * rows] = flat[
                dev * rows : (dev + 1) * rows
            ]

    def expand(index):
        _, tt = at(index)
        slot = lax.rem(index, 2)

        def one(n, carry):
            wide = pl.ds(pl.multiple_of(n * 256, 256), 256)
            u = jnp.dot(low_v[...], wbuf[slot, :, wide], preferred_element_type=F32)
            u = u + bias_v[tt, pl.ds(2 + n, 1)]
            bell, below = gauss(u)
            act_v[tt, :, wide] = (u * below).astype(BF)
            slope_v[tt, :, wide] = (below + u * bell).astype(BF)
            return carry

        lax.fori_loop(0, units // 256, one, 0)

    def contract(index):
        _, tt = at(index)
        slot = lax.rem(index, 2)

        def one(n, carry):
            wide = pl.ds(pl.multiple_of(n * 256, 256), 256)
            acc[:, wide] += lax.dot_general(
                act_v[tt], wbuf[slot, wide, :], (((1,), (1,)), ((), ())), preferred_element_type=F32
            )
            return carry

        lax.fori_loop(0, width // 256, one, 0)

    comm_step(jnp.int32(-1))
    comm_step(jnp.int32(0))
    for s in range(2):
        landed(x_ref.at[s], x_r.at[s])
    for step in range(n_tensor):
        landed(bias_ref, bz_r.at[step])
    acc[...] = xv[...].reshape(tokens, width).astype(F32) + vec_ref[0:1]
    turn_rows(xv[...].reshape(tokens, width), 0)
    lse_v[...] = jnp.zeros_like(lse_v)

    def turn(index, carry):
        comm_step(index + 1)
        load(index)

        @pl.when(index < n_tensor)
        def _():
            project(index)

        @pl.when((index >= 1) & (index <= n_tensor))
        def _():
            attend(index - 1)

        @pl.when(index == n_tensor)
        def _():
            cot_second()
            norm(0, keep_one)
            turn_rows(low_v[...], 1)

        @pl.when((index >= n_tensor) & (index < 2 * n_tensor))
        def _():
            expand(index)

        @pl.when(index >= 2 * n_tensor)
        def _():
            contract(index)

        return carry

    lax.fori_loop(0, pieces, turn, 0)
    norm(1, keep_two)
    lse_out[...] = jnp.transpose(lse_v[...])

    saves = [
        pltpu.make_async_copy(src, dst, save_sem.at[i])
        for i, (src, dst) in enumerate(
            (
                (q_v, q_out),
                (k_v, k_out),
                (v_v, v_out),
                (mixed_v, mixed_out),
                (act_v, act_out),
                (slope_v, slope_out),
                (turned.at[0], xt_out),
                (turned.at[1], ht_out),
                (n1_v, n1_out),
                (n2_v, n2_out),
                (y_v, y_out),
            )
        )
    ]
    for copy in saves:
        copy.start()

    for k in range(KINDS):
        for step in range(1, n_tensor):
            landed(shard_ref.at[k], z_s.at[k, step])
        for step in range(n_tensor):
            tt = lax.rem(t + step, n_tensor)
            for half in range(2):
                for code in range(chips):
                    ref = block(k, tt, chip, half)
                    landed(ref, sib_s.at[k, tt, half, code])
                    if code:
                        landed(ref, xy_s.at[k, tt, half, code])
    for s in range(2):
        sent((lax.div(t, half_t) == core) & (2 * core + s == t), x_ref.at[s], x_s.at[s])
    for step in range(1, n_tensor):
        landed(bias_ref, bz_s.at[step])
    for tt in range(n_tensor):
        for j in range(2):
            landed(q_v.at[tt], kv_s.at[tt, j])
    for step in range(1, n_dp):
        landed(c_one.at[0], c1_s.at[step])
    for step in range(2 * n_dp):
        seq = lax.rem(4 * chip + step, 2 * n_dp)
        goal = 2 * lax.div(seq, 4) + lax.div(t, half_t)
        sent((goal == d) & (lax.rem(seq, 4) == t), c_two.at[0], c2_s.at[step])
    for q in range(half_t):
        for who in range(n_dp):
            landed(c_two.at[0], c2_r.at[q, who])
    for copy in saves:
        copy.wait()


def gauss(u):
    size = jnp.abs(u)
    bell = 0.3989422804014327 * jnp.exp(-0.5 * (u * u))
    s = 1.0 / (1.0 + 0.23164190 * size)
    tail = bell * s * (
        0.319381530 + s * (-0.356563782 + s * (1.781477937 + s * (-1.821255978 + s * 1.330274429)))
    )
    return bell, jnp.where(u < 0, tail, 1.0 - tail)


def run_forward(n_dp, n_tensor, undealing, lengths, vecs, x_in, cot_in, shard, biases):
    slots, span, width = x_in.shape
    rows, cols = shard.shape[1:]
    chips = n_dp // 2
    tokens = 2 * span
    group = cols // 4
    n_pos = min(n_dp, span // 16)
    prow, pcol = span // n_pos, width // (n_dp // n_pos)
    dma = pltpu.SemaphoreType.DMA
    any_space = pl.BlockSpec(memory_space=pl.ANY)
    smem = pl.BlockSpec(memory_space=pltpu.SMEM)
    vmem = pl.BlockSpec(memory_space=pltpu.VMEM)
    shapes = (
        ((2, n_dp, prow, pcol), BF),
        ((KINDS, n_tensor, width, cols), BF),
        ((n_tensor, tokens, group), BF),
        ((n_tensor, 2 * tokens, group), BF),
        ((n_tensor, 2 * tokens, group), BF),
        ((n_tensor, tokens, group), BF),
        ((n_tensor, tokens, cols), BF),
        ((n_tensor, tokens, cols), BF),
        ((2, width // 2, tokens), BF),
        ((2, width // 2, tokens), BF),
        ((tokens, width), BF),
        ((tokens, width), BF),
        ((tokens, width), BF),
        ((128, tokens), F32),
        ((2, tokens, 128), F32),
    )
    return pl.pallas_call(
        functools.partial(forward_kernel, n_dp, n_tensor),
        out_shape=tuple(jax.ShapeDtypeStruct(*shape) for shape in shapes),
        in_specs=[smem, smem, vmem, any_space, any_space, any_space, any_space],
        out_specs=(any_space,) * 13 + (vmem, vmem),
        scratch_shapes=[
            pltpu.VMEM((n_dp, slots, prow, pcol), BF),
            pltpu.VMEM((2 * n_dp, prow, pcol), BF),
            pltpu.VMEM((2, span, width), BF),
            pltpu.VMEM((n_tensor,) + biases.shape, F32),
            pltpu.VMEM((2, width, cols), BF),
            pltpu.VMEM((n_tensor, tokens, group), BF),
            pltpu.VMEM((n_tensor, 2 * tokens, group), BF),
            pltpu.VMEM((n_tensor, 2 * tokens, group), BF),
            pltpu.VMEM((n_tensor, tokens, group), BF),
            pltpu.VMEM((n_tensor, tokens, cols), BF),
            pltpu.VMEM((n_tensor, tokens, cols), BF),
            pltpu.VMEM((2, 2, width // 2, tokens), BF),
            pltpu.VMEM((tokens, width), BF),
            pltpu.VMEM((tokens, width), BF),
            pltpu.VMEM((tokens, width), BF),
            pltpu.VMEM((tokens, width), BF),
            pltpu.VMEM((tokens, width), F32),
            pltpu.VMEM((tokens, 128), F32),
            dma((2,)),
            dma((2,)),
            dma((n_dp,)),
            dma((n_dp,)),
            dma((2 * n_dp,)),
            dma((n_tensor // 2, n_dp)),
            dma((KINDS,)),
            dma((KINDS, n_tensor)),
            dma((KINDS, n_tensor)),
            dma((KINDS, n_tensor, 2, chips)),
            dma((KINDS, n_tensor, 2, chips)),
            dma((KINDS, n_tensor, 2, chips)),
            dma((KINDS, n_tensor, 2, chips)),
            dma((n_tensor, 2)),
            dma((n_tensor, 2)),
            dma((n_tensor,)),
            dma((n_tensor,)),
            dma((2,)),
            dma((11,)),
        ],
        compiler_params=pltpu.CompilerParams(
            collective_id=0, has_side_effects=True, vmem_limit_bytes=VMEM_LIMIT
        ),
        name="forward_layer",
    )(undealing, lengths, vecs, x_in, cot_in, shard, biases)


SMALL = 12


def backward_kernel(
    n_dp,
    n_tensor,
    lengths,
    vec_ref,
    lse_ref,
    rstd_ref,
    cot_ref,
    full_ref,
    q_ref,
    k_ref,
    v_ref,
    mixed_ref,
    act_ref,
    slope_ref,
    xt_ref,
    ht_ref,
    n1_ref,
    n2_ref,
    y_ref,
    sum_ref,
    small_out,
    y_out,
    lts,
    rms,
    q_v,
    k_v,
    v_v,
    n1_v,
    n2_v,
    cot_v,
    acc,
    wbuf,
    mix_grad,
    delta_v,
    dqt_v,
    kt_v,
    dkv_v,
    dkv_in,
    outbox,
    from_core,
    held,
    from_chip,
    from_z,
    small_v,
    small_in,
    load_sem,
    w_sem,
    dkv_s,
    dkv_r,
    y_s,
    y_r,
    b_s,
    b_r,
    bo_s,
    bo_r,
    core_s,
    core_r,
    xy_s,
    xy_r,
    z_s,
    z_r,
):
    d, t, chip, core = place()
    chips = n_dp // 2
    bits = chips.bit_length() - 1
    half_t = n_tensor // 2
    count = n_dp * n_tensor
    me = d * n_tensor + t
    tokens, width = acc.shape
    cols = wbuf.shape[2]
    group = q_v.shape[2]
    rows = from_z.shape[2]
    half_cols = cols // 2
    half_width = width // 2
    pieces = KINDS * n_tensor
    slots = held.shape[0]
    sibling = (d + 1 - 2 * core, t)
    length = lengths[4 * chip + t]
    mine = pl.ds(pl.multiple_of(core * tokens, tokens), tokens)
    others = pl.ds(pl.multiple_of((1 - core) * tokens, tokens), tokens)
    greet(n_dp, n_tensor)

    loads = [
        pltpu.make_async_copy(src, dst, load_sem.at[i])
        for i, (src, dst) in enumerate(
            (
                (cot_ref, cot_v),
                (n2_ref, n2_v),
                (slope_ref, rms.at[1]),
                (act_ref, rms.at[0]),
                (ht_ref, lts.at[1]),
                (n1_ref, n1_v),
                (q_ref, q_v),
                (k_ref, k_v),
                (v_ref, v_v),
                (mixed_ref, rms.at[2, :, :, pl.ds(3 * group, group)]),
                (xt_ref, lts.at[2]),
            )
        )
    ]

    def at(step):
        return lax.rem(t + step, n_tensor)

    def weights(k, step, slot):
        return pltpu.make_async_copy(full_ref.at[k, at(step)], wbuf.at[slot], w_sem.at[slot])

    for copy in loads[:2]:
        copy.start()
    weights(2, 0, 0).start()
    for copy in loads[2:4]:
        copy.start()
    weights(1, 0, 1).start()
    for copy in loads[4:]:
        copy.start()

    def send_output(a, source):
        for q in range(2):
            send_or_keep(
                (lax.div(t, half_t) == core) & (2 * core + q == t),
                source.at[q],
                y_out.at[a, lax.rem(t, half_t)],
                y_s.at[a, q],
                y_r.at[a, lax.rem(t, half_t)],
                (2 * chip + lax.div(t, half_t), 2 * core + q),
            )

    send_output(0, y_ref)

    def kind_of(index):
        return KINDS - 1 - lax.div(index, n_tensor)

    def emit(index):
        order = lax.div(index, n_tensor)
        tt = at(lax.rem(index, n_tensor))
        slot, box = lax.rem(index, slots), lax.rem(index, 2)

        @pl.when(index >= 2)
        def _():
            landed(outbox.at[0], core_s.at[index - 2])

        @pl.when(index >= slots)
        def _():
            for half in range(2):
                for code in range(1, chips):
                    landed(from_chip.at[0, 0, 0], xy_s.at[index - slots, half, code])

            @pl.when(lax.rem(index - slots, n_tensor) > 0)
            def _():
                landed(from_z.at[0, 0], z_s.at[index - slots])

        def one(n, carry):
            wide = pl.ds(pl.multiple_of(n * group, group), group)
            left = order + jnp.where((order == 2) & (n == 3), 1, 0)
            right = rms[order, tt, :, wide]
            outbox[box, :, wide] = jnp.dot(
                lts[left, 1 - core], right, preferred_element_type=F32
            ).astype(BF)
            held[slot, :, wide] = jnp.dot(
                lts[left, core], right, preferred_element_type=F32
            ).astype(BF)
            return carry

        lax.fori_loop(0, cols // group, one, 0)
        remote(
            outbox.at[box], from_core.at[slot], core_s.at[index], core_r.at[index], sibling
        ).start()

    def spot_of(code, order):
        return pl.ds(pl.multiple_of(relative(chip, order, code) * rows, rows), rows)

    def pass_on(index, s):
        slot = lax.rem(index, slots)
        for half in range(2):
            order = orders(bits)[half]
            for code in range(1 << s, 2 << s):
                remote(
                    held.at[slot, spot_of(code, order), pl.ds(half * half_cols, half_cols)],
                    from_chip.at[slot, half, code - 1],
                    xy_s.at[index, half, code],
                    xy_r.at[index, half, code],
                    (2 * flip(chip, order[s]) + core, t),
                ).start()

    def take_in(index, s):
        slot = lax.rem(index, slots)
        for half in range(2):
            order = orders(bits)[half]
            for code in range(1 << s, 2 << s):
                landed(from_chip.at[0, 0, 0], xy_r.at[index, half, code])
                spot = spot_of(code - (1 << s), order)
                wide = pl.ds(half * half_cols, half_cols)
                held[slot, spot, wide] = (
                    held[slot, spot, wide].astype(F32)
                    + from_chip[slot, half, code - 1].astype(F32)
                ).astype(BF)

    def first(index):
        slot = lax.rem(index, slots)
        landed(outbox.at[0], core_r.at[index])
        part = min(128, half_width)

        def add(c, carry):
            spot = pl.ds(pl.multiple_of(c * part, part), part)
            held[slot, spot] = (
                held[slot, spot].astype(F32) + from_core[slot, spot].astype(F32)
            ).astype(BF)
            return carry

        lax.fori_loop(0, half_width // part, add, 0)
        if bits:
            pass_on(index, bits - 1)

    def finish(index):
        slot, step = lax.rem(index, slots), lax.rem(index, n_tensor)
        source = pl.ds(pl.multiple_of(chip * rows, rows), rows)

        @pl.when(step == 0)
        def _():
            from_z[kind_of(index), 0] = held[slot, source]

        @pl.when(step > 0)
        def _():
            remote(
                held.at[slot, source],
                from_z.at[kind_of(index), step],
                z_s.at[index],
                z_r.at[index],
                (d, at(step)),
            ).start()

    def advance(index):
        @pl.when(index < pieces)
        def _():
            emit(index)

        for stage in range(bits + 1):
            earlier = index - 1 - stage

            @pl.when((earlier >= 0) & (earlier < pieces))
            def _(stage=stage, earlier=earlier):
                if stage == 0:
                    first(earlier)
                else:
                    take_in(earlier, bits - stage)
                    if stage < bits:
                        pass_on(earlier, bits - stage - 1)
                if stage == bits:
                    finish(earlier)

    def keep_small(which, row):
        for r in range(8):
            small_v[which, r : r + 1] = row[:, r * 128 : (r + 1) * 128]

    chunk = 64

    def norm_back(which, unit_ref, incoming, low_ref):
        gain = vec_ref[2 + 2 * which : 3 + 2 * which]

        def one(step, carry):
            spot = pl.ds(pl.multiple_of(step * chunk, chunk), chunk)
            e = incoming(step, spot)
            unit = unit_ref[spot].astype(F32)
            ge = e * gain
            first_mean = jnp.mean(ge, axis=-1, keepdims=True)
            second_mean = jnp.mean(ge * unit, axis=-1, keepdims=True)
            grad = (ge - first_mean - unit * second_mean) * rstd_ref[which, spot, 0:1]
            acc[spot] = grad
            low = grad.astype(BF)
            low_ref[spot] = low
            return (
                carry[0] + jnp.sum(e * unit, axis=0, keepdims=True),
                carry[1] + jnp.sum(e, axis=0, keepdims=True),
                carry[2] + jnp.sum(low.astype(F32), axis=0, keepdims=True),
            )

        zero = jnp.zeros((1, width), F32)
        return lax.fori_loop(0, tokens // chunk, one, (zero, zero, zero))

    def turn_rows(source, which):
        flat = jnp.transpose(source)
        for dev in range(n_dp):
            lts[which, dev % 2, (dev // 2) * rows : (dev // 2 + 1) * rows] = flat[
                dev * rows : (dev + 1) * rows
            ]

    loads[0].wait()
    loads[1].wait()

    def seed(step, spot):
        number = core * tokens + step * chunk + lax.broadcasted_iota(jnp.int32, (chunk, 1), 0)
        return jnp.where(number < length, cot_v[spot].astype(F32), 0.0)

    sums = norm_back(1, n2_v, seed, cot_v)
    keep_small(10, sums[0])
    keep_small(11, sums[1])
    keep_small(7, sums[2])
    turn_rows(cot_v[...], 0)
    for copy in loads[2:5]:
        copy.wait()

    def mlp(step, carry):
        tt = at(step)
        weights(2, step, 0).wait()

        def one(n, carry):
            wide = pl.ds(pl.multiple_of(n * 256, 256), 256)
            grad = jnp.dot(cot_v[...], wbuf[0, :, wide], preferred_element_type=F32)
            rms[1, tt, :, wide] = (rms[1, tt, :, wide].astype(F32) * grad).astype(BF)
            return carry

        lax.fori_loop(0, cols // 256, one, 0)

        @pl.when(step < n_tensor - 1)
        def _():
            weights(2, step + 1, 0).start()

        @pl.when(step == n_tensor - 1)
        def _():
            weights(0, 0, 0).start()

        total = jnp.sum(rms[1, tt].astype(F32), axis=0, keepdims=True)
        for r in range(8):
            small_v[3 + tt, r : r + 1] = total[:, r * 128 : (r + 1) * 128]
        weights(1, step, 1).wait()

        def two(n, carry):
            wide = pl.ds(pl.multiple_of(n * 256, 256), 256)
            acc[:, wide] += lax.dot_general(
                rms[1, tt], wbuf[1, wide, :], (((1,), (1,)), ((), ())), preferred_element_type=F32
            )
            return carry

        lax.fori_loop(0, width // 256, two, 0)

        @pl.when(step < n_tensor - 1)
        def _():
            weights(1, step + 1, 1).start()

        @pl.when(step == n_tensor - 1)
        def _():
            weights(0, 1, 1).start()

        advance(step)
        return carry

    lax.fori_loop(0, n_tensor, mlp, 0)

    loads[5].wait()
    sums = norm_back(0, n1_v, lambda step, spot: acc[spot], n2_v)
    keep_small(8, sums[0])
    keep_small(9, sums[1])
    keep_small(2, sums[2])
    turn_rows(n2_v[...], 3)
    for copy in loads[6:]:
        copy.wait()

    key_rows = min(256, 2 * tokens)
    low_lanes = lax.broadcasted_iota(jnp.int32, (tokens, 2 * HEAD_DIM), 1) < HEAD_DIM

    def prepare(step):
        tt, slot = at(step), lax.rem(step, 2)
        weights(0, step, slot).wait()
        grad = jnp.dot(
            n2_v[...], wbuf[slot, :, 3 * group :], preferred_element_type=F32
        ).astype(BF)
        mix_grad[...] = grad
        both = grad.astype(F32) * rms[2, tt, :, 3 * group :].astype(F32)
        high = both.astype(BF)
        rest = (both - high.astype(F32)).astype(BF)
        heads = lax.broadcasted_iota(jnp.int32, (8, group), 0)
        lanes = lax.broadcasted_iota(jnp.int32, (8, group), 1)
        picks = jnp.where(lax.div(lanes, HEAD_DIM) == heads, 1.0, 0.0).astype(BF)
        dims = (((1,), (1,)), ((), ()))
        delta_v[...] = lax.dot_general(
            picks, high, dims, preferred_element_type=F32
        ) + lax.dot_general(picks, rest, dims, preferred_element_type=F32)

        @pl.when(step >= 2)
        def _():
            for j in range(2):
                landed(dkv_in.at[0, 0], dkv_s.at[step - 2, j])

    def pair_back(step, pair):
        tt, slot = at(step), lax.rem(step, 2)
        wide = pl.ds(pl.multiple_of(pair * 2 * HEAD_DIM, 2 * HEAD_DIM), 2 * HEAD_DIM)
        q_pair, o_pair = q_v[tt, :, wide], mix_grad[:, wide]
        q_ones = [jnp.where(low_lanes, q_pair, 0).astype(BF), jnp.where(low_lanes, 0, q_pair).astype(BF)]
        o_ones = [jnp.where(low_lanes, o_pair, 0).astype(BF), jnp.where(low_lanes, 0, o_pair).astype(BF)]
        kt_v[...] = jnp.transpose(k_v[tt, :, wide])
        dqt_v[...] = jnp.zeros_like(dqt_v)
        dims = (((1,), (1,)), ((), ()))

        def block(b, carry):
            spot = pl.ds(pl.multiple_of(b * key_rows, key_rows), key_rows)
            k_part, v_part = k_v[tt, spot, wide], v_v[tt, spot, wide]
            number = b * key_rows + lax.broadcasted_iota(jnp.int32, (key_rows, 1), 0)
            live = number < length
            dv, dk = None, None
            for head in range(2):
                which = tt * (group // HEAD_DIM) + pair * 2 + head
                scores = lax.dot_general(k_part, q_ones[head], dims, preferred_element_type=F32)
                probs = jnp.where(live, jnp.exp(scores - lse_ref[pl.ds(which, 1)]), 0.0)
                prob_grad = lax.dot_general(v_part, o_ones[head], dims, preferred_element_type=F32)
                score_grad = (probs * (prob_grad - delta_v[pl.ds(pair * 2 + head, 1)])).astype(BF)
                one_v = jnp.dot(probs.astype(BF), o_ones[head], preferred_element_type=F32)
                one_k = jnp.dot(score_grad, q_ones[head], preferred_element_type=F32)
                dv = one_v if dv is None else dv + one_v
                dk = one_k if dk is None else dk + one_k
                rows_here = slice(head * HEAD_DIM, (head + 1) * HEAD_DIM)
                dqt_v[rows_here] += jnp.dot(
                    kt_v[rows_here, spot], score_grad, preferred_element_type=F32
                )
            dkv_v[slot, 0, spot, wide] = dk.astype(BF)
            dkv_v[slot, 1, spot, wide] = dv.astype(BF)
            return carry

        lax.fori_loop(0, 2 * tokens // key_rows, block, 0)
        dq = jnp.transpose(dqt_v[...].astype(BF).astype(F32)) * 0.125
        rms[2, tt, :, wide] = dq.astype(BF)
        total = jnp.sum(dq, axis=0, keepdims=True)
        small_v[0, pl.ds(tt * (group // 128) + pair, 1)] = total

    def exchange(step):
        slot = lax.rem(step, 2)
        for j in range(2):
            remote(
                dkv_v.at[slot, j, others],
                dkv_in.at[step, j],
                dkv_s.at[step, j],
                dkv_r.at[step, j],
                sibling,
            ).start()

    def collect(step):
        tt, slot = at(step), lax.rem(step, 2)
        for j in range(2):
            landed(dkv_in.at[0, 0], dkv_r.at[step, j])
            value = (
                dkv_v[slot, j, mine].astype(F32) + dkv_in[step, j].astype(F32)
            ).astype(BF)
            rms[2, tt, :, (1 + j) * group : (2 + j) * group] = value
            if j:
                total = jnp.sum(value.astype(F32), axis=0, keepdims=True)
                for r in range(group // 128):
                    small_v[1, pl.ds(tt * (group // 128) + r, 1)] = total[:, r * 128 : (r + 1) * 128]

        def one(n, carry):
            wide = pl.ds(pl.multiple_of(n * 256, 256), 256)
            acc[:, wide] += lax.dot_general(
                rms[2, tt, :, : 3 * group],
                wbuf[slot, wide, : 3 * group],
                (((1,), (1,)), ((), ())),
                preferred_element_type=F32,
            )
            return carry

        lax.fori_loop(0, width // 256, one, 0)

    def attention(step, carry):
        @pl.when(step < n_tensor)
        def _():
            prepare(step)
            for pair in range(group // (2 * HEAD_DIM)):
                pair_back(step, pair)

                @pl.when(step < 2)
                def _(pair=pair):
                    advance(n_tensor + 2 * step + pair)

            exchange(step)

        @pl.when(step >= 1)
        def _():
            collect(step - 1)

            @pl.when(step < n_tensor - 1)
            def _():
                weights(0, step + 1, lax.rem(step + 1, 2)).start()

            advance(2 * n_tensor + step - 1)

        return carry

    lax.fori_loop(0, n_tensor + 1, attention, 0)

    for q in range(2):
        cot_v[pl.ds(q * (tokens // 2), tokens // 2)] = acc[
            pl.ds(q * (tokens // 2), tokens // 2)
        ].astype(BF)
    for q in range(2):
        send_or_keep(
            (lax.div(t, half_t) == core) & (2 * core + q == t),
            cot_v.at[pl.ds(q * (tokens // 2), tokens // 2)],
            y_out.at[1, lax.rem(t, half_t)],
            y_s.at[1, q],
            y_r.at[1, lax.rem(t, half_t)],
            (2 * chip + lax.div(t, half_t), 2 * core + q),
        )
    for j in range(SMALL):
        send_or_keep(
            me == j,
            small_v.at[j],
            small_in.at[me],
            b_s.at[j],
            b_r.at[me],
            (j // n_tensor, j % n_tensor),
        )
    advance(jnp.int32(pieces))

    @pl.when(me < SMALL)
    def _():
        def arrive(step, total):
            landed(small_in.at[0], b_r.at[step])
            return total + small_in[step]

        total = lax.fori_loop(0, count, arrive, jnp.zeros(small_in.shape[1:], F32))
        small_in[0] = total
        pltpu.make_async_copy(small_in.at[0], small_out.at[me], bo_r.at[me]).start()

        def spread(step, carry):
            other = lax.rem(me + step, count)
            remote(
                small_in.at[0],
                small_out.at[me],
                bo_s.at[step],
                bo_r.at[me],
                (lax.div(other, n_tensor), lax.rem(other, n_tensor)),
            ).start()
            return carry

        lax.fori_loop(1, count, spread, 0)

    for index in range(pieces + 1, pieces + 1 + bits):
        advance(jnp.int32(index))

    for k in range(KINDS):
        total = from_z[k, 0].astype(F32)
        for step in range(1, n_tensor):
            landed(from_z.at[0, 0], z_r.at[(KINDS - 1 - k) * n_tensor + step])
            total = total + from_z[k, step].astype(F32)
        sum_ref[k] = total

    for j in range(SMALL):
        landed(small_v.at[0], bo_r.at[j])
        sent(me == j, small_v.at[0], b_s.at[j])

    @pl.when(me < SMALL)
    def _():
        def gone(step, carry):
            landed(small_v.at[0], bo_s.at[step])
            return carry

        lax.fori_loop(1, count, gone, 0)

    for a in range(2):
        for q in range(2):
            sent((lax.div(t, half_t) == core) & (2 * core + q == t), y_ref.at[q], y_s.at[a, q])
            landed(y_ref.at[q], y_r.at[a, q])
    for step in range(n_tensor - 2, n_tensor):
        for j in range(2):
            landed(dkv_in.at[0, 0], dkv_s.at[step, j])
    for index in range(pieces - 2, pieces):
        landed(outbox.at[0], core_s.at[index])
    for index in range(pieces - slots, pieces):
        for half in range(2):
            for code in range(1, chips):
                landed(from_chip.at[0, 0, 0], xy_s.at[index, half, code])
        if index % n_tensor:
            landed(from_z.at[0, 0], z_s.at[index])


def run_backward(n_dp, n_tensor, lengths, vecs, lse, rstd, cot, full, saved):
    tokens, width = cot.shape
    cols = full.shape[3]
    group = cols // 4
    rows = width // n_dp
    chips = n_dp // 2
    pieces = KINDS * n_tensor
    count = n_dp * n_tensor
    slots = 4
    dma = pltpu.SemaphoreType.DMA
    any_space = pl.BlockSpec(memory_space=pl.ANY)
    smem = pl.BlockSpec(memory_space=pltpu.SMEM)
    vmem = pl.BlockSpec(memory_space=pltpu.VMEM)
    return pl.pallas_call(
        functools.partial(backward_kernel, n_dp, n_tensor),
        out_shape=(
            jax.ShapeDtypeStruct((KINDS, rows, cols), F32),
            jax.ShapeDtypeStruct((SMALL, 8, 128), F32),
            jax.ShapeDtypeStruct((2, 2, tokens // 2, width), BF),
        ),
        in_specs=[smem, vmem, vmem, vmem] + [any_space] * (2 + len(saved)),
        out_specs=(vmem, any_space, any_space),
        scratch_shapes=[
            pltpu.VMEM((4, 2, width // 2, tokens), BF),
            pltpu.VMEM((KINDS, n_tensor, tokens, cols), BF),
            pltpu.VMEM((n_tensor, tokens, group), BF),
            pltpu.VMEM((n_tensor, 2 * tokens, group), BF),
            pltpu.VMEM((n_tensor, 2 * tokens, group), BF),
            pltpu.VMEM((tokens, width), BF),
            pltpu.VMEM((tokens, width), BF),
            pltpu.VMEM((tokens, width), BF),
            pltpu.VMEM((tokens, width), F32),
            pltpu.VMEM((2, width, cols), BF),
            pltpu.VMEM((tokens, group), BF),
            pltpu.VMEM((8, tokens), F32),
            pltpu.VMEM((2 * HEAD_DIM, tokens), F32),
            pltpu.VMEM((2 * HEAD_DIM, 2 * tokens), BF),
            pltpu.VMEM((2, 2, 2 * tokens, group), BF),
            pltpu.VMEM((n_tensor, 2, tokens, group), BF),
            pltpu.VMEM((2, width // 2, cols), BF),
            pltpu.VMEM((slots, width // 2, cols), BF),
            pltpu.VMEM((slots, width // 2, cols), BF),
            pltpu.VMEM((slots, 2, max(chips - 1, 1), rows, cols // 2), BF),
            pltpu.VMEM((KINDS, n_tensor, rows, cols), BF),
            pltpu.VMEM((SMALL, 8, 128), F32),
            pltpu.VMEM((count, 8, 128), F32),
            dma((11,)),
            dma((2,)),
            dma((n_tensor, 2)),
            dma((n_tensor, 2)),
            dma((2, 2)),
            dma((2, 2)),
            dma((SMALL,)),
            dma((count,)),
            dma((count,)),
            dma((SMALL,)),
            dma((pieces,)),
            dma((pieces,)),
            dma((pieces, 2, chips)),
            dma((pieces, 2, chips)),
            dma((pieces,)),
            dma((pieces,)),
        ],
        compiler_params=pltpu.CompilerParams(
            collective_id=1, has_side_effects=True, vmem_limit_bytes=VMEM_LIMIT
        ),
        name="backward_layer",
    )(lengths, vecs, lse, rstd, cot, full, *saved)


def shards(
    n_dp,
    n_tensor,
    inputs,
    cotangent,
    lengths,
    dealing,
    undealing,
    query_weight,
    key_weight,
    value_weight,
    output_weight,
    up_weight,
    down_weight,
    query_bias,
    value_bias,
    output_bias,
    up_bias,
    down_bias,
    first_gain,
    first_shift,
    second_gain,
    second_shift,
):
    span, slots, width = inputs.shape
    group = query_weight.shape[1]
    shard = jnp.stack(
        [
            jnp.concatenate([query_weight, key_weight, value_weight, output_weight.T], axis=1),
            up_weight,
            down_weight.T,
        ]
    ).astype(BF)
    blank = jnp.zeros((group,), F32)
    biases = jnp.concatenate([query_bias, value_bias, up_bias, blank, blank]).reshape(8, group)
    vecs = jnp.stack([output_bias, down_bias, first_gain, first_shift, second_gain, second_shift])
    vecs = jnp.pad(vecs, ((0, 2), (0, 0)))
    (
        cot_loc, full, query, key, value, mixed, activated, slope, x_t, h_t, n1, n2, y, lse, rstd
    ) = run_forward(
        n_dp,
        n_tensor,
        undealing,
        lengths,
        vecs,
        jnp.transpose(inputs, (1, 0, 2)),
        jnp.transpose(cotangent, (1, 0, 2)),
        shard,
        biases,
    )
    n_col = width // cot_loc.shape[3]
    cot = cot_loc.reshape(2, n_dp // n_col, n_col, *cot_loc.shape[2:])
    cot = jnp.transpose(cot, (0, 1, 3, 2, 4)).reshape(2 * span, width)
    sums, small, returned = run_backward(
        n_dp,
        n_tensor,
        lengths,
        vecs,
        lse,
        rstd,
        cot,
        full,
        (query, key, value, mixed, activated, slope, x_t, h_t, n1, n2, y.reshape(2, span, width)),
    )
    returned = jnp.transpose(returned, (0, 2, 1, 3))
    small = small.reshape(SMALL, width)
    t = lax.axis_index("tensor")

    def mine(row):
        return lax.dynamic_slice(small[row], (t * group,), (group,))

    return (
        returned[0],
        returned[1],
        sums[0][:, :group],
        sums[0][:, group : 2 * group],
        sums[0][:, 2 * group : 3 * group],
        sums[0][:, 3 * group :].T,
        sums[1],
        sums[2].T,
        mine(0),
        mine(1),
        small[2],
        lax.dynamic_index_in_dim(small, 3 + t, 0, keepdims=False),
        small[7],
        small[8],
        small[9],
        small[10],
        small[11],
    )


def solution(mesh):
    tokens = P("tensor", "dp", None)
    rows, columns = P("dp", "tensor"), P("tensor", "dp")
    split, copied = P("tensor"), P()
    return jax.shard_map(
        functools.partial(shards, mesh.shape["dp"], mesh.shape["tensor"]),
        mesh=mesh,
        in_specs=(
            (tokens, tokens, copied, copied, copied)
            + (rows, rows, rows, columns, rows, columns)
            + (split, split, copied, split, copied, copied, copied, copied, copied)
        ),
        out_specs=(
            (tokens, tokens, rows, rows, rows, columns, rows, columns)
            + (split, split, copied, split, copied, copied, copied, copied, copied)
        ),
        check_vma=False,
    )
```

```python
import functools

import jax
import jax.numpy as jnp
from jax import lax
from jax.experimental import pallas as pl
from jax.experimental.pallas import tpu as pltpu
from jax.sharding import PartitionSpec as P

HEAD_DIM = 64
KINDS = 3
MESH = pl.DeviceIdType.MESH
VMEM_LIMIT = 63 << 20
BF = jnp.bfloat16
F32 = jnp.float32


def flip(index, bit):
    unit = 1 << bit
    return index + unit * (1 - 2 * lax.rem(lax.div(index, unit), 2))


def orders(bits):
    return (tuple(range(bits)), tuple(reversed(range(bits))))


def relative(chip, order, code):
    for place, bit in enumerate(order):
        if code >> place & 1:
            chip = flip(chip, bit)
    return chip


def place():
    d, t = lax.axis_index("dp"), lax.axis_index("tensor")
    return d, t, lax.div(d, 2), lax.rem(d, 2)


def greet(n_dp, n_tensor):
    d, t, _, _ = place()
    barrier = pltpu.get_barrier_semaphore()
    me = d * n_tensor + t
    count = n_dp * n_tensor

    def one(step, carry):
        other = lax.rem(me + step, count)
        pl.semaphore_signal(
            barrier,
            inc=1,
            device_id=(lax.div(other, n_tensor), lax.rem(other, n_tensor)),
            device_id_type=MESH,
        )
        return carry

    lax.fori_loop(1, count, one, 0)
    pl.semaphore_wait(barrier, count - 1)


def remote(src, dst, ssem, rsem, device):
    return pltpu.make_async_remote_copy(
        src_ref=src,
        dst_ref=dst,
        send_sem=ssem,
        recv_sem=rsem,
        device_id=device,
        device_id_type=MESH,
    )


def landed(ref, sem):
    pltpu.make_async_copy(ref, ref, sem).wait()


def send_or_keep(mine, src, dst, ssem, rsem, device):
    @pl.when(mine)
    def _():
        pltpu.make_async_copy(src, dst, rsem).start()

    @pl.when(jnp.logical_not(mine))
    def _():
        remote(src, dst, ssem, rsem, device).start()


def sent(mine, src, ssem):
    @pl.when(jnp.logical_not(mine))
    def _():
        landed(src, ssem)


LAG = 2
SMALL = 12
SLOTS = 4
COT_ONE, COT_TWO = 3, 8


def layer_kernel(
    n_dp,
    n_tensor,
    undealing,
    lengths,
    vec_ref,
    x_ref,
    cot_ref,
    shard_ref,
    bias_ref,
    full_ref,
    sum_ref,
    small_out,
    y_out,
    c_one,
    c_two,
    bias_v,
    wbuf,
    q_v,
    k_v,
    v_v,
    lts,
    rms,
    n1_v,
    n2_v,
    cot_v,
    y_v,
    acc,
    lse_v,
    lse_rows,
    rstd_v,
    mix_grad,
    delta_v,
    dqt_v,
    kt_v,
    dkv_v,
    dkv_in,
    outbox,
    from_core,
    held,
    from_chip,
    from_z,
    small_v,
    small_in,
    x_s,
    x_r,
    c1_s,
    c1_r,
    c2_s,
    c2_r,
    own_sem,
    gz_s,
    gz_r,
    gxy_s,
    gxy_r,
    sib_s,
    sib_r,
    kv_s,
    kv_r,
    bz_s,
    bz_r,
    w_sem,
    dkv_s,
    dkv_r,
    y_s,
    y_r,
    b_s,
    b_r,
    bo_s,
    bo_r,
    core_s,
    core_r,
    xy_s,
    xy_r,
    z_s,
    z_r,
):
    d, t, chip, core = place()
    chips = n_dp // 2
    bits = chips.bit_length() - 1
    half_t = n_tensor // 2
    count = n_dp * n_tensor
    me = d * n_tensor + t
    rows, cols = shard_ref.shape[1:]
    half_cols = cols // 2
    group = q_v.shape[2]
    span, width = x_ref.shape[1:]
    half_width = width // 2
    tokens = 2 * span
    units = cols
    prow, pcol = c_one.shape[2:]
    n_col = width // pcol
    pieces = KINDS * n_tensor
    sibling = (d + 1 - 2 * core, t)
    length = lengths[4 * chip + t]
    mine = pl.ds(pl.multiple_of(core * tokens, tokens), tokens)
    others = pl.ds(pl.multiple_of((1 - core) * tokens, tokens), tokens)
    greet(n_dp, n_tensor)

    def block(k, tt, who, half):
        return full_ref.at[
            k,
            tt,
            pl.ds(pl.multiple_of((2 * who + core) * rows, rows), rows),
            pl.ds(half * half_cols, half_cols),
        ]

    def arriving(index):
        rest, others = index - KINDS, n_tensor - 1
        return jnp.where(
            index < KINDS,
            index * n_tensor,
            lax.div(rest, others) * n_tensor + 1 + lax.rem(rest, others),
        )

    def stripe(k, tt):
        return full_ref.at[k, tt, pl.ds(pl.multiple_of(d * rows, rows), rows)]

    def at(index):
        step = lax.rem(index, n_tensor)
        near = jnp.where(t < half_t, t, n_tensor - 1 - t)
        spot = jnp.where(step <= near, near - step, step)
        return lax.div(index, n_tensor), jnp.where(t < half_t, spot, n_tensor - 1 - spot)

    for k in range(KINDS):
        pltpu.make_async_copy(shard_ref.at[k], stripe(k, t), own_sem.at[k]).start()

    def relay(index):
        k, tt = at(index)

        @pl.when(tt != t)
        def _():
            landed(shard_ref.at[0], gz_r.at[k, tt])

        for way, wanted in ((1, (tt <= t) & (t < n_tensor - 1)), (0, (tt >= t) & (t > 0))):

            @pl.when(wanted)
            def _(way=way):
                remote(
                    stripe(k, tt),
                    stripe(k, tt),
                    gz_s.at[k, tt, way],
                    gz_r.at[k, tt],
                    (d, t + 2 * way - 1),
                ).start()

    def relayed(k, tt):
        for way, wanted in ((1, (tt <= t) & (t < n_tensor - 1)), (0, (tt >= t) & (t > 0))):

            @pl.when(wanted)
            def _(way=way):
                landed(shard_ref.at[0], gz_s.at[k, tt, way])

    def start_tokens():
        for s in range(2):
            send_or_keep(
                (lax.div(t, half_t) == core) & (2 * core + s == t),
                x_ref.at[s],
                outbox.at[0, pl.ds(pl.multiple_of(lax.rem(t, half_t) * span, span), span)],
                x_s.at[s],
                x_r.at[lax.rem(t, half_t)],
                (2 * chip + lax.div(t, half_t), 2 * core + s),
            )
        pltpu.make_async_copy(bias_ref, bias_v.at[t], bz_r.at[0]).start()
        for step in range(1, n_tensor):
            remote(
                bias_ref,
                bias_v.at[t],
                bz_s.at[step],
                bz_r.at[step],
                (d, lax.rem(t + step, n_tensor)),
            ).start()

    def piece(who):
        return cot_ref.at[
            :,
            pl.ds(pl.multiple_of(lax.div(who, n_col) * prow, prow), prow),
            pl.ds(pl.multiple_of(lax.rem(who, n_col) * pcol, pcol), pcol),
        ]

    def cot_first():
        pltpu.make_async_copy(piece(d), c_one.at[d], c1_r.at[0]).start()
        for step in range(1, n_dp):
            who = lax.rem(d + step, n_dp)
            remote(piece(who), c_one.at[d], c1_s.at[step], c1_r.at[step], (who, t)).start()

    def cot_second():
        for step in range(n_dp):
            landed(c_one.at[0], c1_r.at[step])
        count = 2 * n_dp
        for step in range(count):
            seq = lax.rem(4 * chip + step, count)
            slot = undealing[seq]
            c_two[seq] = c_one[lax.div(slot, 2), lax.rem(slot, 2)]
            goal = 2 * lax.div(seq, 4) + lax.div(t, half_t)
            send_or_keep(
                (goal == d) & (lax.rem(seq, 4) == t),
                c_two.at[seq],
                cot_v.at[
                    pl.ds(
                        pl.multiple_of(lax.rem(t, half_t) * span + lax.div(d, n_col) * prow, prow),
                        prow,
                    ),
                    pl.ds(pl.multiple_of(lax.rem(d, n_col) * pcol, pcol), pcol),
                ],
                c2_s.at[step],
                c2_r.at[lax.rem(t, half_t), d],
                (goal, lax.rem(seq, 4)),
            )

    def forward(k, tt, half, code):
        order = orders(bits)[half]
        ref = block(k, tt, relative(chip, order, code), half)
        for s in range(code.bit_length(), bits):
            target = code | 1 << s
            remote(
                ref,
                ref,
                gxy_s.at[k, tt, half],
                gxy_r.at[k, tt, half, target],
                (2 * flip(chip, order[s]) + core, t),
            ).start()
        remote(
            ref, ref, sib_s.at[k, tt, half], sib_r.at[k, tt, half, code], sibling
        ).start()

    def receive(index, codes):
        k, tt = at(arriving(index))
        for code in codes:
            for half in range(2):
                landed(block(k, tt, chip, half), gxy_r.at[k, tt, half, code])
                forward(k, tt, half, code)

    early, late = range(1, max(chips // 2, 1)), range(max(chips // 2, 1), chips)

    def comm_step(index):
        follow = index + KINDS
        others = n_tensor - 1

        @pl.when(follow < pieces)
        def _():
            relay(arriving(follow))

            @pl.when((lax.rem(index, others) == others - 1) & (follow + 1 < pieces))
            def _():
                relay(lax.div(index, others) * n_tensor + n_tensor)

        @pl.when((index + 2 >= KINDS) & (index + 2 < pieces))
        def _():
            k, tt = at(arriving(index + 2))
            for half in range(2):
                forward(k, tt, half, 0)

        @pl.when(index < pieces)
        def _():
            receive(index, early)

        @pl.when(index >= LAG)
        def _():
            receive(index - LAG, late)

    def load(index):
        k, tt = at(index)
        slot = lax.rem(index, 2)
        for half in range(2):
            for code in range(chips):
                landed(block(k, tt, chip, half), sib_r.at[k, tt, half, code])
        copy = pltpu.make_async_copy(full_ref.at[k, tt], wbuf.at[slot], w_sem.at[slot])
        copy.start()
        copy.wait()

    def project(index):
        _, tt = at(index)
        slot = lax.rem(index, 2)
        x = outbox[0]
        for c in range(3):
            out = jnp.dot(
                x, wbuf[slot, :, c * group : (c + 1) * group], preferred_element_type=F32
            )
            if c == 0:
                q_v[tt] = ((out + bias_v[tt, 0:1]) * 0.125).astype(BF)
            elif c == 1:
                k_v[tt, mine] = out.astype(BF)
            else:
                v_v[tt, mine] = (out + bias_v[tt, 1:2]).astype(BF)
        for j, ref in enumerate((k_v, v_v)):
            remote(
                ref.at[tt, mine], ref.at[tt, mine], kv_s.at[tt, j], kv_r.at[tt, j], sibling
            ).start()

    def attend(index):
        _, tt = at(index)
        slot = lax.rem(index, 2)
        for j, ref in enumerate((k_v, v_v)):
            landed(ref.at[tt, mine], kv_r.at[tt, j])
        block_rows = min(256, tokens)
        low = lax.broadcasted_iota(jnp.int32, (block_rows, 2 * HEAD_DIM), 1) < HEAD_DIM
        lanes = lax.broadcasted_iota(jnp.int32, (block_rows, lse_v.shape[1]), 1)
        live = lax.broadcasted_iota(jnp.int32, (1, 2 * tokens), 1) < length

        def pair_step(step, carry):
            pair, part = lax.div(step, tokens // block_rows), lax.rem(step, tokens // block_rows)
            wide = pl.ds(pl.multiple_of(pair * 2 * HEAD_DIM, 2 * HEAD_DIM), 2 * HEAD_DIM)
            spot = pl.ds(pl.multiple_of(part * block_rows, block_rows), block_rows)
            k_pair, v_pair = k_v[tt, :, wide], v_v[tt, :, wide]
            q_pair = q_v[tt, spot, wide]
            outs = []
            for head in range(2):
                q_one = jnp.where(low if head == 0 else jnp.logical_not(low), q_pair, 0).astype(BF)
                scores = lax.dot_general(
                    q_one, k_pair, (((1,), (1,)), ((), ())), preferred_element_type=F32
                )
                scores = jnp.where(live, scores, -1000000000.0)
                summit = jnp.max(scores, axis=-1, keepdims=True)
                raised = jnp.exp(scores - summit)
                total = jnp.sum(raised, axis=-1, keepdims=True)
                out = jnp.dot(raised.astype(BF), v_pair, preferred_element_type=F32)
                outs.append(out / total)
                number = tt * (group // HEAD_DIM) + pair * 2 + head
                lse_v[spot] = jnp.where(lanes == number, summit + jnp.log(total), lse_v[spot])
            rms[2, tt, spot, pl.ds(pl.multiple_of(3 * group + pair * 2 * HEAD_DIM, 2 * HEAD_DIM), 2 * HEAD_DIM)] = jnp.where(low, outs[0], outs[1]).astype(BF)
            return carry

        lax.fori_loop(0, (group // (2 * HEAD_DIM)) * (tokens // block_rows), pair_step, 0)
        for n in range(width // 256):
            acc[:, n * 256 : (n + 1) * 256] += lax.dot_general(
                rms[2, tt, :, 3 * group :],
                wbuf[slot, n * 256 : (n + 1) * 256, 3 * group :],
                (((1,), (1,)), ((), ())),
                preferred_element_type=F32,
            )

    chunk = 64

    def norm(which, keep):
        gain, shift = vec_ref[2 + 2 * which : 3 + 2 * which], vec_ref[3 + 2 * which : 4 + 2 * which]

        def one(step, carry):
            spot = pl.ds(pl.multiple_of(step * chunk, chunk), chunk)
            value = acc[spot]
            center = value - jnp.mean(value, axis=-1, keepdims=True)
            spread = jnp.mean(center * center, axis=-1, keepdims=True)
            inverse = lax.rsqrt(spread + 1e-05)
            unit = center * inverse
            rstd_v[which, spot] = jnp.broadcast_to(inverse, (chunk, rstd_v.shape[2]))
            keep(spot, unit, unit * gain + shift)
            return carry

        lax.fori_loop(0, tokens // chunk, one, 0)

    def keep_one(spot, unit, hidden):
        n1_v[spot] = unit.astype(BF)
        outbox[1, spot] = hidden.astype(BF)
        acc[spot] = hidden + vec_ref[1:2]

    def keep_two(spot, unit, hidden):
        n2_v[spot] = unit.astype(BF)
        y_v[spot] = hidden.astype(BF)

    def turn_rows(source, which):
        flat = jnp.transpose(source)
        for dev in range(n_dp):
            lts[which, dev % 2, (dev // 2) * rows : (dev // 2 + 1) * rows] = flat[
                dev * rows : (dev + 1) * rows
            ]

    def expand(index):
        _, tt = at(index)
        slot = lax.rem(index, 2)

        def one(n, carry):
            wide = pl.ds(pl.multiple_of(n * 256, 256), 256)
            u = jnp.dot(outbox[1], wbuf[slot, :, wide], preferred_element_type=F32)
            u = u + bias_v[tt, pl.ds(2 + n, 1)]
            bell, below = gauss(u)
            rms[0, tt, :, wide] = (u * below).astype(BF)
            rms[1, tt, :, wide] = (below + u * bell).astype(BF)
            return carry

        lax.fori_loop(0, units // 256, one, 0)

    def contract(index):
        _, tt = at(index)
        slot = lax.rem(index, 2)

        def one(n, carry):
            wide = pl.ds(pl.multiple_of(n * 256, 256), 256)
            acc[:, wide] += lax.dot_general(
                rms[0, tt], wbuf[slot, wide, :], (((1,), (1,)), ((), ())), preferred_element_type=F32
            )
            return carry

        lax.fori_loop(0, width // 256, one, 0)

    landed(shard_ref.at[0], own_sem.at[0])
    relay(jnp.int32(0))
    start_tokens()
    for k in range(KINDS):
        if k:
            landed(shard_ref.at[0], own_sem.at[k])
        for half in range(2):
            forward(k, t, half, 0)
    for s in range(2):
        landed(x_ref.at[s], x_r.at[s])
    for step in range(n_tensor):
        landed(bias_ref, bz_r.at[step])
    acc[...] = outbox[0].astype(F32) + vec_ref[0:1]
    turn_rows(outbox[0], 2)
    lse_v[...] = jnp.zeros_like(lse_v)

    def turn(index, carry):
        comm_step(index)
        done = index - LAG

        @pl.when((done == 1) | ((done >= 4) & (done <= 6)))
        def _():
            attend(jnp.where(done == 1, 0, done - 3))

        @pl.when((done == 0) | ((done >= 3) & (done <= 5)))
        def _():
            group_index = jnp.where(done == 0, 0, done - 2)
            load(group_index)
            project(group_index)

        @pl.when(index == COT_ONE)
        def _():
            cot_first()

        @pl.when(index == COT_TWO)
        def _():
            cot_second()

        @pl.when(done == 6)
        def _():
            norm(0, keep_one)
            turn_rows(outbox[1], 1)
            lse_rows[...] = jnp.transpose(lse_v[...])

        def up(step, carry):
            load(step)
            expand(step)
            return carry

        def down(step, carry):
            load(step)
            contract(step)
            return carry

        lax.fori_loop(
            jnp.where(done == 8, 6, 4), jnp.where(done == 7, 6, jnp.where(done == 8, 8, 4)), up, 0
        )
        lax.fori_loop(
            jnp.where(done == 9, 8, jnp.where(done > 9, done, 8)),
            jnp.where(done == 9, 10, jnp.where(done > 9, done + 1, 8)),
            down,
            0,
        )
        return carry

    lax.fori_loop(0, pieces + LAG, turn, 0)
    norm(1, keep_two)

    def rat(step):
        return lax.rem(t + 1 + step, n_tensor)

    def weights(k, step, slot):
        return pltpu.make_async_copy(full_ref.at[k, rat(step)], wbuf.at[slot], w_sem.at[slot])

    def send_output(a, source):
        for q in range(2):
            send_or_keep(
                (lax.div(t, half_t) == core) & (2 * core + q == t),
                source.at[pl.ds(q * span, span)],
                y_out.at[a, lax.rem(t, half_t)],
                y_s.at[a, q],
                y_r.at[a, lax.rem(t, half_t)],
                (2 * chip + lax.div(t, half_t), 2 * core + q),
            )


    def kind_of(index):
        return KINDS - 1 - lax.div(index, n_tensor)

    def emit(index):
        order = lax.div(index, n_tensor)
        tt = rat(lax.rem(index, n_tensor))
        slot, box = lax.rem(index, SLOTS), lax.rem(index, 2)

        @pl.when(index >= 2)
        def _():
            landed(outbox.at[0], core_s.at[index - 2])

        @pl.when(index >= SLOTS)
        def _():
            for half in range(2):
                landed(from_chip.at[0, 0], xy_s.at[index - SLOTS, half])

            @pl.when(lax.rem(index - SLOTS, n_tensor) < n_tensor - 1)
            def _():
                landed(from_z.at[0, 0], z_s.at[index - SLOTS])

        def one(n, carry):
            wide = pl.ds(pl.multiple_of(n * group, group), group)
            left = order + jnp.where((order == 2) & (n == 3), 1, 0)
            right = rms[order, tt, :, wide]
            outbox[box, :, wide] = jnp.dot(
                lts[left, 1 - core], right, preferred_element_type=F32
            ).astype(BF)
            held[slot, :, wide] = jnp.dot(
                lts[left, core], right, preferred_element_type=F32
            ).astype(BF)
            return carry

        lax.fori_loop(0, cols // group, one, 0)
        remote(
            outbox.at[box], from_core.at[slot], core_s.at[index], core_r.at[index], sibling
        ).start()

    def spot_of(code, order):
        return pl.ds(pl.multiple_of(relative(chip, order, code) * rows, rows), rows)

    def pass_on(index, s):
        slot = lax.rem(index, SLOTS)
        for half in range(2):
            order = orders(bits)[half]
            for code in range(1 << s, 2 << s):
                remote(
                    held.at[slot, spot_of(code, order), pl.ds(half * half_cols, half_cols)],
                    from_chip.at[slot, half, code - 1],
                    xy_s.at[index, half],
                    xy_r.at[index, half, code],
                    (2 * flip(chip, order[s]) + core, t),
                ).start()

    def take_in(index, s):
        slot = lax.rem(index, SLOTS)
        for half in range(2):
            order = orders(bits)[half]
            for code in range(1 << s, 2 << s):
                landed(from_chip.at[0, 0, 0], xy_r.at[index, half, code])
                spot = spot_of(code - (1 << s), order)
                wide = pl.ds(half * half_cols, half_cols)
                held[slot, spot, wide] = (
                    held[slot, spot, wide].astype(F32)
                    + from_chip[slot, half, code - 1].astype(F32)
                ).astype(BF)

    def first(index):
        slot = lax.rem(index, SLOTS)
        landed(outbox.at[0], core_r.at[index])
        part = min(128, half_width)

        def add(c, carry):
            spot = pl.ds(pl.multiple_of(c * part, part), part)
            held[slot, spot] = (
                held[slot, spot].astype(F32) + from_core[slot, spot].astype(F32)
            ).astype(BF)
            return carry

        lax.fori_loop(0, half_width // part, add, 0)
        if bits:
            pass_on(index, bits - 1)

    def finish(index):
        slot, step = lax.rem(index, SLOTS), lax.rem(index, n_tensor)
        source = pl.ds(pl.multiple_of(chip * rows, rows), rows)

        @pl.when(step == n_tensor - 1)
        def _():
            from_z[kind_of(index), step] = held[slot, source]

        @pl.when(step < n_tensor - 1)
        def _():
            remote(
                held.at[slot, source],
                from_z.at[kind_of(index), step],
                z_s.at[index],
                z_r.at[index],
                (d, rat(step)),
            ).start()

    def advance(index):
        @pl.when(index < pieces)
        def _():
            emit(index)

        for stage in range(bits + 1):
            earlier = index - 1 - stage

            @pl.when((earlier >= 0) & (earlier < pieces))
            def _(stage=stage, earlier=earlier):
                if stage == 0:
                    first(earlier)
                else:
                    take_in(earlier, bits - stage)
                    if stage < bits:
                        pass_on(earlier, bits - stage - 1)
                if stage == bits:
                    finish(earlier)

    def keep_small(which, row):
        for r in range(8):
            small_v[which, r : r + 1] = row[:, r * 128 : (r + 1) * 128]

    def norm_back(which, unit_ref, incoming, low_ref):
        gain = vec_ref[2 + 2 * which : 3 + 2 * which]

        def one(step, carry):
            spot = pl.ds(pl.multiple_of(step * chunk, chunk), chunk)
            e = incoming(step, spot)
            unit = unit_ref[spot].astype(F32)
            ge = e * gain
            first_mean = jnp.mean(ge, axis=-1, keepdims=True)
            second_mean = jnp.mean(ge * unit, axis=-1, keepdims=True)
            grad = (ge - first_mean - unit * second_mean) * rstd_v[which, spot, 0:1]
            acc[spot] = grad
            low = grad.astype(BF)
            low_ref[spot] = low
            return (
                carry[0] + jnp.sum(e * unit, axis=0, keepdims=True),
                carry[1] + jnp.sum(e, axis=0, keepdims=True),
                carry[2] + jnp.sum(low.astype(F32), axis=0, keepdims=True),
            )

        zero = jnp.zeros((1, width), F32)
        return lax.fori_loop(0, tokens // chunk, one, (zero, zero, zero))

    for q in range(half_t):
        for who in range(n_dp):
            landed(c_two.at[0], c2_r.at[q, who])
    weights(2, 0, 0).start()
    weights(1, 0, 1).start()
    send_output(0, y_v)

    def seed(step, spot):
        number = core * tokens + step * chunk + lax.broadcasted_iota(jnp.int32, (chunk, 1), 0)
        return jnp.where(number < length, cot_v[spot].astype(F32), 0.0)

    sums = norm_back(1, n2_v, seed, cot_v)
    keep_small(10, sums[0])
    keep_small(11, sums[1])
    keep_small(7, sums[2])
    turn_rows(cot_v[...], 0)
    advance(jnp.int32(0))

    def mlp(step, carry):
        tt = rat(step)
        weights(2, step, 0).wait()

        def one(n, carry):
            wide = pl.ds(pl.multiple_of(n * 256, 256), 256)
            grad = jnp.dot(cot_v[...], wbuf[0, :, wide], preferred_element_type=F32)
            rms[1, tt, :, wide] = (rms[1, tt, :, wide].astype(F32) * grad).astype(BF)
            return carry

        lax.fori_loop(0, cols // 256, one, 0)

        @pl.when(step < n_tensor - 1)
        def _():
            weights(2, step + 1, 0).start()

        @pl.when(step == n_tensor - 1)
        def _():
            weights(0, 0, 0).start()

        total = jnp.sum(rms[1, tt].astype(F32), axis=0, keepdims=True)
        for r in range(8):
            small_v[3 + tt, r : r + 1] = total[:, r * 128 : (r + 1) * 128]
        weights(1, step, 1).wait()

        def two(n, carry):
            wide = pl.ds(pl.multiple_of(n * 256, 256), 256)
            acc[:, wide] += lax.dot_general(
                rms[1, tt], wbuf[1, wide, :], (((1,), (1,)), ((), ())), preferred_element_type=F32
            )
            return carry

        lax.fori_loop(0, width // 256, two, 0)

        @pl.when(step < n_tensor - 1)
        def _():
            weights(1, step + 1, 1).start()

        @pl.when(step == n_tensor - 1)
        def _():
            weights(0, 1, 1).start()

        @pl.when(lax.rem(step, 2) == 1)
        def _():
            advance(1 + lax.div(step, 2))

        return carry

    lax.fori_loop(0, n_tensor, mlp, 0)

    sums = norm_back(0, n1_v, lambda step, spot: acc[spot], n2_v)
    keep_small(8, sums[0])
    keep_small(9, sums[1])
    keep_small(2, sums[2])
    turn_rows(n2_v[...], 3)

    key_rows = min(256, 2 * tokens)
    low_lanes = lax.broadcasted_iota(jnp.int32, (tokens, 2 * HEAD_DIM), 1) < HEAD_DIM

    def prepare(step):
        tt, slot = rat(step), lax.rem(step, 2)
        weights(0, step, slot).wait()
        grad = jnp.dot(
            n2_v[...], wbuf[slot, :, 3 * group :], preferred_element_type=F32
        ).astype(BF)
        mix_grad[...] = grad
        both = grad.astype(F32) * rms[2, tt, :, 3 * group :].astype(F32)
        high = both.astype(BF)
        rest = (both - high.astype(F32)).astype(BF)
        heads = lax.broadcasted_iota(jnp.int32, (8, group), 0)
        lanes = lax.broadcasted_iota(jnp.int32, (8, group), 1)
        picks = jnp.where(lax.div(lanes, HEAD_DIM) == heads, 1.0, 0.0).astype(BF)
        dims = (((1,), (1,)), ((), ()))
        delta_v[...] = lax.dot_general(
            picks, high, dims, preferred_element_type=F32
        ) + lax.dot_general(picks, rest, dims, preferred_element_type=F32)

        @pl.when(step >= 2)
        def _():
            for j in range(2):
                landed(dkv_in.at[0, 0], dkv_s.at[step - 2, j])

    def pair_back(step, pair):
        tt, slot = rat(step), lax.rem(step, 2)
        wide = pl.ds(pl.multiple_of(pair * 2 * HEAD_DIM, 2 * HEAD_DIM), 2 * HEAD_DIM)
        q_pair, o_pair = q_v[tt, :, wide], mix_grad[:, wide]
        q_ones = [jnp.where(low_lanes, q_pair, 0).astype(BF), jnp.where(low_lanes, 0, q_pair).astype(BF)]
        o_ones = [jnp.where(low_lanes, o_pair, 0).astype(BF), jnp.where(low_lanes, 0, o_pair).astype(BF)]
        kt_v[...] = jnp.transpose(k_v[tt, :, wide])
        dqt_v[...] = jnp.zeros_like(dqt_v)
        dims = (((1,), (1,)), ((), ()))

        def block(b, carry):
            spot = pl.ds(pl.multiple_of(b * key_rows, key_rows), key_rows)
            k_part, v_part = k_v[tt, spot, wide], v_v[tt, spot, wide]
            number = b * key_rows + lax.broadcasted_iota(jnp.int32, (key_rows, 1), 0)
            live = number < length
            dv, dk = None, None
            for head in range(2):
                which = tt * (group // HEAD_DIM) + pair * 2 + head
                scores = lax.dot_general(k_part, q_ones[head], dims, preferred_element_type=F32)
                probs = jnp.where(live, jnp.exp(scores - lse_rows[pl.ds(which, 1)]), 0.0)
                prob_grad = lax.dot_general(v_part, o_ones[head], dims, preferred_element_type=F32)
                score_grad = (probs * (prob_grad - delta_v[pl.ds(pair * 2 + head, 1)])).astype(BF)
                one_v = jnp.dot(probs.astype(BF), o_ones[head], preferred_element_type=F32)
                one_k = jnp.dot(score_grad, q_ones[head], preferred_element_type=F32)
                dv = one_v if dv is None else dv + one_v
                dk = one_k if dk is None else dk + one_k
                rows_here = slice(head * HEAD_DIM, (head + 1) * HEAD_DIM)
                dqt_v[rows_here] += jnp.dot(
                    kt_v[rows_here, spot], score_grad, preferred_element_type=F32
                )
            dkv_v[slot, 0, spot, wide] = dk.astype(BF)
            dkv_v[slot, 1, spot, wide] = dv.astype(BF)
            return carry

        lax.fori_loop(0, 2 * tokens // key_rows, block, 0)
        dq = jnp.transpose(dqt_v[...].astype(BF).astype(F32)) * 0.125
        rms[2, tt, :, wide] = dq.astype(BF)
        total = jnp.sum(dq, axis=0, keepdims=True)
        small_v[0, pl.ds(tt * (group // 128) + pair, 1)] = total

    def exchange(step):
        slot = lax.rem(step, 2)
        for j in range(2):
            remote(
                dkv_v.at[slot, j, others],
                dkv_in.at[step, j],
                dkv_s.at[step, j],
                dkv_r.at[step, j],
                sibling,
            ).start()

    def collect(step):
        tt, slot = rat(step), lax.rem(step, 2)
        for j in range(2):
            landed(dkv_in.at[0, 0], dkv_r.at[step, j])
            value = (
                dkv_v[slot, j, mine].astype(F32) + dkv_in[step, j].astype(F32)
            ).astype(BF)
            rms[2, tt, :, (1 + j) * group : (2 + j) * group] = value
            if j:
                total = jnp.sum(value.astype(F32), axis=0, keepdims=True)
                for r in range(group // 128):
                    small_v[1, pl.ds(tt * (group // 128) + r, 1)] = total[:, r * 128 : (r + 1) * 128]

        def one(n, carry):
            wide = pl.ds(pl.multiple_of(n * 256, 256), 256)
            acc[:, wide] += lax.dot_general(
                rms[2, tt, :, : 3 * group],
                wbuf[slot, wide, : 3 * group],
                (((1,), (1,)), ((), ())),
                preferred_element_type=F32,
            )
            return carry

        lax.fori_loop(0, width // 256, one, 0)

    def attention(step, carry):
        @pl.when(step < n_tensor)
        def _():
            prepare(step)
            for pair in range(group // (2 * HEAD_DIM)):
                pair_back(step, pair)

                @pl.when(step < 2)
                def _(pair=pair):
                    advance(3 + 2 * step + pair)

            @pl.when(step == 2)
            def _():
                advance(7)

            exchange(step)

        @pl.when(step >= 1)
        def _():
            collect(step - 1)

            @pl.when(step < n_tensor - 1)
            def _():
                weights(0, step + 1, lax.rem(step + 1, 2)).start()

        return carry

    lax.fori_loop(0, n_tensor + 1, attention, 0)

    cot_v[...] = acc[...].astype(BF)
    send_output(1, cot_v)
    for j in range(SMALL):
        send_or_keep(
            me == j,
            small_v.at[j],
            small_in.at[me],
            b_s.at[j],
            b_r.at[me],
            (j // n_tensor, j % n_tensor),
        )
    def drain(index, carry):
        advance(index)
        return carry

    lax.fori_loop(2 * n_tensor, pieces + 1, drain, 0)

    @pl.when(me < SMALL)
    def _():
        def arrive(step, total):
            landed(small_in.at[0], b_r.at[step])
            return total + small_in[step]

        total = lax.fori_loop(0, count, arrive, jnp.zeros(small_in.shape[1:], F32))
        small_in[0] = total
        pltpu.make_async_copy(small_in.at[0], small_out.at[me], bo_r.at[me]).start()

        def spread(step, carry):
            other = lax.rem(me + step, count)
            remote(
                small_in.at[0],
                small_out.at[me],
                bo_s.at[step],
                bo_r.at[me],
                (lax.div(other, n_tensor), lax.rem(other, n_tensor)),
            ).start()
            return carry

        lax.fori_loop(1, count, spread, 0)

    for index in range(pieces + 1, pieces + 1 + bits):
        advance(jnp.int32(index))

    for k in range(KINDS):
        total = from_z[k, n_tensor - 1].astype(F32)
        for step in range(n_tensor - 1):
            landed(from_z.at[0, 0], z_r.at[(KINDS - 1 - k) * n_tensor + step])
            total = total + from_z[k, step].astype(F32)
        sum_ref[k] = total

    for k in range(KINDS):
        for tt in range(n_tensor):
            relayed(k, tt)
            for half in range(2):
                half_rows = full_ref.at[k, tt, pl.ds(0, width // 2), pl.ds(0, half_cols)]
                landed(half_rows, sib_s.at[k, tt, half])
                if chips > 1:
                    most = full_ref.at[k, tt, pl.ds(0, width // 2 - rows), pl.ds(0, half_cols)]
                    landed(most, gxy_s.at[k, tt, half])
    for s in range(2):
        sent((lax.div(t, half_t) == core) & (2 * core + s == t), x_ref.at[s], x_s.at[s])
    for step in range(1, n_tensor):
        landed(bias_ref, bz_s.at[step])
    for tt in range(n_tensor):
        for j in range(2):
            landed(q_v.at[tt], kv_s.at[tt, j])
    for step in range(1, n_dp):
        landed(c_one.at[0], c1_s.at[step])
    for step in range(2 * n_dp):
        seq = lax.rem(4 * chip + step, 2 * n_dp)
        goal = 2 * lax.div(seq, 4) + lax.div(t, half_t)
        sent((goal == d) & (lax.rem(seq, 4) == t), c_two.at[0], c2_s.at[step])
    for j in range(SMALL):
        landed(small_v.at[0], bo_r.at[j])
        sent(me == j, small_v.at[0], b_s.at[j])

    @pl.when(me < SMALL)
    def _():
        def gone(step, carry):
            landed(small_v.at[0], bo_s.at[step])
            return carry

        lax.fori_loop(1, count, gone, 0)

    for a in range(2):
        for q in range(2):
            sent((lax.div(t, half_t) == core) & (2 * core + q == t), x_ref.at[q], y_s.at[a, q])
            landed(x_ref.at[q], y_r.at[a, q])
    for step in range(n_tensor - 2, n_tensor):
        for j in range(2):
            landed(dkv_in.at[0, 0], dkv_s.at[step, j])
    for index in range(pieces - 2, pieces):
        landed(outbox.at[0], core_s.at[index])
    for index in range(pieces - SLOTS, pieces):
        for half in range(2):
            landed(from_chip.at[0, 0], xy_s.at[index, half])
        if index % n_tensor < n_tensor - 1:
            landed(from_z.at[0, 0], z_s.at[index])


def gauss(u):
    size = jnp.abs(u)
    bell = 0.3989422804014327 * jnp.exp(-0.5 * (u * u))
    s = 1.0 / (1.0 + 0.23164190 * size)
    tail = bell * s * (
        0.319381530 + s * (-0.356563782 + s * (1.781477937 + s * (-1.821255978 + s * 1.330274429)))
    )
    return bell, jnp.where(u < 0, tail, 1.0 - tail)


def run_layer(n_dp, n_tensor, undealing, lengths, vecs, x_in, cot_in, shard, biases):
    slots, span, width = x_in.shape
    rows, cols = shard.shape[1:]
    chips = n_dp // 2
    tokens = 2 * span
    group = cols // 4
    n_pos = min(n_dp, span // 16)
    prow, pcol = span // n_pos, width // (n_dp // n_pos)
    pieces = KINDS * n_tensor
    count = n_dp * n_tensor
    dma = pltpu.SemaphoreType.DMA
    any_space = pl.BlockSpec(memory_space=pl.ANY)
    smem = pl.BlockSpec(memory_space=pltpu.SMEM)
    vmem = pl.BlockSpec(memory_space=pltpu.VMEM)
    shapes = (
        ((KINDS, n_tensor, width, cols), BF),
        ((KINDS, rows, cols), F32),
        ((SMALL, 8, 128), F32),
        ((2, 2, span, width), BF),
    )
    return pl.pallas_call(
        functools.partial(layer_kernel, n_dp, n_tensor),
        out_shape=tuple(jax.ShapeDtypeStruct(*shape) for shape in shapes),
        in_specs=[smem, smem, vmem, any_space, any_space, any_space, any_space],
        out_specs=(any_space, vmem, any_space, any_space),
        scratch_shapes=[
            pltpu.VMEM((n_dp, slots, prow, pcol), BF),
            pltpu.VMEM((2 * n_dp, prow, pcol), BF),
            pltpu.VMEM((n_tensor,) + biases.shape, F32),
            pltpu.VMEM((2, width, cols), BF),
            pltpu.VMEM((n_tensor, tokens, group), BF),
            pltpu.VMEM((n_tensor, 2 * tokens, group), BF),
            pltpu.VMEM((n_tensor, 2 * tokens, group), BF),
            pltpu.VMEM((4, 2, width // 2, tokens), BF),
            pltpu.VMEM((KINDS, n_tensor, tokens, cols), BF),
            pltpu.VMEM((tokens, width), BF),
            pltpu.VMEM((tokens, width), BF),
            pltpu.VMEM((tokens, width), BF),
            pltpu.VMEM((tokens, width), BF),
            pltpu.VMEM((tokens, width), F32),
            pltpu.VMEM((tokens, 128), F32),
            pltpu.VMEM((128, tokens), F32),
            pltpu.VMEM((2, tokens, 128), F32),
            pltpu.VMEM((tokens, group), BF),
            pltpu.VMEM((8, tokens), F32),
            pltpu.VMEM((2 * HEAD_DIM, tokens), F32),
            pltpu.VMEM((2 * HEAD_DIM, 2 * tokens), BF),
            pltpu.VMEM((2, 2, 2 * tokens, group), BF),
            pltpu.VMEM((n_tensor, 2, tokens, group), BF),
            pltpu.VMEM((2, width // 2, cols), BF),
            pltpu.VMEM((SLOTS, width // 2, cols), BF),
            pltpu.VMEM((SLOTS, width // 2, cols), BF),
            pltpu.VMEM((SLOTS, 2, max(chips - 1, 1), rows, cols // 2), BF),
            pltpu.VMEM((KINDS, n_tensor, rows, cols), BF),
            pltpu.VMEM((SMALL, 8, 128), F32),
            pltpu.VMEM((count, 8, 128), F32),
            dma((2,)),
            dma((2,)),
            dma((n_dp,)),
            dma((n_dp,)),
            dma((2 * n_dp,)),
            dma((n_tensor // 2, n_dp)),
            dma((KINDS,)),
            dma((KINDS, n_tensor, 2)),
            dma((KINDS, n_tensor)),
            dma((KINDS, n_tensor, 2)),
            dma((KINDS, n_tensor, 2, chips)),
            dma((KINDS, n_tensor, 2)),
            dma((KINDS, n_tensor, 2, chips)),
            dma((n_tensor, 2)),
            dma((n_tensor, 2)),
            dma((n_tensor,)),
            dma((n_tensor,)),
            dma((2,)),
            dma((n_tensor, 2)),
            dma((n_tensor, 2)),
            dma((2, 2)),
            dma((2, 2)),
            dma((SMALL,)),
            dma((count,)),
            dma((count,)),
            dma((SMALL,)),
            dma((pieces,)),
            dma((pieces,)),
            dma((pieces, 2)),
            dma((pieces, 2, chips)),
            dma((pieces,)),
            dma((pieces,)),
        ],
        compiler_params=pltpu.CompilerParams(
            collective_id=0, has_side_effects=True, vmem_limit_bytes=VMEM_LIMIT
        ),
        name="encoder_layer",
    )(undealing, lengths, vecs, x_in, cot_in, shard, biases)


def shards(
    n_dp,
    n_tensor,
    inputs,
    cotangent,
    lengths,
    dealing,
    undealing,
    query_weight,
    key_weight,
    value_weight,
    output_weight,
    up_weight,
    down_weight,
    query_bias,
    value_bias,
    output_bias,
    up_bias,
    down_bias,
    first_gain,
    first_shift,
    second_gain,
    second_shift,
):
    span, slots, width = inputs.shape
    group = query_weight.shape[1]
    shard = jnp.stack(
        [
            jnp.concatenate([query_weight, key_weight, value_weight, output_weight.T], axis=1),
            up_weight,
            down_weight.T,
        ]
    ).astype(BF)
    blank = jnp.zeros((group,), F32)
    biases = jnp.concatenate([query_bias, value_bias, up_bias, blank, blank]).reshape(8, group)
    vecs = jnp.stack([output_bias, down_bias, first_gain, first_shift, second_gain, second_shift])
    vecs = jnp.pad(vecs, ((0, 2), (0, 0)))
    _, sums, small, returned = run_layer(
        n_dp,
        n_tensor,
        undealing,
        lengths,
        vecs,
        jnp.transpose(inputs, (1, 0, 2)),
        jnp.transpose(cotangent, (1, 0, 2)),
        shard,
        biases,
    )
    returned = jnp.transpose(returned, (0, 2, 1, 3))
    small = small.reshape(SMALL, width)
    t = lax.axis_index("tensor")

    def mine(row):
        return lax.dynamic_slice(small[row], (t * group,), (group,))

    return (
        returned[0],
        returned[1],
        sums[0][:, :group],
        sums[0][:, group : 2 * group],
        sums[0][:, 2 * group : 3 * group],
        sums[0][:, 3 * group :].T,
        sums[1],
        sums[2].T,
        mine(0),
        mine(1),
        small[2],
        lax.dynamic_index_in_dim(small, 3 + t, 0, keepdims=False),
        small[7],
        small[8],
        small[9],
        small[10],
        small[11],
    )


def solution(mesh):
    tokens = P("tensor", "dp", None)
    rows, columns = P("dp", "tensor"), P("tensor", "dp")
    split, copied = P("tensor"), P()
    return jax.shard_map(
        functools.partial(shards, mesh.shape["dp"], mesh.shape["tensor"]),
        mesh=mesh,
        in_specs=(
            (tokens, tokens, copied, copied, copied)
            + (rows, rows, rows, columns, rows, columns)
            + (split, split, copied, split, copied, copied, copied, copied, copied)
        ),
        out_specs=(
            (tokens, tokens, rows, rows, rows, columns, rows, columns)
            + (split, split, copied, split, copied, copied, copied, copied, copied)
        ),
        check_vma=False,
    )
```

```python
import functools

import jax
import jax.numpy as jnp
from jax import lax
from jax.experimental import pallas as pl
from jax.experimental.pallas import tpu as pltpu
from jax.sharding import PartitionSpec as P

HEAD_DIM = 64
KINDS = 3
MESH = pl.DeviceIdType.MESH
VMEM_LIMIT = 63 << 20
BF = jnp.bfloat16
F32 = jnp.float32


def flip(index, bit):
    unit = 1 << bit
    return index + unit * (1 - 2 * lax.rem(lax.div(index, unit), 2))


def orders(bits):
    return (tuple(range(bits)), tuple(reversed(range(bits))))


def relative(chip, order, code):
    for place, bit in enumerate(order):
        if code >> place & 1:
            chip = flip(chip, bit)
    return chip


def place():
    d, t = lax.axis_index("dp"), lax.axis_index("tensor")
    return d, t, lax.div(d, 2), lax.rem(d, 2)


def greet(n_dp, n_tensor):
    d, t, _, _ = place()
    barrier = pltpu.get_barrier_semaphore()
    me = d * n_tensor + t
    count = n_dp * n_tensor

    def one(step, carry):
        other = lax.rem(me + step, count)
        pl.semaphore_signal(
            barrier,
            inc=1,
            device_id=(lax.div(other, n_tensor), lax.rem(other, n_tensor)),
            device_id_type=MESH,
        )
        return carry

    lax.fori_loop(1, count, one, 0)
    pl.semaphore_wait(barrier, count - 1)


def remote(src, dst, ssem, rsem, device):
    return pltpu.make_async_remote_copy(
        src_ref=src,
        dst_ref=dst,
        send_sem=ssem,
        recv_sem=rsem,
        device_id=device,
        device_id_type=MESH,
    )


def landed(ref, sem):
    pltpu.make_async_copy(ref, ref, sem).wait()


def send_or_keep(mine, src, dst, ssem, rsem, device):
    @pl.when(mine)
    def _():
        pltpu.make_async_copy(src, dst, rsem).start()

    @pl.when(jnp.logical_not(mine))
    def _():
        remote(src, dst, ssem, rsem, device).start()


def sent(mine, src, ssem):
    @pl.when(jnp.logical_not(mine))
    def _():
        landed(src, ssem)


LAG = 2
SMALL = 12
SLOTS = 4
DEEP = 0
PLAN = (((3, 3), (4, 4), (5, 6), (7, 8)), ((3, 4), (4, 5), (6, 7), (8, 9)))
LAST = 9
COT_ONE, COT_TWO, X_START = 4, 9, 1


def layer_kernel(
    n_dp,
    n_tensor,
    undealing,
    lengths,
    vec_ref,
    x_ref,
    cot_ref,
    shard_ref,
    bias_ref,
    full_ref,
    sum_ref,
    small_out,
    y_out,
    c_one,
    c_two,
    bias_v,
    wbuf,
    q_v,
    k_v,
    v_v,
    lts,
    rms,
    n1_v,
    n2_v,
    cot_v,
    y_v,
    acc,
    lse_v,
    lse_rows,
    rstd_v,
    mix_grad,
    delta_v,
    dqt_v,
    kt_v,
    dkv_v,
    dkv_in,
    outbox,
    from_core,
    held,
    from_chip,
    from_z,
    small_v,
    small_in,
    x_s,
    x_r,
    c1_s,
    c1_r,
    c2_s,
    c2_r,
    own_sem,
    gz_s,
    gz_r,
    gxy_s,
    gxy_r,
    sib_s,
    sib_r,
    kv_s,
    kv_r,
    bz_s,
    bz_r,
    w_sem,
    dkv_s,
    dkv_r,
    y_s,
    y_r,
    b_s,
    b_r,
    bo_s,
    bo_r,
    core_s,
    core_r,
    xy_s,
    xy_r,
    z_s,
    z_r,
    out_sem,
):
    d, t, chip, core = place()
    chips = n_dp // 2
    bits = chips.bit_length() - 1
    half_t = n_tensor // 2
    count = n_dp * n_tensor
    me = d * n_tensor + t
    rows, cols = shard_ref.shape[1:]
    half_cols = cols // 2
    group = q_v.shape[2]
    span, width = x_ref.shape[1:]
    half_width = width // 2
    tokens = 2 * span
    units = cols
    prow, pcol = c_one.shape[2:]
    n_col = width // pcol
    pieces = KINDS * n_tensor
    sibling = (d + 1 - 2 * core, t)
    length = lengths[4 * chip + t]
    mine = pl.ds(pl.multiple_of(core * tokens, tokens), tokens)
    others = pl.ds(pl.multiple_of((1 - core) * tokens, tokens), tokens)
    greet(n_dp, n_tensor)

    def block(k, tt, who, half):
        return full_ref.at[
            k,
            tt,
            pl.ds(pl.multiple_of((2 * who + core) * rows, rows), rows),
            pl.ds(half * half_cols, half_cols),
        ]

    def arriving(index):
        rest, others = index - KINDS, n_tensor - 1
        return jnp.where(
            index < KINDS,
            index * n_tensor,
            lax.div(rest, others) * n_tensor + 1 + lax.rem(rest, others),
        )

    def stripe(k, tt):
        return full_ref.at[k, tt, pl.ds(pl.multiple_of(d * rows, rows), rows)]

    def at(index):
        step = lax.rem(index, n_tensor)
        near = jnp.where(t < half_t, t, n_tensor - 1 - t)
        spot = jnp.where(step <= near, near - step, step)
        return lax.div(index, n_tensor), jnp.where(t < half_t, spot, n_tensor - 1 - spot)

    for k in range(KINDS):
        pltpu.make_async_copy(shard_ref.at[k], stripe(k, t), own_sem.at[k]).start()

    def relay(index):
        k, tt = at(index)

        @pl.when(tt != t)
        def _():
            landed(shard_ref.at[0], gz_r.at[k, tt])

        for way, wanted in ((1, (tt <= t) & (t < n_tensor - 1)), (0, (tt >= t) & (t > 0))):

            @pl.when(wanted)
            def _(way=way):
                remote(
                    stripe(k, tt),
                    stripe(k, tt),
                    gz_s.at[k, tt, way],
                    gz_r.at[k, tt],
                    (d, t + 2 * way - 1),
                ).start()

    def relayed(k, tt):
        for way, wanted in ((1, (tt <= t) & (t < n_tensor - 1)), (0, (tt >= t) & (t > 0))):

            @pl.when(wanted)
            def _(way=way):
                landed(shard_ref.at[0], gz_s.at[k, tt, way])

    def start_tokens():
        for s in range(2):
            send_or_keep(
                (lax.div(t, half_t) == core) & (2 * core + s == t),
                x_ref.at[s],
                outbox.at[0, pl.ds(pl.multiple_of(lax.rem(t, half_t) * span, span), span)],
                x_s.at[s],
                x_r.at[lax.rem(t, half_t)],
                (2 * chip + lax.div(t, half_t), 2 * core + s),
            )

    def start_biases():
        pltpu.make_async_copy(bias_ref, bias_v.at[t], bz_r.at[0]).start()
        for step in range(1, n_tensor):
            remote(
                bias_ref,
                bias_v.at[t],
                bz_s.at[step],
                bz_r.at[step],
                (d, lax.rem(t + step, n_tensor)),
            ).start()

    def piece(who):
        return cot_ref.at[
            :,
            pl.ds(pl.multiple_of(lax.div(who, n_col) * prow, prow), prow),
            pl.ds(pl.multiple_of(lax.rem(who, n_col) * pcol, pcol), pcol),
        ]

    def cot_first():
        pltpu.make_async_copy(piece(d), c_one.at[d], c1_r.at[0]).start()
        for step in range(1, n_dp):
            who = lax.rem(d + step, n_dp)
            remote(piece(who), c_one.at[d], c1_s.at[step], c1_r.at[step], (who, t)).start()

    def cot_second():
        for step in range(n_dp):
            landed(c_one.at[0], c1_r.at[step])
        count = 2 * n_dp
        for step in range(count):
            seq = lax.rem(4 * chip + step, count)
            slot = undealing[seq]
            c_two[seq] = c_one[lax.div(slot, 2), lax.rem(slot, 2)]
            goal = 2 * lax.div(seq, 4) + lax.div(t, half_t)
            send_or_keep(
                (goal == d) & (lax.rem(seq, 4) == t),
                c_two.at[seq],
                cot_v.at[
                    pl.ds(
                        pl.multiple_of(lax.rem(t, half_t) * span + lax.div(d, n_col) * prow, prow),
                        prow,
                    ),
                    pl.ds(pl.multiple_of(lax.rem(d, n_col) * pcol, pcol), pcol),
                ],
                c2_s.at[step],
                c2_r.at[lax.rem(t, half_t), d],
                (goal, lax.rem(seq, 4)),
            )

    def forward(k, tt, half, code):
        order = orders(bits)[half]
        ref = block(k, tt, relative(chip, order, code), half)
        for s in range(code.bit_length(), bits):
            target = code | 1 << s
            remote(
                ref,
                ref,
                gxy_s.at[k, tt, half],
                gxy_r.at[k, tt, half, target],
                (2 * flip(chip, order[s]) + core, t),
            ).start()
        remote(
            ref, ref, sib_s.at[k, tt, half], sib_r.at[k, tt, half, code], sibling
        ).start()

    def receive(index, codes):
        k, tt = at(arriving(index))
        for code in codes:
            for half in range(2):
                landed(block(k, tt, chip, half), gxy_r.at[k, tt, half, code])
                forward(k, tt, half, code)

    early, late = range(1, max(chips // 2, 1)), range(max(chips // 2, 1), chips)

    def comm_step(index):
        @pl.when((index + 2 >= KINDS) & (index + 2 < pieces))
        def _():
            k, tt = at(arriving(index + 2))
            for half in range(2):
                forward(k, tt, half, 0)

        @pl.when(index < pieces)
        def _():
            receive(index, early)

        @pl.when(index >= LAG)
        def _():
            receive(index - LAG, late)

        follow = index + KINDS
        others = n_tensor - 1

        @pl.when(follow < pieces)
        def _():
            relay(arriving(follow))

            @pl.when((lax.rem(index, others) == others - 1) & (follow + 1 < pieces))
            def _():
                relay(lax.div(index, others) * n_tensor + n_tensor)

    def load(index):
        k, tt = at(index)
        slot = lax.rem(index, 2)
        for half in range(2):
            for code in range(chips):
                landed(block(k, tt, chip, half), sib_r.at[k, tt, half, code])
        copy = pltpu.make_async_copy(full_ref.at[k, tt], wbuf.at[slot], w_sem.at[slot])
        copy.start()
        copy.wait()

    def project(index):
        _, tt = at(index)
        slot = lax.rem(index, 2)
        x = outbox[0]
        for c in range(3):
            out = jnp.dot(
                x, wbuf[slot, :, c * group : (c + 1) * group], preferred_element_type=F32
            )
            if c == 0:
                q_v[tt] = ((out + bias_v[tt, 0:1]) * 0.125).astype(BF)
            elif c == 1:
                k_v[tt, mine] = out.astype(BF)
            else:
                v_v[tt, mine] = (out + bias_v[tt, 1:2]).astype(BF)
        for j, ref in enumerate((k_v, v_v)):
            remote(
                ref.at[tt, mine], ref.at[tt, mine], kv_s.at[tt, j], kv_r.at[tt, j], sibling
            ).start()

    def attend(index):
        _, tt = at(index)
        slot = lax.rem(index, 2)
        for j, ref in enumerate((k_v, v_v)):
            landed(ref.at[tt, mine], kv_r.at[tt, j])
        block_rows = min(256, tokens)
        low = lax.broadcasted_iota(jnp.int32, (block_rows, 2 * HEAD_DIM), 1) < HEAD_DIM
        lanes = lax.broadcasted_iota(jnp.int32, (block_rows, lse_v.shape[1]), 1)
        live = lax.broadcasted_iota(jnp.int32, (1, 2 * tokens), 1) < length

        def pair_step(step, carry):
            pair, part = lax.div(step, tokens // block_rows), lax.rem(step, tokens // block_rows)
            wide = pl.ds(pl.multiple_of(pair * 2 * HEAD_DIM, 2 * HEAD_DIM), 2 * HEAD_DIM)
            spot = pl.ds(pl.multiple_of(part * block_rows, block_rows), block_rows)
            k_pair, v_pair = k_v[tt, :, wide], v_v[tt, :, wide]
            q_pair = q_v[tt, spot, wide]
            outs = []
            for head in range(2):
                q_one = jnp.where(low if head == 0 else jnp.logical_not(low), q_pair, 0).astype(BF)
                scores = lax.dot_general(
                    q_one, k_pair, (((1,), (1,)), ((), ())), preferred_element_type=F32
                )
                scores = jnp.where(live, scores, -1000000000.0)
                summit = jnp.max(scores, axis=-1, keepdims=True)
                raised = jnp.exp(scores - summit)
                total = jnp.sum(raised, axis=-1, keepdims=True)
                out = jnp.dot(raised.astype(BF), v_pair, preferred_element_type=F32)
                outs.append(out / total)
                number = tt * (group // HEAD_DIM) + pair * 2 + head
                lse_v[spot] = jnp.where(lanes == number, summit + jnp.log(total), lse_v[spot])
            rms[2, tt, spot, pl.ds(pl.multiple_of(3 * group + pair * 2 * HEAD_DIM, 2 * HEAD_DIM), 2 * HEAD_DIM)] = jnp.where(low, outs[0], outs[1]).astype(BF)
            return carry

        lax.fori_loop(0, (group // (2 * HEAD_DIM)) * (tokens // block_rows), pair_step, 0)
        for n in range(width // 256):
            acc[:, n * 256 : (n + 1) * 256] += lax.dot_general(
                rms[2, tt, :, 3 * group :],
                wbuf[slot, n * 256 : (n + 1) * 256, 3 * group :],
                (((1,), (1,)), ((), ())),
                preferred_element_type=F32,
            )

    chunk = 64

    def norm(which, keep):
        gain, shift = vec_ref[2 + 2 * which : 3 + 2 * which], vec_ref[3 + 2 * which : 4 + 2 * which]

        def one(step, carry):
            spot = pl.ds(pl.multiple_of(step * chunk, chunk), chunk)
            value = acc[spot]
            center = value - jnp.mean(value, axis=-1, keepdims=True)
            spread = jnp.mean(center * center, axis=-1, keepdims=True)
            inverse = lax.rsqrt(spread + 1e-05)
            unit = center * inverse
            rstd_v[which, spot] = jnp.broadcast_to(inverse, (chunk, rstd_v.shape[2]))
            keep(spot, unit, unit * gain + shift)
            return carry

        lax.fori_loop(0, tokens // chunk, one, 0)

    def keep_one(spot, unit, hidden):
        n1_v[spot] = unit.astype(BF)
        outbox[1, spot] = hidden.astype(BF)
        acc[spot] = hidden + vec_ref[1:2]

    def keep_two(spot, unit, hidden):
        n2_v[spot] = unit.astype(BF)
        y_v[spot] = hidden.astype(BF)

    def turn_rows(source, which):
        flat = jnp.transpose(source)
        for dev in range(n_dp):
            lts[which, dev % 2, (dev // 2) * rows : (dev // 2 + 1) * rows] = flat[
                dev * rows : (dev + 1) * rows
            ]

    def expand(index):
        _, tt = at(index)
        slot = lax.rem(index, 2)

        def one(n, carry):
            wide = pl.ds(pl.multiple_of(n * 256, 256), 256)
            u = jnp.dot(outbox[1], wbuf[slot, :, wide], preferred_element_type=F32)
            u = u + bias_v[tt, pl.ds(2 + n, 1)]
            bell, below = gauss(u)
            rms[0, tt, :, wide] = (u * below).astype(BF)
            rms[1, tt, :, wide] = (below + u * bell).astype(BF)
            return carry

        lax.fori_loop(0, units // 256, one, 0)

    def contract(index):
        _, tt = at(index)
        slot = lax.rem(index, 2)

        def one(n, carry):
            wide = pl.ds(pl.multiple_of(n * 256, 256), 256)
            acc[:, wide] += lax.dot_general(
                rms[0, tt], wbuf[slot, wide, :], (((1,), (1,)), ((), ())), preferred_element_type=F32
            )
            return carry

        lax.fori_loop(0, width // 256, one, 0, unroll=True)

    landed(shard_ref.at[0], own_sem.at[0])
    relay(jnp.int32(0))
    start_biases()
    for k in range(KINDS):
        if k:
            landed(shard_ref.at[0], own_sem.at[k])
        for half in range(2):
            forward(k, t, half, 0)
    def tokens_here():
        for s in range(2):
            landed(x_ref.at[s], x_r.at[s])
        for step in range(n_tensor):
            landed(bias_ref, bz_r.at[step])
        acc[...] = outbox[0].astype(F32) + vec_ref[0:1]
        turn_rows(outbox[0], 2)
        lse_v[...] = jnp.zeros_like(lse_v)

    def turn(index, carry):
        comm_step(index)
        done = index - LAG

        @pl.when(index == X_START)
        def _():
            start_tokens()

        @pl.when(done == 2)
        def _():
            tokens_here()

        @pl.when((done >= 3) & (done <= 6))
        def _():
            attend(done - 3)

        @pl.when((done >= 2) & (done <= 5))
        def _():
            load(done - 2)
            project(done - 2)

        @pl.when(index == COT_ONE)
        def _():
            cot_first()

        @pl.when(index == COT_TWO)
        def _():
            cot_second()

        @pl.when(done == 6)
        def _():
            norm(0, keep_one)
            turn_rows(outbox[1], 1)
            lse_rows[...] = jnp.transpose(lse_v[...])

        def up(step, carry):
            load(step)
            expand(step)
            return carry

        def down(step, carry):
            load(step)
            contract(step)
            return carry

        lax.fori_loop(
            jnp.where(done == 8, 6, 4), jnp.where(done == 7, 6, jnp.where(done == 8, 8, 4)), up, 0
        )
        lax.fori_loop(
            jnp.where(done == 9, 8, jnp.where(done > 9, done, 8)),
            jnp.where(done == 9, 10, jnp.where(done > 9, done + 1, 8)),
            down,
            0,
        )
        return carry

    lax.fori_loop(0, pieces + LAG, turn, 0)
    norm(1, keep_two)

    def rat(step):
        return lax.rem(t + 1 + step, n_tensor)

    def weights(k, step, slot):
        return pltpu.make_async_copy(full_ref.at[k, rat(step)], wbuf.at[slot], w_sem.at[slot])

    def send_output(a, source):
        for q in range(2):
            send_or_keep(
                (lax.div(t, half_t) == core) & (2 * core + q == t),
                source.at[pl.ds(q * span, span)],
                y_out.at[a, lax.rem(t, half_t)],
                y_s.at[a, q],
                y_r.at[a, lax.rem(t, half_t)],
                (2 * chip + lax.div(t, half_t), 2 * core + q),
            )


    def kind_of(index):
        return KINDS - 1 - lax.div(index, n_tensor)

    def emit(index):
        order = lax.div(index, n_tensor)
        tt = rat(lax.rem(index, n_tensor))
        slot, box = lax.rem(index, SLOTS), lax.rem(index, 2)

        @pl.when(index >= 2)
        def _():
            landed(outbox.at[0], core_s.at[index - 2])

        @pl.when(index >= SLOTS)
        def _():
            for half in range(2):
                landed(from_chip.at[0, 0], xy_s.at[index - SLOTS, half])

            @pl.when(lax.rem(index - SLOTS, n_tensor) < n_tensor - 1)
            def _():
                landed(from_z.at[0, 0], z_s.at[index - SLOTS])

        def one(n, carry):
            wide = pl.ds(pl.multiple_of(n * group, group), group)
            left = order + jnp.where((order == 2) & (n == 3), 1, 0)
            right = rms[order, tt, :, wide]
            outbox[box, :, wide] = jnp.dot(
                lts[left, 1 - core], right, preferred_element_type=F32
            ).astype(BF)
            held[slot, :, wide] = jnp.dot(
                lts[left, core], right, preferred_element_type=F32
            ).astype(BF)
            return carry

        lax.fori_loop(0, cols // group, one, 0, unroll=True)
        remote(
            outbox.at[box], from_core.at[lax.rem(index, 4)], core_s.at[index], core_r.at[index], sibling
        ).start()

    def spot_of(code, order):
        return pl.ds(pl.multiple_of(relative(chip, order, code) * rows, rows), rows)

    def pass_on(index, s):
        slot = lax.rem(index, SLOTS)
        for half in range(2):
            order = orders(bits)[half]
            for code in range(1 << s, 2 << s):
                remote(
                    held.at[slot, spot_of(code, order), pl.ds(half * half_cols, half_cols)],
                    from_chip.at[slot, half, code - 1],
                    xy_s.at[index, half],
                    xy_r.at[index, half, code],
                    (2 * flip(chip, order[s]) + core, t),
                ).start()

    def take_in(index, s):
        slot = lax.rem(index, SLOTS)
        for half in range(2):
            order = orders(bits)[half]
            for code in range(1 << s, 2 << s):
                landed(from_chip.at[0, 0, 0], xy_r.at[index, half, code])
                spot = spot_of(code - (1 << s), order)
                wide = pl.ds(half * half_cols, half_cols)
                held[slot, spot, wide] = (
                    held[slot, spot, wide].astype(F32)
                    + from_chip[slot, half, code - 1].astype(F32)
                ).astype(BF)

    def first(index):
        slot = lax.rem(index, SLOTS)
        landed(outbox.at[0], core_r.at[index])
        part = min(128, half_width)

        def add(c, carry):
            spot = pl.ds(pl.multiple_of(c * part, part), part)
            held[slot, spot] = (
                held[slot, spot].astype(F32) + from_core[lax.rem(index, 4), spot].astype(F32)
            ).astype(BF)
            return carry

        lax.fori_loop(0, half_width // part, add, 0)
        if bits:
            pass_on(index, bits - 1)

    def finish(index):
        slot, step = lax.rem(index, SLOTS), lax.rem(index, n_tensor)
        source = pl.ds(pl.multiple_of(chip * rows, rows), rows)

        @pl.when(step == n_tensor - 1)
        def _():
            from_z[kind_of(index), step] = held[slot, source]

        @pl.when(step < n_tensor - 1)
        def _():
            remote(
                held.at[slot, source],
                from_z.at[kind_of(index), step],
                z_s.at[index],
                z_r.at[index],
                (d, rat(step)),
            ).start()

    def advance(index):
        @pl.when(index < pieces)
        def _():
            emit(index)

        for stage in range(bits + 1):
            earlier = index - 1 - stage - (DEEP if stage else 0)

            @pl.when((earlier >= 0) & (earlier < pieces))
            def _(stage=stage, earlier=earlier):
                if stage == 0:
                    first(earlier)
                else:
                    take_in(earlier, bits - stage)
                    if stage < bits:
                        pass_on(earlier, bits - stage - 1)
                if stage == bits:
                    finish(earlier)

    def keep_small(which, row):
        for r in range(8):
            small_v[which, r : r + 1] = row[:, r * 128 : (r + 1) * 128]

    def norm_back(which, unit_ref, incoming, low_ref):
        gain = vec_ref[2 + 2 * which : 3 + 2 * which]

        def one(step, carry):
            spot = pl.ds(pl.multiple_of(step * chunk, chunk), chunk)
            e = incoming(step, spot)
            unit = unit_ref[spot].astype(F32)
            ge = e * gain
            first_mean = jnp.mean(ge, axis=-1, keepdims=True)
            second_mean = jnp.mean(ge * unit, axis=-1, keepdims=True)
            grad = (ge - first_mean - unit * second_mean) * rstd_v[which, spot, 0:1]
            acc[spot] = grad
            low = grad.astype(BF)
            low_ref[spot] = low
            return (
                carry[0] + jnp.sum(e * unit, axis=0, keepdims=True),
                carry[1] + jnp.sum(e, axis=0, keepdims=True),
                carry[2] + jnp.sum(low.astype(F32), axis=0, keepdims=True),
            )

        zero = jnp.zeros((1, width), F32)
        return lax.fori_loop(0, tokens // chunk, one, (zero, zero, zero))

    for q in range(half_t):
        for who in range(n_dp):
            landed(c_two.at[0], c2_r.at[q, who])
    weights(2, 0, 0).start()
    weights(1, 0, 1).start()
    send_output(0, y_v)

    def seed(step, spot):
        number = core * tokens + step * chunk + lax.broadcasted_iota(jnp.int32, (chunk, 1), 0)
        return jnp.where(number < length, cot_v[spot].astype(F32), 0.0)

    sums = norm_back(1, n2_v, seed, cot_v)
    keep_small(10, sums[0])
    keep_small(11, sums[1])
    keep_small(7, sums[2])
    turn_rows(cot_v[...], 0)
    advance(jnp.int32(0))

    def mlp(step, carry):
        tt = rat(step)
        weights(2, step, 0).wait()

        def one(n, carry):
            wide = pl.ds(pl.multiple_of(n * 256, 256), 256)
            grad = jnp.dot(cot_v[...], wbuf[0, :, wide], preferred_element_type=F32)
            rms[1, tt, :, wide] = (rms[1, tt, :, wide].astype(F32) * grad).astype(BF)
            return carry

        lax.fori_loop(0, cols // 256, one, 0, unroll=True)

        @pl.when(step < n_tensor - 1)
        def _():
            weights(2, step + 1, 0).start()

        @pl.when(step == n_tensor - 1)
        def _():
            weights(0, 0, 0).start()

        total = jnp.sum(rms[1, tt].astype(F32), axis=0, keepdims=True)
        for r in range(8):
            small_v[3 + tt, r : r + 1] = total[:, r * 128 : (r + 1) * 128]
        weights(1, step, 1).wait()

        def two(n, carry):
            wide = pl.ds(pl.multiple_of(n * 256, 256), 256)
            acc[:, wide] += lax.dot_general(
                rms[1, tt], wbuf[1, wide, :], (((1,), (1,)), ((), ())), preferred_element_type=F32
            )
            return carry

        lax.fori_loop(0, width // 256, two, 0, unroll=True)

        @pl.when(step < n_tensor - 1)
        def _():
            weights(1, step + 1, 1).start()

        @pl.when(step == n_tensor - 1)
        def _():
            weights(0, 1, 1).start()

        @pl.when(lax.rem(step, 2) == 1)
        def _():
            advance(1 + lax.div(step, 2))

        return carry

    lax.fori_loop(0, n_tensor, mlp, 0)

    sums = norm_back(0, n1_v, lambda step, spot: acc[spot], n2_v)
    keep_small(8, sums[0])
    keep_small(9, sums[1])
    keep_small(2, sums[2])
    turn_rows(n2_v[...], 3)

    key_rows = min(256, 2 * tokens)
    low_lanes = lax.broadcasted_iota(jnp.int32, (tokens, 2 * HEAD_DIM), 1) < HEAD_DIM

    def prepare(step):
        tt, slot = rat(step), lax.rem(step, 2)
        weights(0, step, slot).wait()
        grad = jnp.dot(
            n2_v[...], wbuf[slot, :, 3 * group :], preferred_element_type=F32
        ).astype(BF)
        mix_grad[...] = grad
        both = grad.astype(F32) * rms[2, tt, :, 3 * group :].astype(F32)
        high = both.astype(BF)
        rest = (both - high.astype(F32)).astype(BF)
        heads = lax.broadcasted_iota(jnp.int32, (8, group), 0)
        lanes = lax.broadcasted_iota(jnp.int32, (8, group), 1)
        picks = jnp.where(lax.div(lanes, HEAD_DIM) == heads, 1.0, 0.0).astype(BF)
        dims = (((1,), (1,)), ((), ()))
        delta_v[...] = lax.dot_general(
            picks, high, dims, preferred_element_type=F32
        ) + lax.dot_general(picks, rest, dims, preferred_element_type=F32)

        @pl.when(step >= 2)
        def _():
            for j in range(2):
                landed(dkv_in.at[0, 0], dkv_s.at[step - 2, j])

    def pair_back(step, pair):
        tt, slot = rat(step), lax.rem(step, 2)
        wide = pl.ds(pl.multiple_of(pair * 2 * HEAD_DIM, 2 * HEAD_DIM), 2 * HEAD_DIM)
        q_pair, o_pair = q_v[tt, :, wide], mix_grad[:, wide]
        q_ones = [jnp.where(low_lanes, q_pair, 0).astype(BF), jnp.where(low_lanes, 0, q_pair).astype(BF)]
        o_ones = [jnp.where(low_lanes, o_pair, 0).astype(BF), jnp.where(low_lanes, 0, o_pair).astype(BF)]
        kt_v[...] = jnp.transpose(k_v[tt, :, wide])
        dqt_v[...] = jnp.zeros_like(dqt_v)
        dims = (((1,), (1,)), ((), ()))

        def block(b, carry):
            spot = pl.ds(pl.multiple_of(b * key_rows, key_rows), key_rows)
            k_part, v_part = k_v[tt, spot, wide], v_v[tt, spot, wide]
            number = b * key_rows + lax.broadcasted_iota(jnp.int32, (key_rows, 1), 0)
            live = number < length
            dv, dk = None, None
            for head in range(2):
                which = tt * (group // HEAD_DIM) + pair * 2 + head
                scores = lax.dot_general(k_part, q_ones[head], dims, preferred_element_type=F32)
                probs = jnp.where(live, jnp.exp(scores - lse_rows[pl.ds(which, 1)]), 0.0)
                prob_grad = lax.dot_general(v_part, o_ones[head], dims, preferred_element_type=F32)
                score_grad = (probs * (prob_grad - delta_v[pl.ds(pair * 2 + head, 1)])).astype(BF)
                one_v = jnp.dot(probs.astype(BF), o_ones[head], preferred_element_type=F32)
                one_k = jnp.dot(score_grad, q_ones[head], preferred_element_type=F32)
                dv = one_v if dv is None else dv + one_v
                dk = one_k if dk is None else dk + one_k
                rows_here = slice(head * HEAD_DIM, (head + 1) * HEAD_DIM)
                dqt_v[rows_here] += jnp.dot(
                    kt_v[rows_here, spot], score_grad, preferred_element_type=F32
                )
            dkv_v[slot, 0, spot, wide] = dk.astype(BF)
            dkv_v[slot, 1, spot, wide] = dv.astype(BF)
            return carry

        lax.fori_loop(0, 2 * tokens // key_rows, block, 0)
        dq = jnp.transpose(dqt_v[...].astype(BF).astype(F32)) * 0.125
        rms[2, tt, :, wide] = dq.astype(BF)
        total = jnp.sum(dq, axis=0, keepdims=True)
        small_v[0, pl.ds(tt * (group // 128) + pair, 1)] = total

    def exchange(step):
        slot = lax.rem(step, 2)
        for j in range(2):
            remote(
                dkv_v.at[slot, j, others],
                dkv_in.at[step, j],
                dkv_s.at[step, j],
                dkv_r.at[step, j],
                sibling,
            ).start()

    def collect(step):
        tt, slot = rat(step), lax.rem(step, 2)
        for j in range(2):
            landed(dkv_in.at[0, 0], dkv_r.at[step, j])
            value = (
                dkv_v[slot, j, mine].astype(F32) + dkv_in[step, j].astype(F32)
            ).astype(BF)
            rms[2, tt, :, (1 + j) * group : (2 + j) * group] = value
            if j:
                total = jnp.sum(value.astype(F32), axis=0, keepdims=True)
                for r in range(group // 128):
                    small_v[1, pl.ds(tt * (group // 128) + r, 1)] = total[:, r * 128 : (r + 1) * 128]

        def one(n, carry):
            wide = pl.ds(pl.multiple_of(n * 256, 256), 256)
            acc[:, wide] += lax.dot_general(
                rms[2, tt, :, : 3 * group],
                wbuf[slot, wide, : 3 * group],
                (((1,), (1,)), ((), ())),
                preferred_element_type=F32,
            )
            return carry

        lax.fori_loop(0, width // 256, one, 0, unroll=True)

    def run(index, carry):
        advance(index)
        return carry

    def attention(step, carry):
        @pl.when(step < n_tensor)
        def _():
            prepare(step)
            for pair in range(group // (2 * HEAD_DIM)):
                pair_back(step, pair)
                low, high = jnp.int32(0), jnp.int32(0)
                for s, (begin, end) in enumerate(PLAN[pair]):
                    low, high = jnp.where(step == s, begin, low), jnp.where(step == s, end, high)
                lax.fori_loop(low, high, run, 0)

            exchange(step)

        @pl.when(step >= 1)
        def _():
            collect(step - 1)

            @pl.when(step < n_tensor - 1)
            def _():
                weights(0, step + 1, lax.rem(step + 1, 2)).start()

        return carry

    lax.fori_loop(0, n_tensor + 1, attention, 0)

    cot_v[...] = acc[...].astype(BF)
    send_output(1, cot_v)
    for j in range(SMALL):
        send_or_keep(
            me == j,
            small_v.at[j],
            small_in.at[me],
            b_s.at[j],
            b_r.at[me],
            (j // n_tensor, j % n_tensor),
        )
    def drain(index, carry):
        advance(index)
        return carry

    lax.fori_loop(LAST, pieces, drain, 0)

    @pl.when(me < SMALL)
    def _():
        def arrive(step, total):
            landed(small_in.at[0], b_r.at[step])
            return total + small_in[step]

        total = lax.fori_loop(0, count, arrive, jnp.zeros(small_in.shape[1:], F32))
        small_in[0] = total
        pltpu.make_async_copy(small_in.at[0], small_out.at[me], bo_r.at[me]).start()

        def spread(step, carry):
            other = lax.rem(me + step, count)
            remote(
                small_in.at[0],
                small_out.at[me],
                bo_s.at[step],
                bo_r.at[me],
                (lax.div(other, n_tensor), lax.rem(other, n_tensor)),
            ).start()
            return carry

        lax.fori_loop(1, count, spread, 0)

    lax.fori_loop(pieces, pieces + 1 + bits + DEEP, drain, 0)

    for k in range(KINDS):
        total = from_z[k, n_tensor - 1].astype(F32)
        for step in range(n_tensor - 1):
            landed(from_z.at[0, 0], z_r.at[(KINDS - 1 - k) * n_tensor + step])
            total = total + from_z[k, step].astype(F32)
        acc[k * rows : (k + 1) * rows] = total
        pltpu.make_async_copy(acc.at[pl.ds(k * rows, rows)], sum_ref.at[k], out_sem.at[k]).start()
    for k in range(KINDS):
        landed(acc.at[pl.ds(0, rows)], out_sem.at[k])

    for k in range(KINDS):
        for tt in range(n_tensor):
            relayed(k, tt)
            for half in range(2):
                half_rows = full_ref.at[k, tt, pl.ds(0, width // 2), pl.ds(0, half_cols)]
                landed(half_rows, sib_s.at[k, tt, half])
                if chips > 1:
                    most = full_ref.at[k, tt, pl.ds(0, width // 2 - rows), pl.ds(0, half_cols)]
                    landed(most, gxy_s.at[k, tt, half])
    for s in range(2):
        sent((lax.div(t, half_t) == core) & (2 * core + s == t), x_ref.at[s], x_s.at[s])
    for step in range(1, n_tensor):
        landed(bias_ref, bz_s.at[step])
    for tt in range(n_tensor):
        for j in range(2):
            landed(q_v.at[tt], kv_s.at[tt, j])
    for step in range(1, n_dp):
        landed(c_one.at[0], c1_s.at[step])
    for step in range(2 * n_dp):
        seq = lax.rem(4 * chip + step, 2 * n_dp)
        goal = 2 * lax.div(seq, 4) + lax.div(t, half_t)
        sent((goal == d) & (lax.rem(seq, 4) == t), c_two.at[0], c2_s.at[step])
    for j in range(SMALL):
        landed(small_v.at[0], bo_r.at[j])
        sent(me == j, small_v.at[0], b_s.at[j])

    @pl.when(me < SMALL)
    def _():
        def gone(step, carry):
            landed(small_v.at[0], bo_s.at[step])
            return carry

        lax.fori_loop(1, count, gone, 0)

    for a in range(2):
        for q in range(2):
            sent((lax.div(t, half_t) == core) & (2 * core + q == t), x_ref.at[q], y_s.at[a, q])
            landed(x_ref.at[q], y_r.at[a, q])
    for step in range(n_tensor - 2, n_tensor):
        for j in range(2):
            landed(dkv_in.at[0, 0], dkv_s.at[step, j])
    for index in range(pieces - 2, pieces):
        landed(outbox.at[0], core_s.at[index])
    for index in range(pieces - SLOTS, pieces):
        for half in range(2):
            landed(from_chip.at[0, 0], xy_s.at[index, half])
        if index % n_tensor < n_tensor - 1:
            landed(from_z.at[0, 0], z_s.at[index])


def gauss(u):
    size = jnp.abs(u)
    bell = 0.3989422804014327 * jnp.exp(-0.5 * (u * u))
    s = 1.0 / (1.0 + 0.23164190 * size)
    tail = bell * s * (
        0.319381530 + s * (-0.356563782 + s * (1.781477937 + s * (-1.821255978 + s * 1.330274429)))
    )
    return bell, jnp.where(u < 0, tail, 1.0 - tail)


def run_layer(n_dp, n_tensor, undealing, lengths, vecs, x_in, cot_in, shard, biases):
    slots, span, width = x_in.shape
    rows, cols = shard.shape[1:]
    chips = n_dp // 2
    tokens = 2 * span
    group = cols // 4
    n_pos = min(n_dp, span // 16)
    prow, pcol = span // n_pos, width // (n_dp // n_pos)
    pieces = KINDS * n_tensor
    count = n_dp * n_tensor
    dma = pltpu.SemaphoreType.DMA
    any_space = pl.BlockSpec(memory_space=pl.ANY)
    smem = pl.BlockSpec(memory_space=pltpu.SMEM)
    vmem = pl.BlockSpec(memory_space=pltpu.VMEM)
    shapes = (
        ((KINDS, n_tensor, width, cols), BF),
        ((KINDS, rows, cols), F32),
        ((SMALL, 8, 128), F32),
        ((2, 2, span, width), BF),
    )
    return pl.pallas_call(
        functools.partial(layer_kernel, n_dp, n_tensor),
        out_shape=tuple(jax.ShapeDtypeStruct(*shape) for shape in shapes),
        in_specs=[smem, smem, vmem, any_space, any_space, vmem, vmem],
        out_specs=(any_space, any_space, any_space, any_space),
        scratch_shapes=[
            pltpu.VMEM((n_dp, slots, prow, pcol), BF),
            pltpu.VMEM((2 * n_dp, prow, pcol), BF),
            pltpu.VMEM((n_tensor,) + biases.shape, F32),
            pltpu.VMEM((2, width, cols), BF),
            pltpu.VMEM((n_tensor, tokens, group), BF),
            pltpu.VMEM((n_tensor, 2 * tokens, group), BF),
            pltpu.VMEM((n_tensor, 2 * tokens, group), BF),
            pltpu.VMEM((4, 2, width // 2, tokens), BF),
            pltpu.VMEM((KINDS, n_tensor, tokens, cols), BF),
            pltpu.VMEM((tokens, width), BF),
            pltpu.VMEM((tokens, width), BF),
            pltpu.VMEM((tokens, width), BF),
            pltpu.VMEM((tokens, width), BF),
            pltpu.VMEM((tokens, width), F32),
            pltpu.VMEM((tokens, 128), F32),
            pltpu.VMEM((128, tokens), F32),
            pltpu.VMEM((2, tokens, 128), F32),
            pltpu.VMEM((tokens, group), BF),
            pltpu.VMEM((8, tokens), F32),
            pltpu.VMEM((2 * HEAD_DIM, tokens), F32),
            pltpu.VMEM((2 * HEAD_DIM, 2 * tokens), BF),
            pltpu.VMEM((2, 2, 2 * tokens, group), BF),
            pltpu.VMEM((n_tensor, 2, tokens, group), BF),
            pltpu.VMEM((2, width // 2, cols), BF),
            pltpu.VMEM((4, width // 2, cols), BF),
            pltpu.VMEM((SLOTS, width // 2, cols), BF),
            pltpu.VMEM((SLOTS, 2, max(chips - 1, 1), rows, cols // 2), BF),
            pltpu.VMEM((KINDS, n_tensor, rows, cols), BF),
            pltpu.VMEM((SMALL, 8, 128), F32),
            pltpu.VMEM((count, 8, 128), F32),
            dma((2,)),
            dma((2,)),
            dma((n_dp,)),
            dma((n_dp,)),
            dma((2 * n_dp,)),
            dma((n_tensor // 2, n_dp)),
            dma((KINDS,)),
            dma((KINDS, n_tensor, 2)),
            dma((KINDS, n_tensor)),
            dma((KINDS, n_tensor, 2)),
            dma((KINDS, n_tensor, 2, chips)),
            dma((KINDS, n_tensor, 2)),
            dma((KINDS, n_tensor, 2, chips)),
            dma((n_tensor, 2)),
            dma((n_tensor, 2)),
            dma((n_tensor,)),
            dma((n_tensor,)),
            dma((2,)),
            dma((n_tensor, 2)),
            dma((n_tensor, 2)),
            dma((2, 2)),
            dma((2, 2)),
            dma((SMALL,)),
            dma((count,)),
            dma((count,)),
            dma((SMALL,)),
            dma((pieces,)),
            dma((pieces,)),
            dma((pieces, 2)),
            dma((pieces, 2, chips)),
            dma((pieces,)),
            dma((pieces,)),
            dma((KINDS,)),
        ],
        compiler_params=pltpu.CompilerParams(
            collective_id=0, has_side_effects=True, vmem_limit_bytes=VMEM_LIMIT
        ),
        name="encoder_layer",
    )(undealing, lengths, vecs, x_in, cot_in, shard, biases)


def shards(
    n_dp,
    n_tensor,
    inputs,
    cotangent,
    lengths,
    dealing,
    undealing,
    query_weight,
    key_weight,
    value_weight,
    output_weight,
    up_weight,
    down_weight,
    query_bias,
    value_bias,
    output_bias,
    up_bias,
    down_bias,
    first_gain,
    first_shift,
    second_gain,
    second_shift,
):
    span, slots, width = inputs.shape
    group = query_weight.shape[1]
    shard = jnp.stack(
        [
            jnp.concatenate([query_weight, key_weight, value_weight, output_weight.T], axis=1),
            up_weight,
            down_weight.T,
        ]
    ).astype(BF)
    blank = jnp.zeros((group,), F32)
    biases = jnp.concatenate([query_bias, value_bias, up_bias, blank, blank]).reshape(8, group)
    vecs = jnp.stack([output_bias, down_bias, first_gain, first_shift, second_gain, second_shift])
    vecs = jnp.pad(vecs, ((0, 2), (0, 0)))
    _, sums, small, returned = run_layer(
        n_dp,
        n_tensor,
        undealing,
        lengths,
        vecs,
        jnp.transpose(inputs, (1, 0, 2)),
        jnp.transpose(cotangent, (1, 0, 2)),
        shard,
        biases,
    )
    returned = jnp.transpose(returned, (0, 2, 1, 3))
    small = small.reshape(SMALL, width)
    t = lax.axis_index("tensor")

    def mine(row):
        return lax.dynamic_slice(small[row], (t * group,), (group,))

    return (
        returned[0],
        returned[1],
        sums[0][:, :group],
        sums[0][:, group : 2 * group],
        sums[0][:, 2 * group : 3 * group],
        sums[0][:, 3 * group :].T,
        sums[1],
        sums[2].T,
        mine(0),
        mine(1),
        small[2],
        lax.dynamic_index_in_dim(small, 3 + t, 0, keepdims=False),
        small[7],
        small[8],
        small[9],
        small[10],
        small[11],
    )


def solution(mesh):
    tokens = P("tensor", "dp", None)
    rows, columns = P("dp", "tensor"), P("tensor", "dp")
    split, copied = P("tensor"), P()
    return jax.shard_map(
        functools.partial(shards, mesh.shape["dp"], mesh.shape["tensor"]),
        mesh=mesh,
        in_specs=(
            (tokens, tokens, copied, copied, copied)
            + (rows, rows, rows, columns, rows, columns)
            + (split, split, copied, split, copied, copied, copied, copied, copied)
        ),
        out_specs=(
            (tokens, tokens, rows, rows, rows, columns, rows, columns)
            + (split, split, copied, split, copied, copied, copied, copied, copied)
        ),
        check_vma=False,
    )
```

```python
import functools

import jax
import jax.numpy as jnp
from jax import lax
from jax.experimental import pallas as pl
from jax.experimental.pallas import tpu as pltpu
from jax.sharding import PartitionSpec as P

HEAD_DIM = 64
KINDS = 3
MESH = pl.DeviceIdType.MESH
VMEM_LIMIT = 63 << 20
BF = jnp.bfloat16
F32 = jnp.float32


def flip(index, bit):
    unit = 1 << bit
    return index + unit * (1 - 2 * lax.rem(lax.div(index, unit), 2))


def orders(bits):
    return (tuple(range(bits)), tuple(reversed(range(bits))))


def relative(chip, order, code):
    for place, bit in enumerate(order):
        if code >> place & 1:
            chip = flip(chip, bit)
    return chip


def place():
    d, t = lax.axis_index("dp"), lax.axis_index("tensor")
    return d, t, lax.div(d, 2), lax.rem(d, 2)


def greet(n_dp, n_tensor):
    d, t, _, _ = place()
    barrier = pltpu.get_barrier_semaphore()
    me = d * n_tensor + t
    count = n_dp * n_tensor

    def one(step, carry):
        other = lax.rem(me + step, count)
        pl.semaphore_signal(
            barrier,
            inc=1,
            device_id=(lax.div(other, n_tensor), lax.rem(other, n_tensor)),
            device_id_type=MESH,
        )
        return carry

    lax.fori_loop(1, count, one, 0)
    pl.semaphore_wait(barrier, count - 1)


def remote(src, dst, ssem, rsem, device):
    return pltpu.make_async_remote_copy(
        src_ref=src,
        dst_ref=dst,
        send_sem=ssem,
        recv_sem=rsem,
        device_id=device,
        device_id_type=MESH,
    )


def landed(ref, sem):
    pltpu.make_async_copy(ref, ref, sem).wait()


def send_or_keep(mine, src, dst, ssem, rsem, device):
    @pl.when(mine)
    def _():
        pltpu.make_async_copy(src, dst, rsem).start()

    @pl.when(jnp.logical_not(mine))
    def _():
        remote(src, dst, ssem, rsem, device).start()


def sent(mine, src, ssem):
    @pl.when(jnp.logical_not(mine))
    def _():
        landed(src, ssem)


LAG = 2
SMALL = 12
SLOTS = 6
DEEP = 0
PLAN = (((3, 3), (4, 4), (5, 6), (7, 8)), ((3, 4), (4, 5), (6, 7), (8, 9)))
LAST = 9
COT_ONE, COT_TWO, X_START = 4, 9, 1


def layer_kernel(
    n_dp,
    n_tensor,
    undealing,
    lengths,
    vec_ref,
    x_ref,
    cot_ref,
    shard_ref,
    bias_ref,
    full_ref,
    sum_ref,
    small_out,
    y_out,
    c_one,
    c_two,
    bias_v,
    wbuf,
    q_v,
    k_v,
    v_v,
    lts,
    rms,
    n1_v,
    n2_v,
    cot_v,
    y_v,
    acc,
    lse_v,
    lse_rows,
    rstd_v,
    mix_grad,
    delta_v,
    dqt_v,
    kt_v,
    dkv_v,
    dkv_in,
    outbox,
    from_core,
    held,
    from_chip,
    from_z,
    small_v,
    small_in,
    x_s,
    x_r,
    c1_s,
    c1_r,
    c2_s,
    c2_r,
    own_sem,
    gz_s,
    gz_r,
    gxy_s,
    gxy_r,
    sib_s,
    sib_r,
    kv_s,
    kv_r,
    bz_s,
    bz_r,
    w_sem,
    dkv_s,
    dkv_r,
    y_s,
    y_r,
    b_s,
    b_r,
    bo_s,
    bo_r,
    core_s,
    core_r,
    xy_s,
    xy_r,
    z_s,
    z_r,
    out_sem,
):
    d, t, chip, core = place()
    chips = n_dp // 2
    bits = chips.bit_length() - 1
    half_t = n_tensor // 2
    count = n_dp * n_tensor
    me = d * n_tensor + t
    rows, cols = shard_ref.shape[1:]
    half_cols = cols // 2
    group = q_v.shape[2]
    span, width = x_ref.shape[1:]
    half_width = width // 2
    tokens = 2 * span
    units = cols
    prow, pcol = c_one.shape[2:]
    n_col = width // pcol
    pieces = KINDS * n_tensor
    sibling = (d + 1 - 2 * core, t)
    length = lengths[4 * chip + t]
    mine = pl.ds(pl.multiple_of(core * tokens, tokens), tokens)
    others = pl.ds(pl.multiple_of((1 - core) * tokens, tokens), tokens)
    greet(n_dp, n_tensor)

    def block(k, tt, who, half):
        return full_ref.at[
            k,
            tt,
            pl.ds(pl.multiple_of((2 * who + core) * rows, rows), rows),
            pl.ds(half * half_cols, half_cols),
        ]

    def arriving(index):
        rest, others = index - KINDS, n_tensor - 1
        return jnp.where(
            index < KINDS,
            index * n_tensor,
            lax.div(rest, others) * n_tensor + 1 + lax.rem(rest, others),
        )

    def stripe(k, tt):
        return full_ref.at[k, tt, pl.ds(pl.multiple_of(d * rows, rows), rows)]

    def at(index):
        step = lax.rem(index, n_tensor)
        near = jnp.where(t < half_t, t, n_tensor - 1 - t)
        spot = jnp.where(step <= near, near - step, step)
        return lax.div(index, n_tensor), jnp.where(t < half_t, spot, n_tensor - 1 - spot)

    for k in range(KINDS):
        pltpu.make_async_copy(shard_ref.at[k], stripe(k, t), own_sem.at[k]).start()

    def relay(index):
        k, tt = at(index)

        @pl.when(tt != t)
        def _():
            landed(shard_ref.at[0], gz_r.at[k, tt])

        for way, wanted in ((1, (tt <= t) & (t < n_tensor - 1)), (0, (tt >= t) & (t > 0))):

            @pl.when(wanted)
            def _(way=way):
                remote(
                    stripe(k, tt),
                    stripe(k, tt),
                    gz_s.at[k, tt, way],
                    gz_r.at[k, tt],
                    (d, t + 2 * way - 1),
                ).start()

    def relayed(k, tt):
        for way, wanted in ((1, (tt <= t) & (t < n_tensor - 1)), (0, (tt >= t) & (t > 0))):

            @pl.when(wanted)
            def _(way=way):
                landed(shard_ref.at[0], gz_s.at[k, tt, way])

    def start_tokens():
        for s in range(2):
            send_or_keep(
                (lax.div(t, half_t) == core) & (2 * core + s == t),
                x_ref.at[s],
                outbox.at[0, pl.ds(pl.multiple_of(lax.rem(t, half_t) * span, span), span)],
                x_s.at[s],
                x_r.at[lax.rem(t, half_t)],
                (2 * chip + lax.div(t, half_t), 2 * core + s),
            )

    def start_biases():
        pltpu.make_async_copy(bias_ref, bias_v.at[t], bz_r.at[0]).start()
        for step in range(1, n_tensor):
            remote(
                bias_ref,
                bias_v.at[t],
                bz_s.at[step],
                bz_r.at[step],
                (d, lax.rem(t + step, n_tensor)),
            ).start()

    def piece(who):
        return cot_ref.at[
            :,
            pl.ds(pl.multiple_of(lax.div(who, n_col) * prow, prow), prow),
            pl.ds(pl.multiple_of(lax.rem(who, n_col) * pcol, pcol), pcol),
        ]

    def cot_first():
        pltpu.make_async_copy(piece(d), c_one.at[d], c1_r.at[0]).start()
        for step in range(1, n_dp):
            who = lax.rem(d + step, n_dp)
            remote(piece(who), c_one.at[d], c1_s.at[step], c1_r.at[step], (who, t)).start()

    def cot_second():
        for step in range(n_dp):
            landed(c_one.at[0], c1_r.at[step])
        count = 2 * n_dp
        for step in range(count):
            seq = lax.rem(4 * chip + step, count)
            slot = undealing[seq]
            c_two[seq] = c_one[lax.div(slot, 2), lax.rem(slot, 2)]
            goal = 2 * lax.div(seq, 4) + lax.div(t, half_t)
            send_or_keep(
                (goal == d) & (lax.rem(seq, 4) == t),
                c_two.at[seq],
                cot_v.at[
                    pl.ds(
                        pl.multiple_of(lax.rem(t, half_t) * span + lax.div(d, n_col) * prow, prow),
                        prow,
                    ),
                    pl.ds(pl.multiple_of(lax.rem(d, n_col) * pcol, pcol), pcol),
                ],
                c2_s.at[step],
                c2_r.at[lax.rem(t, half_t), d],
                (goal, lax.rem(seq, 4)),
            )

    def forward(k, tt, half, code):
        order = orders(bits)[half]
        ref = block(k, tt, relative(chip, order, code), half)
        for s in range(code.bit_length(), bits):
            target = code | 1 << s
            remote(
                ref,
                ref,
                gxy_s.at[k, tt, half],
                gxy_r.at[k, tt, half, target],
                (2 * flip(chip, order[s]) + core, t),
            ).start()
        remote(
            ref, ref, sib_s.at[k, tt, half], sib_r.at[k, tt, half, code], sibling
        ).start()

    def receive(index, codes):
        k, tt = at(arriving(index))
        for code in codes:
            for half in range(2):
                landed(block(k, tt, chip, half), gxy_r.at[k, tt, half, code])
                forward(k, tt, half, code)

    early, late = range(1, max(chips // 2, 1)), range(max(chips // 2, 1), chips)

    def comm_step(index):
        @pl.when((index + 2 >= KINDS) & (index + 2 < pieces))
        def _():
            k, tt = at(arriving(index + 2))
            for half in range(2):
                forward(k, tt, half, 0)

        @pl.when(index < pieces)
        def _():
            receive(index, early)

        @pl.when(index >= LAG)
        def _():
            receive(index - LAG, late)

        follow = index + KINDS
        others = n_tensor - 1

        @pl.when(follow < pieces)
        def _():
            relay(arriving(follow))

            @pl.when((lax.rem(index, others) == others - 1) & (follow + 1 < pieces))
            def _():
                relay(lax.div(index, others) * n_tensor + n_tensor)

    def load(index):
        k, tt = at(index)
        slot = lax.rem(index, 2)
        for half in range(2):
            for code in range(chips):
                landed(block(k, tt, chip, half), sib_r.at[k, tt, half, code])
        copy = pltpu.make_async_copy(full_ref.at[k, tt], wbuf.at[slot], w_sem.at[slot])
        copy.start()
        copy.wait()

    def project(index):
        _, tt = at(index)
        slot = lax.rem(index, 2)
        x = outbox[0]
        for c in range(3):
            out = jnp.dot(
                x, wbuf[slot, :, c * group : (c + 1) * group], preferred_element_type=F32
            )
            if c == 0:
                q_v[tt] = ((out + bias_v[tt, 0:1]) * 0.125).astype(BF)
            elif c == 1:
                k_v[tt, mine] = out.astype(BF)
            else:
                v_v[tt, mine] = (out + bias_v[tt, 1:2]).astype(BF)
        for j, ref in enumerate((k_v, v_v)):
            remote(
                ref.at[tt, mine], ref.at[tt, mine], kv_s.at[tt, j], kv_r.at[tt, j], sibling
            ).start()

    def attend(index):
        _, tt = at(index)
        slot = lax.rem(index, 2)
        for j, ref in enumerate((k_v, v_v)):
            landed(ref.at[tt, mine], kv_r.at[tt, j])
        block_rows = min(256, tokens)
        low = lax.broadcasted_iota(jnp.int32, (block_rows, 2 * HEAD_DIM), 1) < HEAD_DIM
        lanes = lax.broadcasted_iota(jnp.int32, (block_rows, lse_v.shape[1]), 1)
        live = lax.broadcasted_iota(jnp.int32, (1, 2 * tokens), 1) < length

        def pair_step(step, carry):
            pair, part = lax.div(step, tokens // block_rows), lax.rem(step, tokens // block_rows)
            wide = pl.ds(pl.multiple_of(pair * 2 * HEAD_DIM, 2 * HEAD_DIM), 2 * HEAD_DIM)
            spot = pl.ds(pl.multiple_of(part * block_rows, block_rows), block_rows)
            k_pair, v_pair = k_v[tt, :, wide], v_v[tt, :, wide]
            q_pair = q_v[tt, spot, wide]
            outs = []
            for head in range(2):
                q_one = jnp.where(low if head == 0 else jnp.logical_not(low), q_pair, 0).astype(BF)
                scores = lax.dot_general(
                    q_one, k_pair, (((1,), (1,)), ((), ())), preferred_element_type=F32
                )
                scores = jnp.where(live, scores, -1000000000.0)
                summit = jnp.max(scores, axis=-1, keepdims=True)
                raised = jnp.exp(scores - summit)
                total = jnp.sum(raised, axis=-1, keepdims=True)
                out = jnp.dot(raised.astype(BF), v_pair, preferred_element_type=F32)
                outs.append(out / total)
                number = tt * (group // HEAD_DIM) + pair * 2 + head
                lse_v[spot] = jnp.where(lanes == number, summit + jnp.log(total), lse_v[spot])
            rms[2, tt, spot, pl.ds(pl.multiple_of(3 * group + pair * 2 * HEAD_DIM, 2 * HEAD_DIM), 2 * HEAD_DIM)] = jnp.where(low, outs[0], outs[1]).astype(BF)
            return carry

        lax.fori_loop(0, (group // (2 * HEAD_DIM)) * (tokens // block_rows), pair_step, 0)
        for n in range(width // 256):
            acc[:, n * 256 : (n + 1) * 256] += lax.dot_general(
                rms[2, tt, :, 3 * group :],
                wbuf[slot, n * 256 : (n + 1) * 256, 3 * group :],
                (((1,), (1,)), ((), ())),
                preferred_element_type=F32,
            )

    chunk = 64

    def norm(which, keep):
        gain, shift = vec_ref[2 + 2 * which : 3 + 2 * which], vec_ref[3 + 2 * which : 4 + 2 * which]

        def one(step, carry):
            spot = pl.ds(pl.multiple_of(step * chunk, chunk), chunk)
            value = acc[spot]
            center = value - jnp.mean(value, axis=-1, keepdims=True)
            spread = jnp.mean(center * center, axis=-1, keepdims=True)
            inverse = lax.rsqrt(spread + 1e-05)
            unit = center * inverse
            rstd_v[which, spot] = jnp.broadcast_to(inverse, (chunk, rstd_v.shape[2]))
            keep(spot, unit, unit * gain + shift)
            return carry

        lax.fori_loop(0, tokens // chunk, one, 0)

    def keep_one(spot, unit, hidden):
        n1_v[spot] = unit.astype(BF)
        outbox[1, spot] = hidden.astype(BF)
        acc[spot] = hidden + vec_ref[1:2]

    def keep_two(spot, unit, hidden):
        n2_v[spot] = unit.astype(BF)
        y_v[spot] = hidden.astype(BF)

    def turn_rows(source, which):
        flat = jnp.transpose(source)
        for dev in range(n_dp):
            lts[which, dev % 2, (dev // 2) * rows : (dev // 2 + 1) * rows] = flat[
                dev * rows : (dev + 1) * rows
            ]

    def expand(index):
        _, tt = at(index)
        slot = lax.rem(index, 2)

        def one(n, carry):
            wide = pl.ds(pl.multiple_of(n * 256, 256), 256)
            u = jnp.dot(outbox[1], wbuf[slot, :, wide], preferred_element_type=F32)
            u = u + bias_v[tt, pl.ds(2 + n, 1)]
            bell, below = gauss(u)
            rms[0, tt, :, wide] = (u * below).astype(BF)
            rms[1, tt, :, wide] = (below + u * bell).astype(BF)
            return carry

        lax.fori_loop(0, units // 256, one, 0)

    def contract(index):
        _, tt = at(index)
        slot = lax.rem(index, 2)

        def one(n, carry):
            wide = pl.ds(pl.multiple_of(n * 256, 256), 256)
            acc[:, wide] += lax.dot_general(
                rms[0, tt], wbuf[slot, wide, :], (((1,), (1,)), ((), ())), preferred_element_type=F32
            )
            return carry

        lax.fori_loop(0, width // 256, one, 0, unroll=True)

    landed(shard_ref.at[0], own_sem.at[0])
    relay(jnp.int32(0))
    start_biases()
    for k in range(KINDS):
        if k:
            landed(shard_ref.at[0], own_sem.at[k])
        for half in range(2):
            forward(k, t, half, 0)
    def tokens_here():
        for s in range(2):
            landed(x_ref.at[s], x_r.at[s])
        for step in range(n_tensor):
            landed(bias_ref, bz_r.at[step])
        acc[...] = outbox[0].astype(F32) + vec_ref[0:1]
        turn_rows(outbox[0], 2)
        lse_v[...] = jnp.zeros_like(lse_v)

    def turn(index, carry):
        comm_step(index)
        done = index - LAG

        @pl.when(index == X_START)
        def _():
            start_tokens()

        @pl.when(done == 2)
        def _():
            tokens_here()

        @pl.when((done >= 3) & (done <= 6))
        def _():
            attend(done - 3)

        @pl.when((done >= 2) & (done <= 5))
        def _():
            load(done - 2)
            project(done - 2)

        @pl.when(index == COT_ONE)
        def _():
            cot_first()

        @pl.when(index == COT_TWO)
        def _():
            cot_second()

        @pl.when(done == 6)
        def _():
            norm(0, keep_one)
            turn_rows(outbox[1], 1)
            lse_rows[...] = jnp.transpose(lse_v[...])

        def up(step, carry):
            load(step)
            expand(step)
            return carry

        def down(step, carry):
            load(step)
            contract(step)
            return carry

        lax.fori_loop(
            jnp.where(done == 8, 6, 4), jnp.where(done == 7, 6, jnp.where(done == 8, 8, 4)), up, 0
        )
        lax.fori_loop(
            jnp.where(done == 9, 8, jnp.where(done > 9, done, 8)),
            jnp.where(done == 9, 10, jnp.where(done > 9, done + 1, 8)),
            down,
            0,
        )
        return carry

    lax.fori_loop(0, pieces + LAG, turn, 0)
    norm(1, keep_two)

    def rat(step):
        near = jnp.where(step < 2, flip(t, 0), t)
        return jnp.where((step == 1) | (step == 2), flip(near, 1), near)

    def weights(k, step, slot):
        return pltpu.make_async_copy(full_ref.at[k, rat(step)], wbuf.at[slot], w_sem.at[slot])

    def send_output(a, source):
        for q in range(2):
            send_or_keep(
                (lax.div(t, half_t) == core) & (2 * core + q == t),
                source.at[pl.ds(q * span, span)],
                y_out.at[a, lax.rem(t, half_t)],
                y_s.at[a, q],
                y_r.at[a, lax.rem(t, half_t)],
                (2 * chip + lax.div(t, half_t), 2 * core + q),
            )


    def kind_of(index):
        return KINDS - 1 - lax.div(index, n_tensor)

    def emit(index):
        order = lax.div(index, n_tensor)
        tt = rat(lax.rem(index, n_tensor))
        slot, box = lax.rem(index, SLOTS), lax.rem(index, 2)

        @pl.when(index >= 2)
        def _():
            landed(outbox.at[0], core_s.at[index - 2])

        @pl.when(index >= SLOTS)
        def _():
            for half in range(2):
                landed(from_chip.at[0, 0], xy_s.at[index - SLOTS, half])

            @pl.when(lax.rem(index - SLOTS, n_tensor) < n_tensor - 1)
            def _():
                landed(from_z.at[0, 0], z_s.at[index - SLOTS])

        def one(n, carry):
            wide = pl.ds(pl.multiple_of(n * group, group), group)
            left = order + jnp.where((order == 2) & (n == 3), 1, 0)
            right = rms[order, tt, :, wide]
            outbox[box, :, wide] = jnp.dot(
                lts[left, 1 - core], right, preferred_element_type=F32
            ).astype(BF)
            held[slot, :, wide] = jnp.dot(
                lts[left, core], right, preferred_element_type=F32
            ).astype(BF)
            return carry

        lax.fori_loop(0, cols // group, one, 0, unroll=True)
        remote(
            outbox.at[box], from_core.at[lax.rem(index, 4)], core_s.at[index], core_r.at[index], sibling
        ).start()

    def spot_of(code, order):
        return pl.ds(pl.multiple_of(relative(chip, order, code) * rows, rows), rows)

    def pass_on(index, s):
        slot = lax.rem(index, SLOTS)
        for half in range(2):
            order = orders(bits)[half]
            for code in range(1 << s, 2 << s):
                remote(
                    held.at[slot, spot_of(code, order), pl.ds(half * half_cols, half_cols)],
                    from_chip.at[slot, half, code - 1],
                    xy_s.at[index, half],
                    xy_r.at[index, half, code],
                    (2 * flip(chip, order[s]) + core, t),
                ).start()

    def take_in(index, s):
        slot = lax.rem(index, SLOTS)
        for half in range(2):
            order = orders(bits)[half]
            for code in range(1 << s, 2 << s):
                landed(from_chip.at[0, 0, 0], xy_r.at[index, half, code])
                spot = spot_of(code - (1 << s), order)
                wide = pl.ds(half * half_cols, half_cols)
                held[slot, spot, wide] = (
                    held[slot, spot, wide].astype(F32)
                    + from_chip[slot, half, code - 1].astype(F32)
                ).astype(BF)

    def first(index):
        slot = lax.rem(index, SLOTS)
        landed(outbox.at[0], core_r.at[index])
        part = min(128, half_width)

        def add(c, carry):
            spot = pl.ds(pl.multiple_of(c * part, part), part)
            held[slot, spot] = (
                held[slot, spot].astype(F32) + from_core[lax.rem(index, 4), spot].astype(F32)
            ).astype(BF)
            return carry

        lax.fori_loop(0, half_width // part, add, 0)
        if bits:
            pass_on(index, bits - 1)

    def finish(index):
        slot, step = lax.rem(index, SLOTS), lax.rem(index, n_tensor)
        source = pl.ds(pl.multiple_of(chip * rows, rows), rows)

        k = kind_of(index)

        @pl.when(step >= 2)
        def _():
            given = 3 - step
            landed(from_z.at[0, 0], z_r.at[index - step + given])
            held[slot, source] = (
                held[slot, source].astype(F32) + from_z[k, given].astype(F32)
            ).astype(BF)

        @pl.when(step == n_tensor - 1)
        def _():
            from_z[k, step] = held[slot, source]

        @pl.when(step < n_tensor - 1)
        def _():
            remote(
                held.at[slot, source],
                from_z.at[k, step],
                z_s.at[index],
                z_r.at[index],
                (d, jnp.where(step < 2, flip(t, 0), flip(t, 1))),
            ).start()

    def advance(index):
        @pl.when(index < pieces)
        def _():
            emit(index)

        for stage in range(bits + 1):
            earlier = index - 1 - stage - (DEEP if stage else 0)

            @pl.when((earlier >= 0) & (earlier < pieces))
            def _(stage=stage, earlier=earlier):
                if stage == 0:
                    first(earlier)
                else:
                    take_in(earlier, bits - stage)
                    if stage < bits:
                        pass_on(earlier, bits - stage - 1)
                if stage == bits:
                    finish(earlier)

    def keep_small(which, row):
        for r in range(8):
            small_v[which, r : r + 1] = row[:, r * 128 : (r + 1) * 128]

    def norm_back(which, unit_ref, incoming, low_ref):
        gain = vec_ref[2 + 2 * which : 3 + 2 * which]

        def one(step, carry):
            spot = pl.ds(pl.multiple_of(step * chunk, chunk), chunk)
            e = incoming(step, spot)
            unit = unit_ref[spot].astype(F32)
            ge = e * gain
            first_mean = jnp.mean(ge, axis=-1, keepdims=True)
            second_mean = jnp.mean(ge * unit, axis=-1, keepdims=True)
            grad = (ge - first_mean - unit * second_mean) * rstd_v[which, spot, 0:1]
            acc[spot] = grad
            low = grad.astype(BF)
            low_ref[spot] = low
            return (
                carry[0] + jnp.sum(e * unit, axis=0, keepdims=True),
                carry[1] + jnp.sum(e, axis=0, keepdims=True),
                carry[2] + jnp.sum(low.astype(F32), axis=0, keepdims=True),
            )

        zero = jnp.zeros((1, width), F32)
        return lax.fori_loop(0, tokens // chunk, one, (zero, zero, zero))

    for q in range(half_t):
        for who in range(n_dp):
            landed(c_two.at[0], c2_r.at[q, who])
    weights(2, 0, 0).start()
    weights(1, 0, 1).start()
    send_output(0, y_v)

    def seed(step, spot):
        number = core * tokens + step * chunk + lax.broadcasted_iota(jnp.int32, (chunk, 1), 0)
        return jnp.where(number < length, cot_v[spot].astype(F32), 0.0)

    sums = norm_back(1, n2_v, seed, cot_v)
    keep_small(10, sums[0])
    keep_small(11, sums[1])
    keep_small(7, sums[2])
    turn_rows(cot_v[...], 0)
    advance(jnp.int32(0))

    def mlp(step, carry):
        tt = rat(step)
        weights(2, step, 0).wait()

        def one(n, carry):
            wide = pl.ds(pl.multiple_of(n * 256, 256), 256)
            grad = jnp.dot(cot_v[...], wbuf[0, :, wide], preferred_element_type=F32)
            rms[1, tt, :, wide] = (rms[1, tt, :, wide].astype(F32) * grad).astype(BF)
            return carry

        lax.fori_loop(0, cols // 256, one, 0, unroll=True)

        @pl.when(step < n_tensor - 1)
        def _():
            weights(2, step + 1, 0).start()

        @pl.when(step == n_tensor - 1)
        def _():
            weights(0, 0, 0).start()

        total = jnp.sum(rms[1, tt].astype(F32), axis=0, keepdims=True)
        for r in range(8):
            small_v[3 + tt, r : r + 1] = total[:, r * 128 : (r + 1) * 128]
        weights(1, step, 1).wait()

        def two(n, carry):
            wide = pl.ds(pl.multiple_of(n * 256, 256), 256)
            acc[:, wide] += lax.dot_general(
                rms[1, tt], wbuf[1, wide, :], (((1,), (1,)), ((), ())), preferred_element_type=F32
            )
            return carry

        lax.fori_loop(0, width // 256, two, 0, unroll=True)

        @pl.when(step < n_tensor - 1)
        def _():
            weights(1, step + 1, 1).start()

        @pl.when(step == n_tensor - 1)
        def _():
            weights(0, 1, 1).start()

        @pl.when(lax.rem(step, 2) == 1)
        def _():
            advance(1 + lax.div(step, 2))

        return carry

    lax.fori_loop(0, n_tensor, mlp, 0)

    sums = norm_back(0, n1_v, lambda step, spot: acc[spot], n2_v)
    keep_small(8, sums[0])
    keep_small(9, sums[1])
    keep_small(2, sums[2])
    turn_rows(n2_v[...], 3)

    key_rows = min(256, 2 * tokens)
    low_lanes = lax.broadcasted_iota(jnp.int32, (tokens, 2 * HEAD_DIM), 1) < HEAD_DIM

    def prepare(step):
        tt, slot = rat(step), lax.rem(step, 2)
        weights(0, step, slot).wait()
        grad = jnp.dot(
            n2_v[...], wbuf[slot, :, 3 * group :], preferred_element_type=F32
        ).astype(BF)
        mix_grad[...] = grad
        both = grad.astype(F32) * rms[2, tt, :, 3 * group :].astype(F32)
        high = both.astype(BF)
        rest = (both - high.astype(F32)).astype(BF)
        heads = lax.broadcasted_iota(jnp.int32, (8, group), 0)
        lanes = lax.broadcasted_iota(jnp.int32, (8, group), 1)
        picks = jnp.where(lax.div(lanes, HEAD_DIM) == heads, 1.0, 0.0).astype(BF)
        dims = (((1,), (1,)), ((), ()))
        delta_v[...] = lax.dot_general(
            picks, high, dims, preferred_element_type=F32
        ) + lax.dot_general(picks, rest, dims, preferred_element_type=F32)

        @pl.when(step >= 2)
        def _():
            for j in range(2):
                landed(dkv_in.at[0, 0], dkv_s.at[step - 2, j])

    def pair_back(step, pair):
        tt, slot = rat(step), lax.rem(step, 2)
        wide = pl.ds(pl.multiple_of(pair * 2 * HEAD_DIM, 2 * HEAD_DIM), 2 * HEAD_DIM)
        q_pair, o_pair = q_v[tt, :, wide], mix_grad[:, wide]
        q_ones = [jnp.where(low_lanes, q_pair, 0).astype(BF), jnp.where(low_lanes, 0, q_pair).astype(BF)]
        o_ones = [jnp.where(low_lanes, o_pair, 0).astype(BF), jnp.where(low_lanes, 0, o_pair).astype(BF)]
        kt_v[...] = jnp.transpose(k_v[tt, :, wide])
        dqt_v[...] = jnp.zeros_like(dqt_v)
        dims = (((1,), (1,)), ((), ()))

        def block(b, carry):
            spot = pl.ds(pl.multiple_of(b * key_rows, key_rows), key_rows)
            k_part, v_part = k_v[tt, spot, wide], v_v[tt, spot, wide]
            number = b * key_rows + lax.broadcasted_iota(jnp.int32, (key_rows, 1), 0)
            live = number < length
            dv, dk = None, None
            for head in range(2):
                which = tt * (group // HEAD_DIM) + pair * 2 + head
                scores = lax.dot_general(k_part, q_ones[head], dims, preferred_element_type=F32)
                probs = jnp.where(live, jnp.exp(scores - lse_rows[pl.ds(which, 1)]), 0.0)
                prob_grad = lax.dot_general(v_part, o_ones[head], dims, preferred_element_type=F32)
                score_grad = (probs * (prob_grad - delta_v[pl.ds(pair * 2 + head, 1)])).astype(BF)
                one_v = jnp.dot(probs.astype(BF), o_ones[head], preferred_element_type=F32)
                one_k = jnp.dot(score_grad, q_ones[head], preferred_element_type=F32)
                dv = one_v if dv is None else dv + one_v
                dk = one_k if dk is None else dk + one_k
                rows_here = slice(head * HEAD_DIM, (head + 1) * HEAD_DIM)
                dqt_v[rows_here] += jnp.dot(
                    kt_v[rows_here, spot], score_grad, preferred_element_type=F32
                )
            dkv_v[slot, 0, spot, wide] = dk.astype(BF)
            dkv_v[slot, 1, spot, wide] = dv.astype(BF)
            return carry

        lax.fori_loop(0, 2 * tokens // key_rows, block, 0)
        dq = jnp.transpose(dqt_v[...].astype(BF).astype(F32)) * 0.125
        rms[2, tt, :, wide] = dq.astype(BF)
        total = jnp.sum(dq, axis=0, keepdims=True)
        small_v[0, pl.ds(tt * (group // 128) + pair, 1)] = total

    def exchange(step):
        slot = lax.rem(step, 2)
        for j in range(2):
            remote(
                dkv_v.at[slot, j, others],
                dkv_in.at[step, j],
                dkv_s.at[step, j],
                dkv_r.at[step, j],
                sibling,
            ).start()

    def collect(step):
        tt, slot = rat(step), lax.rem(step, 2)
        for j in range(2):
            landed(dkv_in.at[0, 0], dkv_r.at[step, j])
            value = (
                dkv_v[slot, j, mine].astype(F32) + dkv_in[step, j].astype(F32)
            ).astype(BF)
            rms[2, tt, :, (1 + j) * group : (2 + j) * group] = value
            if j:
                total = jnp.sum(value.astype(F32), axis=0, keepdims=True)
                for r in range(group // 128):
                    small_v[1, pl.ds(tt * (group // 128) + r, 1)] = total[:, r * 128 : (r + 1) * 128]

        def one(n, carry):
            wide = pl.ds(pl.multiple_of(n * 256, 256), 256)
            acc[:, wide] += lax.dot_general(
                rms[2, tt, :, : 3 * group],
                wbuf[slot, wide, : 3 * group],
                (((1,), (1,)), ((), ())),
                preferred_element_type=F32,
            )
            return carry

        lax.fori_loop(0, width // 256, one, 0, unroll=True)

    def run(index, carry):
        advance(index)
        return carry

    def attention(step, carry):
        @pl.when(step < n_tensor)
        def _():
            prepare(step)
            for pair in range(group // (2 * HEAD_DIM)):
                pair_back(step, pair)
                low, high = jnp.int32(0), jnp.int32(0)
                for s, (begin, end) in enumerate(PLAN[pair]):
                    low, high = jnp.where(step == s, begin, low), jnp.where(step == s, end, high)
                lax.fori_loop(low, high, run, 0)

            exchange(step)

        @pl.when(step >= 1)
        def _():
            collect(step - 1)

            @pl.when(step < n_tensor - 1)
            def _():
                weights(0, step + 1, lax.rem(step + 1, 2)).start()

        return carry

    lax.fori_loop(0, n_tensor + 1, attention, 0)

    cot_v[...] = acc[...].astype(BF)
    send_output(1, cot_v)
    for j in range(SMALL):
        send_or_keep(
            me == j,
            small_v.at[j],
            small_in.at[me],
            b_s.at[j],
            b_r.at[me],
            (j // n_tensor, j % n_tensor),
        )
    def drain(index, carry):
        advance(index)
        return carry

    lax.fori_loop(LAST, pieces, drain, 0)

    @pl.when(me < SMALL)
    def _():
        def arrive(step, total):
            landed(small_in.at[0], b_r.at[step])
            return total + small_in[step]

        total = lax.fori_loop(0, count, arrive, jnp.zeros(small_in.shape[1:], F32))
        small_in[0] = total
        pltpu.make_async_copy(small_in.at[0], small_out.at[me], bo_r.at[me]).start()

        def spread(step, carry):
            other = lax.rem(me + step, count)
            remote(
                small_in.at[0],
                small_out.at[me],
                bo_s.at[step],
                bo_r.at[me],
                (lax.div(other, n_tensor), lax.rem(other, n_tensor)),
            ).start()
            return carry

        lax.fori_loop(1, count, spread, 0)

    lax.fori_loop(pieces, pieces + 1 + bits + DEEP, drain, 0)

    for k in range(KINDS):
        total = from_z[k, n_tensor - 1].astype(F32)
        landed(from_z.at[0, 0], z_r.at[(KINDS - 1 - k) * n_tensor + 2])
        total = total + from_z[k, 2].astype(F32)
        acc[k * rows : (k + 1) * rows] = total
        pltpu.make_async_copy(acc.at[pl.ds(k * rows, rows)], sum_ref.at[k], out_sem.at[k]).start()
    for k in range(KINDS):
        landed(acc.at[pl.ds(0, rows)], out_sem.at[k])

    for k in range(KINDS):
        for tt in range(n_tensor):
            relayed(k, tt)
            for half in range(2):
                half_rows = full_ref.at[k, tt, pl.ds(0, width // 2), pl.ds(0, half_cols)]
                landed(half_rows, sib_s.at[k, tt, half])
                if chips > 1:
                    most = full_ref.at[k, tt, pl.ds(0, width // 2 - rows), pl.ds(0, half_cols)]
                    landed(most, gxy_s.at[k, tt, half])
    for s in range(2):
        sent((lax.div(t, half_t) == core) & (2 * core + s == t), x_ref.at[s], x_s.at[s])
    for step in range(1, n_tensor):
        landed(bias_ref, bz_s.at[step])
    for tt in range(n_tensor):
        for j in range(2):
            landed(q_v.at[tt], kv_s.at[tt, j])
    for step in range(1, n_dp):
        landed(c_one.at[0], c1_s.at[step])
    for step in range(2 * n_dp):
        seq = lax.rem(4 * chip + step, 2 * n_dp)
        goal = 2 * lax.div(seq, 4) + lax.div(t, half_t)
        sent((goal == d) & (lax.rem(seq, 4) == t), c_two.at[0], c2_s.at[step])
    for j in range(SMALL):
        landed(small_v.at[0], bo_r.at[j])
        sent(me == j, small_v.at[0], b_s.at[j])

    @pl.when(me < SMALL)
    def _():
        def gone(step, carry):
            landed(small_v.at[0], bo_s.at[step])
            return carry

        lax.fori_loop(1, count, gone, 0)

    for a in range(2):
        for q in range(2):
            sent((lax.div(t, half_t) == core) & (2 * core + q == t), x_ref.at[q], y_s.at[a, q])
            landed(x_ref.at[q], y_r.at[a, q])
    for step in range(n_tensor - 2, n_tensor):
        for j in range(2):
            landed(dkv_in.at[0, 0], dkv_s.at[step, j])
    for index in range(pieces - 2, pieces):
        landed(outbox.at[0], core_s.at[index])
    for index in range(pieces - SLOTS, pieces):
        for half in range(2):
            landed(from_chip.at[0, 0], xy_s.at[index, half])
        if index % n_tensor < n_tensor - 1:
            landed(from_z.at[0, 0], z_s.at[index])


def gauss(u):
    size = jnp.abs(u)
    bell = 0.3989422804014327 * jnp.exp(-0.5 * (u * u))
    s = 1.0 / (1.0 + 0.23164190 * size)
    tail = bell * s * (
        0.319381530 + s * (-0.356563782 + s * (1.781477937 + s * (-1.821255978 + s * 1.330274429)))
    )
    return bell, jnp.where(u < 0, tail, 1.0 - tail)


def run_layer(n_dp, n_tensor, undealing, lengths, vecs, x_in, cot_in, shard, biases):
    slots, span, width = x_in.shape
    rows, cols = shard.shape[1:]
    chips = n_dp // 2
    tokens = 2 * span
    group = cols // 4
    n_pos = min(n_dp, span // 16)
    prow, pcol = span // n_pos, width // (n_dp // n_pos)
    pieces = KINDS * n_tensor
    count = n_dp * n_tensor
    dma = pltpu.SemaphoreType.DMA
    any_space = pl.BlockSpec(memory_space=pl.ANY)
    smem = pl.BlockSpec(memory_space=pltpu.SMEM)
    vmem = pl.BlockSpec(memory_space=pltpu.VMEM)
    shapes = (
        ((KINDS, n_tensor, width, cols), BF),
        ((KINDS, rows, cols), F32),
        ((SMALL, 8, 128), F32),
        ((2, 2, span, width), BF),
    )
    return pl.pallas_call(
        functools.partial(layer_kernel, n_dp, n_tensor),
        out_shape=tuple(jax.ShapeDtypeStruct(*shape) for shape in shapes),
        in_specs=[smem, smem, vmem, any_space, any_space, vmem, vmem],
        out_specs=(any_space, any_space, any_space, any_space),
        scratch_shapes=[
            pltpu.VMEM((n_dp, slots, prow, pcol), BF),
            pltpu.VMEM((2 * n_dp, prow, pcol), BF),
            pltpu.VMEM((n_tensor,) + biases.shape, F32),
            pltpu.VMEM((2, width, cols), BF),
            pltpu.VMEM((n_tensor, tokens, group), BF),
            pltpu.VMEM((n_tensor, 2 * tokens, group), BF),
            pltpu.VMEM((n_tensor, 2 * tokens, group), BF),
            pltpu.VMEM((4, 2, width // 2, tokens), BF),
            pltpu.VMEM((KINDS, n_tensor, tokens, cols), BF),
            pltpu.VMEM((tokens, width), BF),
            pltpu.VMEM((tokens, width), BF),
            pltpu.VMEM((tokens, width), BF),
            pltpu.VMEM((tokens, width), BF),
            pltpu.VMEM((tokens, width), F32),
            pltpu.VMEM((tokens, 128), F32),
            pltpu.VMEM((128, tokens), F32),
            pltpu.VMEM((2, tokens, 128), F32),
            pltpu.VMEM((tokens, group), BF),
            pltpu.VMEM((8, tokens), F32),
            pltpu.VMEM((2 * HEAD_DIM, tokens), F32),
            pltpu.VMEM((2 * HEAD_DIM, 2 * tokens), BF),
            pltpu.VMEM((2, 2, 2 * tokens, group), BF),
            pltpu.VMEM((n_tensor, 2, tokens, group), BF),
            pltpu.VMEM((2, width // 2, cols), BF),
            pltpu.VMEM((4, width // 2, cols), BF),
            pltpu.VMEM((SLOTS, width // 2, cols), BF),
            pltpu.VMEM((SLOTS, 2, max(chips - 1, 1), rows, cols // 2), BF),
            pltpu.VMEM((KINDS, n_tensor, rows, cols), BF),
            pltpu.VMEM((SMALL, 8, 128), F32),
            pltpu.VMEM((count, 8, 128), F32),
            dma((2,)),
            dma((2,)),
            dma((n_dp,)),
            dma((n_dp,)),
            dma((2 * n_dp,)),
            dma((n_tensor // 2, n_dp)),
            dma((KINDS,)),
            dma((KINDS, n_tensor, 2)),
            dma((KINDS, n_tensor)),
            dma((KINDS, n_tensor, 2)),
            dma((KINDS, n_tensor, 2, chips)),
            dma((KINDS, n_tensor, 2)),
            dma((KINDS, n_tensor, 2, chips)),
            dma((n_tensor, 2)),
            dma((n_tensor, 2)),
            dma((n_tensor,)),
            dma((n_tensor,)),
            dma((2,)),
            dma((n_tensor, 2)),
            dma((n_tensor, 2)),
            dma((2, 2)),
            dma((2, 2)),
            dma((SMALL,)),
            dma((count,)),
            dma((count,)),
            dma((SMALL,)),
            dma((pieces,)),
            dma((pieces,)),
            dma((pieces, 2)),
            dma((pieces, 2, chips)),
            dma((pieces,)),
            dma((pieces,)),
            dma((KINDS,)),
        ],
        compiler_params=pltpu.CompilerParams(
            collective_id=0, has_side_effects=True, vmem_limit_bytes=VMEM_LIMIT
        ),
        name="encoder_layer",
    )(undealing, lengths, vecs, x_in, cot_in, shard, biases)


def shards(
    n_dp,
    n_tensor,
    inputs,
    cotangent,
    lengths,
    dealing,
    undealing,
    query_weight,
    key_weight,
    value_weight,
    output_weight,
    up_weight,
    down_weight,
    query_bias,
    value_bias,
    output_bias,
    up_bias,
    down_bias,
    first_gain,
    first_shift,
    second_gain,
    second_shift,
):
    span, slots, width = inputs.shape
    group = query_weight.shape[1]
    shard = jnp.stack(
        [
            jnp.concatenate([query_weight, key_weight, value_weight, output_weight.T], axis=1),
            up_weight,
            down_weight.T,
        ]
    ).astype(BF)
    blank = jnp.zeros((group,), F32)
    biases = jnp.concatenate([query_bias, value_bias, up_bias, blank, blank]).reshape(8, group)
    vecs = jnp.stack([output_bias, down_bias, first_gain, first_shift, second_gain, second_shift])
    vecs = jnp.pad(vecs, ((0, 2), (0, 0)))
    _, sums, small, returned = run_layer(
        n_dp,
        n_tensor,
        undealing,
        lengths,
        vecs,
        jnp.transpose(inputs, (1, 0, 2)),
        jnp.transpose(cotangent, (1, 0, 2)),
        shard,
        biases,
    )
    returned = jnp.transpose(returned, (0, 2, 1, 3))
    small = small.reshape(SMALL, width)
    t = lax.axis_index("tensor")

    def mine(row):
        return lax.dynamic_slice(small[row], (t * group,), (group,))

    return (
        returned[0],
        returned[1],
        sums[0][:, :group],
        sums[0][:, group : 2 * group],
        sums[0][:, 2 * group : 3 * group],
        sums[0][:, 3 * group :].T,
        sums[1],
        sums[2].T,
        mine(0),
        mine(1),
        small[2],
        lax.dynamic_index_in_dim(small, 3 + t, 0, keepdims=False),
        small[7],
        small[8],
        small[9],
        small[10],
        small[11],
    )


def solution(mesh):
    tokens = P("tensor", "dp", None)
    rows, columns = P("dp", "tensor"), P("tensor", "dp")
    split, copied = P("tensor"), P()
    return jax.shard_map(
        functools.partial(shards, mesh.shape["dp"], mesh.shape["tensor"]),
        mesh=mesh,
        in_specs=(
            (tokens, tokens, copied, copied, copied)
            + (rows, rows, rows, columns, rows, columns)
            + (split, split, copied, split, copied, copied, copied, copied, copied)
        ),
        out_specs=(
            (tokens, tokens, rows, rows, rows, columns, rows, columns)
            + (split, split, copied, split, copied, copied, copied, copied, copied)
        ),
        check_vma=False,
    )
```

```python
import functools

import jax
import jax.numpy as jnp
from jax import lax
from jax.experimental import pallas as pl
from jax.experimental.pallas import tpu as pltpu
from jax.sharding import PartitionSpec as P

HEAD_DIM = 64
KINDS = 3
MESH = pl.DeviceIdType.MESH
VMEM_LIMIT = 63 << 20
BF = jnp.bfloat16
F32 = jnp.float32


def flip(index, bit):
    unit = 1 << bit
    return index + unit * (1 - 2 * lax.rem(lax.div(index, unit), 2))


def orders(bits):
    return (tuple(range(bits)), tuple(reversed(range(bits))))


def relative(chip, order, code):
    for place, bit in enumerate(order):
        if code >> place & 1:
            chip = flip(chip, bit)
    return chip


def place():
    d, t = lax.axis_index("dp"), lax.axis_index("tensor")
    return d, t, lax.div(d, 2), lax.rem(d, 2)


def greet(n_dp, n_tensor):
    d, t, _, _ = place()
    barrier = pltpu.get_barrier_semaphore()
    me = d * n_tensor + t
    count = n_dp * n_tensor

    def one(step, carry):
        other = lax.rem(me + step, count)
        pl.semaphore_signal(
            barrier,
            inc=1,
            device_id=(lax.div(other, n_tensor), lax.rem(other, n_tensor)),
            device_id_type=MESH,
        )
        return carry

    lax.fori_loop(1, count, one, 0)
    pl.semaphore_wait(barrier, count - 1)


def remote(src, dst, ssem, rsem, device):
    return pltpu.make_async_remote_copy(
        src_ref=src,
        dst_ref=dst,
        send_sem=ssem,
        recv_sem=rsem,
        device_id=device,
        device_id_type=MESH,
    )


def landed(ref, sem):
    pltpu.make_async_copy(ref, ref, sem).wait()


def send_or_keep(mine, src, dst, ssem, rsem, device):
    @pl.when(mine)
    def _():
        pltpu.make_async_copy(src, dst, rsem).start()

    @pl.when(jnp.logical_not(mine))
    def _():
        remote(src, dst, ssem, rsem, device).start()


def sent(mine, src, ssem):
    @pl.when(jnp.logical_not(mine))
    def _():
        landed(src, ssem)


LAG = 2
SMALL = 12
SLOTS = 6
DEEP = 0
PLAN = (((3, 3), (4, 4), (5, 6), (7, 8)), ((3, 4), (4, 5), (6, 7), (8, 9)))
LAST = 9
COT_ONE, COT_TWO, X_START = 4, 9, 0


def layer_kernel(
    n_dp,
    n_tensor,
    undealing,
    lengths,
    vec_ref,
    x_ref,
    cot_ref,
    shard_ref,
    bias_ref,
    full_ref,
    sum_ref,
    small_out,
    y_out,
    c_one,
    c_two,
    bias_v,
    wbuf,
    q_v,
    k_v,
    v_v,
    lts,
    rms,
    n1_v,
    n2_v,
    cot_v,
    y_v,
    acc,
    lse_v,
    lse_rows,
    rstd_v,
    mix_grad,
    delta_v,
    dqt_v,
    kt_v,
    dkv_v,
    dkv_in,
    outbox,
    from_core,
    held,
    from_chip,
    from_z,
    small_v,
    small_in,
    x_s,
    x_r,
    c1_s,
    c1_r,
    c2_s,
    c2_r,
    own_sem,
    gz_s,
    gz_r,
    gxy_s,
    gxy_r,
    sib_s,
    sib_r,
    kv_s,
    kv_r,
    bz_s,
    bz_r,
    w_sem,
    dkv_s,
    dkv_r,
    y_s,
    y_r,
    b_s,
    b_r,
    bo_s,
    bo_r,
    core_s,
    core_r,
    xy_s,
    xy_r,
    z_s,
    z_r,
    out_sem,
):
    d, t, chip, core = place()
    chips = n_dp // 2
    bits = chips.bit_length() - 1
    half_t = n_tensor // 2
    count = n_dp * n_tensor
    me = d * n_tensor + t
    rows, cols = shard_ref.shape[1:]
    half_cols = cols // 2
    group = q_v.shape[2]
    span, width = x_ref.shape[1:]
    half_width = width // 2
    tokens = 2 * span
    units = cols
    prow, pcol = c_one.shape[2:]
    n_col = width // pcol
    pieces = KINDS * n_tensor
    sibling = (d + 1 - 2 * core, t)
    length = lengths[4 * chip + t]
    mine = pl.ds(pl.multiple_of(core * tokens, tokens), tokens)
    others = pl.ds(pl.multiple_of((1 - core) * tokens, tokens), tokens)
    greet(n_dp, n_tensor)

    def block(k, tt, who, half):
        return full_ref.at[
            k,
            tt,
            pl.ds(pl.multiple_of((2 * who + core) * rows, rows), rows),
            pl.ds(half * half_cols, half_cols),
        ]

    def arriving(index):
        rest, others = index - KINDS, n_tensor - 1
        return jnp.where(
            index < KINDS,
            index * n_tensor,
            lax.div(rest, others) * n_tensor + 1 + lax.rem(rest, others),
        )

    def stripe(k, tt):
        return full_ref.at[k, tt, pl.ds(pl.multiple_of(d * rows, rows), rows)]

    def at(index):
        step = lax.rem(index, n_tensor)
        near = jnp.where(t < half_t, t, n_tensor - 1 - t)
        spot = jnp.where(step <= near, near - step, step)
        return lax.div(index, n_tensor), jnp.where(t < half_t, spot, n_tensor - 1 - spot)

    for k in range(KINDS):
        pltpu.make_async_copy(shard_ref.at[k], stripe(k, t), own_sem.at[k]).start()

    def relay(index):
        k, tt = at(index)

        @pl.when(tt != t)
        def _():
            landed(shard_ref.at[0], gz_r.at[k, tt])

        for way, wanted in ((1, (tt <= t) & (t < n_tensor - 1)), (0, (tt >= t) & (t > 0))):

            @pl.when(wanted)
            def _(way=way):
                remote(
                    stripe(k, tt),
                    stripe(k, tt),
                    gz_s.at[k, tt, way],
                    gz_r.at[k, tt],
                    (d, t + 2 * way - 1),
                ).start()

    def relayed(k, tt):
        for way, wanted in ((1, (tt <= t) & (t < n_tensor - 1)), (0, (tt >= t) & (t > 0))):

            @pl.when(wanted)
            def _(way=way):
                landed(shard_ref.at[0], gz_s.at[k, tt, way])

    def start_tokens():
        for s in range(2):
            send_or_keep(
                (lax.div(t, half_t) == core) & (2 * core + s == t),
                x_ref.at[s],
                outbox.at[0, pl.ds(pl.multiple_of(lax.rem(t, half_t) * span, span), span)],
                x_s.at[s],
                x_r.at[lax.rem(t, half_t)],
                (2 * chip + lax.div(t, half_t), 2 * core + s),
            )

    def start_biases():
        pltpu.make_async_copy(bias_ref, bias_v.at[t], bz_r.at[0]).start()
        for step in range(1, n_tensor):
            remote(
                bias_ref,
                bias_v.at[t],
                bz_s.at[step],
                bz_r.at[step],
                (d, lax.rem(t + step, n_tensor)),
            ).start()

    def piece(who):
        return cot_ref.at[
            :,
            pl.ds(pl.multiple_of(lax.div(who, n_col) * prow, prow), prow),
            pl.ds(pl.multiple_of(lax.rem(who, n_col) * pcol, pcol), pcol),
        ]

    def cot_first():
        pltpu.make_async_copy(piece(d), c_one.at[d], c1_r.at[0]).start()
        for step in range(1, n_dp):
            who = lax.rem(d + step, n_dp)
            remote(piece(who), c_one.at[d], c1_s.at[step], c1_r.at[step], (who, t)).start()

    def cot_second():
        for step in range(n_dp):
            landed(c_one.at[0], c1_r.at[step])
        count = 2 * n_dp
        for step in range(count):
            seq = lax.rem(4 * chip + step, count)
            slot = undealing[seq]
            c_two[seq] = c_one[lax.div(slot, 2), lax.rem(slot, 2)]
            goal = 2 * lax.div(seq, 4) + lax.div(t, half_t)
            send_or_keep(
                (goal == d) & (lax.rem(seq, 4) == t),
                c_two.at[seq],
                cot_v.at[
                    pl.ds(
                        pl.multiple_of(lax.rem(t, half_t) * span + lax.div(d, n_col) * prow, prow),
                        prow,
                    ),
                    pl.ds(pl.multiple_of(lax.rem(d, n_col) * pcol, pcol), pcol),
                ],
                c2_s.at[step],
                c2_r.at[lax.rem(t, half_t), d],
                (goal, lax.rem(seq, 4)),
            )

    def forward(k, tt, half, code):
        order = orders(bits)[half]
        ref = block(k, tt, relative(chip, order, code), half)
        for s in range(code.bit_length(), bits):
            target = code | 1 << s
            remote(
                ref,
                ref,
                gxy_s.at[k, tt, half],
                gxy_r.at[k, tt, half, target],
                (2 * flip(chip, order[s]) + core, t),
            ).start()
        remote(
            ref, ref, sib_s.at[k, tt, half], sib_r.at[k, tt, half, code], sibling
        ).start()

    def receive(index, codes):
        k, tt = at(arriving(index))
        for code in codes:
            for half in range(2):
                landed(block(k, tt, chip, half), gxy_r.at[k, tt, half, code])
                forward(k, tt, half, code)

    early, late = range(1, max(chips // 2, 1)), range(max(chips // 2, 1), chips)

    def comm_step(index):
        @pl.when((index + 2 >= KINDS) & (index + 2 < pieces))
        def _():
            k, tt = at(arriving(index + 2))
            for half in range(2):
                forward(k, tt, half, 0)

        @pl.when(index < pieces)
        def _():
            receive(index, early)

        @pl.when(index >= LAG)
        def _():
            receive(index - LAG, late)

        follow = index + KINDS
        others = n_tensor - 1

        @pl.when(follow < pieces)
        def _():
            relay(arriving(follow))

            @pl.when((lax.rem(index, others) == others - 1) & (follow + 1 < pieces))
            def _():
                relay(lax.div(index, others) * n_tensor + n_tensor)

    def load(index):
        k, tt = at(index)
        slot = lax.rem(index, 2)
        for half in range(2):
            for code in range(chips):
                landed(block(k, tt, chip, half), sib_r.at[k, tt, half, code])
        copy = pltpu.make_async_copy(full_ref.at[k, tt], wbuf.at[slot], w_sem.at[slot])
        copy.start()
        copy.wait()

    def project(index):
        _, tt = at(index)
        slot = lax.rem(index, 2)
        x = outbox[0]
        for c in range(3):
            out = jnp.dot(
                x, wbuf[slot, :, c * group : (c + 1) * group], preferred_element_type=F32
            )
            if c == 0:
                q_v[tt] = ((out + bias_v[tt, 0:1]) * 0.125).astype(BF)
            elif c == 1:
                k_v[tt, mine] = out.astype(BF)
            else:
                v_v[tt, mine] = (out + bias_v[tt, 1:2]).astype(BF)
        for j, ref in enumerate((k_v, v_v)):
            remote(
                ref.at[tt, mine], ref.at[tt, mine], kv_s.at[tt, j], kv_r.at[tt, j], sibling
            ).start()

    def attend(index):
        _, tt = at(index)
        slot = lax.rem(index, 2)
        for j, ref in enumerate((k_v, v_v)):
            landed(ref.at[tt, mine], kv_r.at[tt, j])
        block_rows = min(256, tokens)
        low = lax.broadcasted_iota(jnp.int32, (block_rows, 2 * HEAD_DIM), 1) < HEAD_DIM
        lanes = lax.broadcasted_iota(jnp.int32, (block_rows, lse_v.shape[1]), 1)
        live = lax.broadcasted_iota(jnp.int32, (1, 2 * tokens), 1) < length

        def pair_step(step, carry):
            pair, part = lax.div(step, tokens // block_rows), lax.rem(step, tokens // block_rows)
            wide = pl.ds(pl.multiple_of(pair * 2 * HEAD_DIM, 2 * HEAD_DIM), 2 * HEAD_DIM)
            spot = pl.ds(pl.multiple_of(part * block_rows, block_rows), block_rows)
            k_pair, v_pair = k_v[tt, :, wide], v_v[tt, :, wide]
            q_pair = q_v[tt, spot, wide]
            outs = []
            for head in range(2):
                q_one = jnp.where(low if head == 0 else jnp.logical_not(low), q_pair, 0).astype(BF)
                scores = lax.dot_general(
                    q_one, k_pair, (((1,), (1,)), ((), ())), preferred_element_type=F32
                )
                scores = jnp.where(live, scores, -1000000000.0)
                summit = jnp.max(scores, axis=-1, keepdims=True)
                raised = jnp.exp(scores - summit)
                total = jnp.sum(raised, axis=-1, keepdims=True)
                out = jnp.dot(raised.astype(BF), v_pair, preferred_element_type=F32)
                outs.append(out / total)
                number = tt * (group // HEAD_DIM) + pair * 2 + head
                lse_v[spot] = jnp.where(lanes == number, summit + jnp.log(total), lse_v[spot])
            rms[2, tt, spot, pl.ds(pl.multiple_of(3 * group + pair * 2 * HEAD_DIM, 2 * HEAD_DIM), 2 * HEAD_DIM)] = jnp.where(low, outs[0], outs[1]).astype(BF)
            return carry

        lax.fori_loop(0, (group // (2 * HEAD_DIM)) * (tokens // block_rows), pair_step, 0)
        for n in range(width // 256):
            acc[:, n * 256 : (n + 1) * 256] += lax.dot_general(
                rms[2, tt, :, 3 * group :],
                wbuf[slot, n * 256 : (n + 1) * 256, 3 * group :],
                (((1,), (1,)), ((), ())),
                preferred_element_type=F32,
            )

    chunk = 64

    def norm(which, keep):
        gain, shift = vec_ref[2 + 2 * which : 3 + 2 * which], vec_ref[3 + 2 * which : 4 + 2 * which]

        def one(step, carry):
            spot = pl.ds(pl.multiple_of(step * chunk, chunk), chunk)
            value = acc[spot]
            center = value - jnp.mean(value, axis=-1, keepdims=True)
            spread = jnp.mean(center * center, axis=-1, keepdims=True)
            inverse = lax.rsqrt(spread + 1e-05)
            unit = center * inverse
            rstd_v[which, spot] = jnp.broadcast_to(inverse, (chunk, rstd_v.shape[2]))
            keep(spot, unit, unit * gain + shift)
            return carry

        lax.fori_loop(0, tokens // chunk, one, 0)

    def keep_one(spot, unit, hidden):
        n1_v[spot] = unit.astype(BF)
        outbox[1, spot] = hidden.astype(BF)
        acc[spot] = hidden + vec_ref[1:2]

    def keep_two(spot, unit, hidden):
        n2_v[spot] = unit.astype(BF)
        y_v[spot] = hidden.astype(BF)

    def turn_rows(source, which):
        flat = jnp.transpose(source)
        for dev in range(n_dp):
            lts[which, dev % 2, (dev // 2) * rows : (dev // 2 + 1) * rows] = flat[
                dev * rows : (dev + 1) * rows
            ]

    def expand(index):
        _, tt = at(index)
        slot = lax.rem(index, 2)

        def one(n, carry):
            wide = pl.ds(pl.multiple_of(n * 256, 256), 256)
            u = jnp.dot(outbox[1], wbuf[slot, :, wide], preferred_element_type=F32)
            u = u + bias_v[tt, pl.ds(2 + n, 1)]
            bell, below = gauss(u)
            rms[0, tt, :, wide] = (u * below).astype(BF)
            rms[1, tt, :, wide] = (below + u * bell).astype(BF)
            return carry

        lax.fori_loop(0, units // 256, one, 0)

    def contract(index):
        _, tt = at(index)
        slot = lax.rem(index, 2)

        def one(n, carry):
            wide = pl.ds(pl.multiple_of(n * 256, 256), 256)
            acc[:, wide] += lax.dot_general(
                rms[0, tt], wbuf[slot, wide, :], (((1,), (1,)), ((), ())), preferred_element_type=F32
            )
            return carry

        lax.fori_loop(0, width // 256, one, 0, unroll=True)

    landed(shard_ref.at[0], own_sem.at[0])
    relay(jnp.int32(0))
    start_biases()
    for k in range(KINDS):
        if k:
            landed(shard_ref.at[0], own_sem.at[k])
        for half in range(2):
            forward(k, t, half, 0)
    def tokens_here():
        for s in range(2):
            landed(x_ref.at[s], x_r.at[s])
        for step in range(n_tensor):
            landed(bias_ref, bz_r.at[step])
        acc[...] = outbox[0].astype(F32) + vec_ref[0:1]
        turn_rows(outbox[0], 2)
        lse_v[...] = jnp.zeros_like(lse_v)

    def turn(index, carry):
        comm_step(index)
        done = index - LAG

        @pl.when(index == X_START)
        def _():
            start_tokens()

        @pl.when(done == 2)
        def _():
            tokens_here()

        @pl.when((done >= 3) & (done <= 6))
        def _():
            attend(done - 3)

        @pl.when((done >= 2) & (done <= 5))
        def _():
            load(done - 2)
            project(done - 2)

        @pl.when(index == COT_ONE)
        def _():
            cot_first()

        @pl.when(index == COT_TWO)
        def _():
            cot_second()

        @pl.when(done == 6)
        def _():
            norm(0, keep_one)
            turn_rows(outbox[1], 1)
            lse_rows[...] = jnp.transpose(lse_v[...])

        def up(step, carry):
            load(step)
            expand(step)
            return carry

        def down(step, carry):
            load(step)
            contract(step)
            return carry

        lax.fori_loop(
            jnp.where(done == 8, 6, 4), jnp.where(done == 7, 6, jnp.where(done == 8, 8, 4)), up, 0
        )
        lax.fori_loop(
            jnp.where(done == 9, 8, jnp.where(done > 9, done, 8)),
            jnp.where(done == 9, 10, jnp.where(done > 9, done + 1, 8)),
            down,
            0,
        )
        return carry

    lax.fori_loop(0, pieces + LAG, turn, 0)
    norm(1, keep_two)

    def rat(step):
        near = jnp.where(step < 2, flip(t, 0), t)
        return jnp.where((step == 1) | (step == 2), flip(near, 1), near)

    def weights(k, step, slot):
        return pltpu.make_async_copy(full_ref.at[k, rat(step)], wbuf.at[slot], w_sem.at[slot])

    def send_output(a, source):
        for q in range(2):
            send_or_keep(
                (lax.div(t, half_t) == core) & (2 * core + q == t),
                source.at[pl.ds(q * span, span)],
                y_out.at[a, lax.rem(t, half_t)],
                y_s.at[a, q],
                y_r.at[a, lax.rem(t, half_t)],
                (2 * chip + lax.div(t, half_t), 2 * core + q),
            )


    def kind_of(index):
        return KINDS - 1 - lax.div(index, n_tensor)

    def emit(index):
        order = lax.div(index, n_tensor)
        tt = rat(lax.rem(index, n_tensor))
        slot, box = lax.rem(index, SLOTS), lax.rem(index, 2)

        @pl.when(index >= 2)
        def _():
            landed(outbox.at[0], core_s.at[index - 2])

        def one(n, carry):
            wide = pl.ds(pl.multiple_of(n * group, group), group)
            left = order + jnp.where((order == 2) & (n == 3), 1, 0)
            right = rms[order, tt, :, wide]
            outbox[box, :, wide] = jnp.dot(
                lts[left, 1 - core], right, preferred_element_type=F32
            ).astype(BF)
            return carry

        lax.fori_loop(0, cols // group, one, 0, unroll=True)
        remote(
            outbox.at[box], from_core.at[lax.rem(index, 4)], core_s.at[index], core_r.at[index], sibling
        ).start()

    def spot_of(code, order):
        return pl.ds(pl.multiple_of(relative(chip, order, code) * rows, rows), rows)

    def pass_on(index, s):
        slot = lax.rem(index, SLOTS)
        for half in range(2):
            order = orders(bits)[half]
            for code in range(1 << s, 2 << s):
                remote(
                    held.at[slot, spot_of(code, order), pl.ds(half * half_cols, half_cols)],
                    from_chip.at[slot, half, code - 1],
                    xy_s.at[index, half],
                    xy_r.at[index, half, code],
                    (2 * flip(chip, order[s]) + core, t),
                ).start()

    def take_in(index, s):
        slot = lax.rem(index, SLOTS)
        for half in range(2):
            order = orders(bits)[half]
            for code in range(1 << s, 2 << s):
                landed(from_chip.at[0, 0, 0], xy_r.at[index, half, code])
                spot = spot_of(code - (1 << s), order)
                wide = pl.ds(half * half_cols, half_cols)
                held[slot, spot, wide] = (
                    held[slot, spot, wide].astype(F32)
                    + from_chip[slot, half, code - 1].astype(F32)
                ).astype(BF)

    def first(index):
        slot = lax.rem(index, SLOTS)
        @pl.when(index >= SLOTS)
        def _():
            for half in range(2):
                landed(from_chip.at[0, 0], xy_s.at[index - SLOTS, half])

            @pl.when(lax.rem(index - SLOTS, n_tensor) < n_tensor - 1)
            def _():
                landed(from_z.at[0, 0], z_s.at[index - SLOTS])

        landed(outbox.at[0], core_r.at[index])
        order = lax.div(index, n_tensor)
        tt = rat(lax.rem(index, n_tensor))

        def one(n, carry):
            wide = pl.ds(pl.multiple_of(n * group, group), group)
            left = order + jnp.where((order == 2) & (n == 3), 1, 0)
            held[slot, :, wide] = (
                jnp.dot(lts[left, core], rms[order, tt, :, wide], preferred_element_type=F32)
                + from_core[lax.rem(index, 4), :, wide].astype(F32)
            ).astype(BF)
            return carry

        lax.fori_loop(0, cols // group, one, 0, unroll=True)
        if bits:
            pass_on(index, bits - 1)

    def finish(index):
        slot, step = lax.rem(index, SLOTS), lax.rem(index, n_tensor)
        source = pl.ds(pl.multiple_of(chip * rows, rows), rows)

        k = kind_of(index)

        @pl.when(step >= 2)
        def _():
            given = 3 - step
            landed(from_z.at[0, 0], z_r.at[index - step + given])
            held[slot, source] = (
                held[slot, source].astype(F32) + from_z[k, given].astype(F32)
            ).astype(BF)

        @pl.when(step == n_tensor - 1)
        def _():
            from_z[k, step] = held[slot, source]

        @pl.when(step < n_tensor - 1)
        def _():
            remote(
                held.at[slot, source],
                from_z.at[k, step],
                z_s.at[index],
                z_r.at[index],
                (d, jnp.where(step < 2, flip(t, 0), flip(t, 1))),
            ).start()

    def advance(index):
        @pl.when(index < pieces)
        def _():
            emit(index)

        for stage in range(bits + 1):
            earlier = index - 1 - stage - (DEEP if stage else 0)

            @pl.when((earlier >= 0) & (earlier < pieces))
            def _(stage=stage, earlier=earlier):
                if stage == 0:
                    first(earlier)
                else:
                    take_in(earlier, bits - stage)
                    if stage < bits:
                        pass_on(earlier, bits - stage - 1)
                if stage == bits:
                    finish(earlier)

    def keep_small(which, row):
        for r in range(8):
            small_v[which, r : r + 1] = row[:, r * 128 : (r + 1) * 128]

    def norm_back(which, unit_ref, incoming, low_ref):
        gain = vec_ref[2 + 2 * which : 3 + 2 * which]

        def one(step, carry):
            spot = pl.ds(pl.multiple_of(step * chunk, chunk), chunk)
            e = incoming(step, spot)
            unit = unit_ref[spot].astype(F32)
            ge = e * gain
            first_mean = jnp.mean(ge, axis=-1, keepdims=True)
            second_mean = jnp.mean(ge * unit, axis=-1, keepdims=True)
            grad = (ge - first_mean - unit * second_mean) * rstd_v[which, spot, 0:1]
            acc[spot] = grad
            low = grad.astype(BF)
            low_ref[spot] = low
            return (
                carry[0] + jnp.sum(e * unit, axis=0, keepdims=True),
                carry[1] + jnp.sum(e, axis=0, keepdims=True),
                carry[2] + jnp.sum(low.astype(F32), axis=0, keepdims=True),
            )

        zero = jnp.zeros((1, width), F32)
        return lax.fori_loop(0, tokens // chunk, one, (zero, zero, zero))

    for q in range(half_t):
        for who in range(n_dp):
            landed(c_two.at[0], c2_r.at[q, who])
    weights(2, 0, 0).start()
    weights(1, 0, 1).start()
    send_output(0, y_v)

    def seed(step, spot):
        number = core * tokens + step * chunk + lax.broadcasted_iota(jnp.int32, (chunk, 1), 0)
        return jnp.where(number < length, cot_v[spot].astype(F32), 0.0)

    sums = norm_back(1, n2_v, seed, cot_v)
    keep_small(10, sums[0])
    keep_small(11, sums[1])
    keep_small(7, sums[2])
    turn_rows(cot_v[...], 0)
    advance(jnp.int32(0))

    def mlp(step, carry):
        tt = rat(step)
        weights(2, step, 0).wait()

        def one(n, carry):
            wide = pl.ds(pl.multiple_of(n * 256, 256), 256)
            grad = jnp.dot(cot_v[...], wbuf[0, :, wide], preferred_element_type=F32)
            rms[1, tt, :, wide] = (rms[1, tt, :, wide].astype(F32) * grad).astype(BF)
            return carry

        lax.fori_loop(0, cols // 256, one, 0, unroll=True)

        @pl.when(step < n_tensor - 1)
        def _():
            weights(2, step + 1, 0).start()

        @pl.when(step == n_tensor - 1)
        def _():
            weights(0, 0, 0).start()

        total = jnp.sum(rms[1, tt].astype(F32), axis=0, keepdims=True)
        for r in range(8):
            small_v[3 + tt, r : r + 1] = total[:, r * 128 : (r + 1) * 128]
        weights(1, step, 1).wait()

        def two(n, carry):
            wide = pl.ds(pl.multiple_of(n * 256, 256), 256)
            acc[:, wide] += lax.dot_general(
                rms[1, tt], wbuf[1, wide, :], (((1,), (1,)), ((), ())), preferred_element_type=F32
            )
            return carry

        lax.fori_loop(0, width // 256, two, 0, unroll=True)

        @pl.when(step < n_tensor - 1)
        def _():
            weights(1, step + 1, 1).start()

        @pl.when(step == n_tensor - 1)
        def _():
            weights(0, 1, 1).start()

        @pl.when(lax.rem(step, 2) == 1)
        def _():
            advance(1 + lax.div(step, 2))

        return carry

    lax.fori_loop(0, n_tensor, mlp, 0)

    sums = norm_back(0, n1_v, lambda step, spot: acc[spot], n2_v)
    keep_small(8, sums[0])
    keep_small(9, sums[1])
    keep_small(2, sums[2])
    turn_rows(n2_v[...], 3)

    key_rows = min(256, 2 * tokens)
    low_lanes = lax.broadcasted_iota(jnp.int32, (tokens, 2 * HEAD_DIM), 1) < HEAD_DIM

    def prepare(step):
        tt, slot = rat(step), lax.rem(step, 2)
        weights(0, step, slot).wait()
        grad = jnp.dot(
            n2_v[...], wbuf[slot, :, 3 * group :], preferred_element_type=F32
        ).astype(BF)
        mix_grad[...] = grad
        both = grad.astype(F32) * rms[2, tt, :, 3 * group :].astype(F32)
        high = both.astype(BF)
        rest = (both - high.astype(F32)).astype(BF)
        heads = lax.broadcasted_iota(jnp.int32, (8, group), 0)
        lanes = lax.broadcasted_iota(jnp.int32, (8, group), 1)
        picks = jnp.where(lax.div(lanes, HEAD_DIM) == heads, 1.0, 0.0).astype(BF)
        dims = (((1,), (1,)), ((), ()))
        delta_v[...] = lax.dot_general(
            picks, high, dims, preferred_element_type=F32
        ) + lax.dot_general(picks, rest, dims, preferred_element_type=F32)

        @pl.when(step >= 2)
        def _():
            for j in range(2):
                landed(dkv_in.at[0, 0], dkv_s.at[step - 2, j])

    def pair_back(step, pair):
        tt, slot = rat(step), lax.rem(step, 2)
        wide = pl.ds(pl.multiple_of(pair * 2 * HEAD_DIM, 2 * HEAD_DIM), 2 * HEAD_DIM)
        q_pair, o_pair = q_v[tt, :, wide], mix_grad[:, wide]
        q_ones = [jnp.where(low_lanes, q_pair, 0).astype(BF), jnp.where(low_lanes, 0, q_pair).astype(BF)]
        o_ones = [jnp.where(low_lanes, o_pair, 0).astype(BF), jnp.where(low_lanes, 0, o_pair).astype(BF)]
        kt_v[...] = jnp.transpose(k_v[tt, :, wide])
        dqt_v[...] = jnp.zeros_like(dqt_v)
        dims = (((1,), (1,)), ((), ()))

        def block(b, carry):
            spot = pl.ds(pl.multiple_of(b * key_rows, key_rows), key_rows)
            k_part, v_part = k_v[tt, spot, wide], v_v[tt, spot, wide]
            number = b * key_rows + lax.broadcasted_iota(jnp.int32, (key_rows, 1), 0)
            live = number < length
            dv, dk = None, None
            for head in range(2):
                which = tt * (group // HEAD_DIM) + pair * 2 + head
                scores = lax.dot_general(k_part, q_ones[head], dims, preferred_element_type=F32)
                probs = jnp.where(live, jnp.exp(scores - lse_rows[pl.ds(which, 1)]), 0.0)
                prob_grad = lax.dot_general(v_part, o_ones[head], dims, preferred_element_type=F32)
                score_grad = (probs * (prob_grad - delta_v[pl.ds(pair * 2 + head, 1)])).astype(BF)
                one_v = jnp.dot(probs.astype(BF), o_ones[head], preferred_element_type=F32)
                one_k = jnp.dot(score_grad, q_ones[head], preferred_element_type=F32)
                dv = one_v if dv is None else dv + one_v
                dk = one_k if dk is None else dk + one_k
                rows_here = slice(head * HEAD_DIM, (head + 1) * HEAD_DIM)
                dqt_v[rows_here] += jnp.dot(
                    kt_v[rows_here, spot], score_grad, preferred_element_type=F32
                )
            dkv_v[slot, 0, spot, wide] = dk.astype(BF)
            dkv_v[slot, 1, spot, wide] = dv.astype(BF)
            return carry

        lax.fori_loop(0, 2 * tokens // key_rows, block, 0)
        dq = jnp.transpose(dqt_v[...].astype(BF).astype(F32)) * 0.125
        rms[2, tt, :, wide] = dq.astype(BF)
        total = jnp.sum(dq, axis=0, keepdims=True)
        small_v[0, pl.ds(tt * (group // 128) + pair, 1)] = total

    def exchange(step):
        slot = lax.rem(step, 2)
        for j in range(2):
            remote(
                dkv_v.at[slot, j, others],
                dkv_in.at[step, j],
                dkv_s.at[step, j],
                dkv_r.at[step, j],
                sibling,
            ).start()

    def collect(step):
        tt, slot = rat(step), lax.rem(step, 2)
        for j in range(2):
            landed(dkv_in.at[0, 0], dkv_r.at[step, j])
            value = (
                dkv_v[slot, j, mine].astype(F32) + dkv_in[step, j].astype(F32)
            ).astype(BF)
            rms[2, tt, :, (1 + j) * group : (2 + j) * group] = value
            if j:
                total = jnp.sum(value.astype(F32), axis=0, keepdims=True)
                for r in range(group // 128):
                    small_v[1, pl.ds(tt * (group // 128) + r, 1)] = total[:, r * 128 : (r + 1) * 128]

        def one(n, carry):
            wide = pl.ds(pl.multiple_of(n * 256, 256), 256)
            acc[:, wide] += lax.dot_general(
                rms[2, tt, :, : 3 * group],
                wbuf[slot, wide, : 3 * group],
                (((1,), (1,)), ((), ())),
                preferred_element_type=F32,
            )
            return carry

        lax.fori_loop(0, width // 256, one, 0, unroll=True)

    def run(index, carry):
        advance(index)
        return carry

    def attention(step, carry):
        @pl.when(step < n_tensor)
        def _():
            prepare(step)
            for pair in range(group // (2 * HEAD_DIM)):
                pair_back(step, pair)
                low, high = jnp.int32(0), jnp.int32(0)
                for s, (begin, end) in enumerate(PLAN[pair]):
                    low, high = jnp.where(step == s, begin, low), jnp.where(step == s, end, high)
                lax.fori_loop(low, high, run, 0)

            exchange(step)

        @pl.when(step >= 1)
        def _():
            collect(step - 1)

            @pl.when(step < n_tensor - 1)
            def _():
                weights(0, step + 1, lax.rem(step + 1, 2)).start()

        return carry

    lax.fori_loop(0, n_tensor + 1, attention, 0)

    cot_v[...] = acc[...].astype(BF)
    send_output(1, cot_v)
    for j in range(SMALL):
        send_or_keep(
            me == j,
            small_v.at[j],
            small_in.at[me],
            b_s.at[j],
            b_r.at[me],
            (j // n_tensor, j % n_tensor),
        )
    def drain(index, carry):
        advance(index)
        return carry

    lax.fori_loop(LAST, pieces, drain, 0)

    @pl.when(me < SMALL)
    def _():
        def arrive(step, total):
            landed(small_in.at[0], b_r.at[step])
            return total + small_in[step]

        total = lax.fori_loop(0, count, arrive, jnp.zeros(small_in.shape[1:], F32))
        small_in[0] = total
        pltpu.make_async_copy(small_in.at[0], small_out.at[me], bo_r.at[me]).start()

        def spread(step, carry):
            other = lax.rem(me + step, count)
            remote(
                small_in.at[0],
                small_out.at[me],
                bo_s.at[step],
                bo_r.at[me],
                (lax.div(other, n_tensor), lax.rem(other, n_tensor)),
            ).start()
            return carry

        lax.fori_loop(1, count, spread, 0)

    lax.fori_loop(pieces, pieces + 1 + bits + DEEP, drain, 0)

    for k in range(KINDS):
        total = from_z[k, n_tensor - 1].astype(F32)
        landed(from_z.at[0, 0], z_r.at[(KINDS - 1 - k) * n_tensor + 2])
        total = total + from_z[k, 2].astype(F32)
        acc[k * rows : (k + 1) * rows] = total
        pltpu.make_async_copy(acc.at[pl.ds(k * rows, rows)], sum_ref.at[k], out_sem.at[k]).start()
    for k in range(KINDS):
        landed(acc.at[pl.ds(0, rows)], out_sem.at[k])

    for k in range(KINDS):
        for tt in range(n_tensor):
            relayed(k, tt)
            for half in range(2):
                half_rows = full_ref.at[k, tt, pl.ds(0, width // 2), pl.ds(0, half_cols)]
                landed(half_rows, sib_s.at[k, tt, half])
                if chips > 1:
                    most = full_ref.at[k, tt, pl.ds(0, width // 2 - rows), pl.ds(0, half_cols)]
                    landed(most, gxy_s.at[k, tt, half])
    for s in range(2):
        sent((lax.div(t, half_t) == core) & (2 * core + s == t), x_ref.at[s], x_s.at[s])
    for step in range(1, n_tensor):
        landed(bias_ref, bz_s.at[step])
    for tt in range(n_tensor):
        for j in range(2):
            landed(q_v.at[tt], kv_s.at[tt, j])
    for step in range(1, n_dp):
        landed(c_one.at[0], c1_s.at[step])
    for step in range(2 * n_dp):
        seq = lax.rem(4 * chip + step, 2 * n_dp)
        goal = 2 * lax.div(seq, 4) + lax.div(t, half_t)
        sent((goal == d) & (lax.rem(seq, 4) == t), c_two.at[0], c2_s.at[step])
    for j in range(SMALL):
        landed(small_v.at[0], bo_r.at[j])
        sent(me == j, small_v.at[0], b_s.at[j])

    @pl.when(me < SMALL)
    def _():
        def gone(step, carry):
            landed(small_v.at[0], bo_s.at[step])
            return carry

        lax.fori_loop(1, count, gone, 0)

    for a in range(2):
        for q in range(2):
            sent((lax.div(t, half_t) == core) & (2 * core + q == t), x_ref.at[q], y_s.at[a, q])
            landed(x_ref.at[q], y_r.at[a, q])
    for step in range(n_tensor - 2, n_tensor):
        for j in range(2):
            landed(dkv_in.at[0, 0], dkv_s.at[step, j])
    for index in range(pieces - 2, pieces):
        landed(outbox.at[0], core_s.at[index])
    for index in range(pieces - SLOTS, pieces):
        for half in range(2):
            landed(from_chip.at[0, 0], xy_s.at[index, half])
        if index % n_tensor < n_tensor - 1:
            landed(from_z.at[0, 0], z_s.at[index])


def gauss(u):
    size = jnp.abs(u)
    bell = 0.3989422804014327 * jnp.exp(-0.5 * (u * u))
    s = 1.0 / (1.0 + 0.23164190 * size)
    tail = bell * s * (
        0.319381530 + s * (-0.356563782 + s * (1.781477937 + s * (-1.821255978 + s * 1.330274429)))
    )
    return bell, jnp.where(u < 0, tail, 1.0 - tail)


def run_layer(n_dp, n_tensor, undealing, lengths, vecs, x_in, cot_in, shard, biases):
    slots, span, width = x_in.shape
    rows, cols = shard.shape[1:]
    chips = n_dp // 2
    tokens = 2 * span
    group = cols // 4
    n_pos = min(n_dp, span // 16)
    prow, pcol = span // n_pos, width // (n_dp // n_pos)
    pieces = KINDS * n_tensor
    count = n_dp * n_tensor
    dma = pltpu.SemaphoreType.DMA
    any_space = pl.BlockSpec(memory_space=pl.ANY)
    smem = pl.BlockSpec(memory_space=pltpu.SMEM)
    vmem = pl.BlockSpec(memory_space=pltpu.VMEM)
    shapes = (
        ((KINDS, n_tensor, width, cols), BF),
        ((KINDS, rows, cols), F32),
        ((SMALL, 8, 128), F32),
        ((2, 2, span, width), BF),
    )
    return pl.pallas_call(
        functools.partial(layer_kernel, n_dp, n_tensor),
        out_shape=tuple(jax.ShapeDtypeStruct(*shape) for shape in shapes),
        in_specs=[smem, smem, vmem, any_space, any_space, vmem, vmem],
        out_specs=(any_space, any_space, any_space, any_space),
        scratch_shapes=[
            pltpu.VMEM((n_dp, slots, prow, pcol), BF),
            pltpu.VMEM((2 * n_dp, prow, pcol), BF),
            pltpu.VMEM((n_tensor,) + biases.shape, F32),
            pltpu.VMEM((2, width, cols), BF),
            pltpu.VMEM((n_tensor, tokens, group), BF),
            pltpu.VMEM((n_tensor, 2 * tokens, group), BF),
            pltpu.VMEM((n_tensor, 2 * tokens, group), BF),
            pltpu.VMEM((4, 2, width // 2, tokens), BF),
            pltpu.VMEM((KINDS, n_tensor, tokens, cols), BF),
            pltpu.VMEM((tokens, width), BF),
            pltpu.VMEM((tokens, width), BF),
            pltpu.VMEM((tokens, width), BF),
            pltpu.VMEM((tokens, width), BF),
            pltpu.VMEM((tokens, width), F32),
            pltpu.VMEM((tokens, 128), F32),
            pltpu.VMEM((128, tokens), F32),
            pltpu.VMEM((2, tokens, 128), F32),
            pltpu.VMEM((tokens, group), BF),
            pltpu.VMEM((8, tokens), F32),
            pltpu.VMEM((2 * HEAD_DIM, tokens), F32),
            pltpu.VMEM((2 * HEAD_DIM, 2 * tokens), BF),
            pltpu.VMEM((2, 2, 2 * tokens, group), BF),
            pltpu.VMEM((n_tensor, 2, tokens, group), BF),
            pltpu.VMEM((2, width // 2, cols), BF),
            pltpu.VMEM((4, width // 2, cols), BF),
            pltpu.VMEM((SLOTS, width // 2, cols), BF),
            pltpu.VMEM((SLOTS, 2, max(chips - 1, 1), rows, cols // 2), BF),
            pltpu.VMEM((KINDS, n_tensor, rows, cols), BF),
            pltpu.VMEM((SMALL, 8, 128), F32),
            pltpu.VMEM((count, 8, 128), F32),
            dma((2,)),
            dma((2,)),
            dma((n_dp,)),
            dma((n_dp,)),
            dma((2 * n_dp,)),
            dma((n_tensor // 2, n_dp)),
            dma((KINDS,)),
            dma((KINDS, n_tensor, 2)),
            dma((KINDS, n_tensor)),
            dma((KINDS, n_tensor, 2)),
            dma((KINDS, n_tensor, 2, chips)),
            dma((KINDS, n_tensor, 2)),
            dma((KINDS, n_tensor, 2, chips)),
            dma((n_tensor, 2)),
            dma((n_tensor, 2)),
            dma((n_tensor,)),
            dma((n_tensor,)),
            dma((2,)),
            dma((n_tensor, 2)),
            dma((n_tensor, 2)),
            dma((2, 2)),
            dma((2, 2)),
            dma((SMALL,)),
            dma((count,)),
            dma((count,)),
            dma((SMALL,)),
            dma((pieces,)),
            dma((pieces,)),
            dma((pieces, 2)),
            dma((pieces, 2, chips)),
            dma((pieces,)),
            dma((pieces,)),
            dma((KINDS,)),
        ],
        compiler_params=pltpu.CompilerParams(
            collective_id=0, has_side_effects=True, vmem_limit_bytes=VMEM_LIMIT
        ),
        name="encoder_layer",
    )(undealing, lengths, vecs, x_in, cot_in, shard, biases)


def shards(
    n_dp,
    n_tensor,
    inputs,
    cotangent,
    lengths,
    dealing,
    undealing,
    query_weight,
    key_weight,
    value_weight,
    output_weight,
    up_weight,
    down_weight,
    query_bias,
    value_bias,
    output_bias,
    up_bias,
    down_bias,
    first_gain,
    first_shift,
    second_gain,
    second_shift,
):
    span, slots, width = inputs.shape
    group = query_weight.shape[1]
    shard = jnp.stack(
        [
            jnp.concatenate([query_weight, key_weight, value_weight, output_weight.T], axis=1),
            up_weight,
            down_weight.T,
        ]
    ).astype(BF)
    blank = jnp.zeros((group,), F32)
    biases = jnp.concatenate([query_bias, value_bias, up_bias, blank, blank]).reshape(8, group)
    vecs = jnp.stack([output_bias, down_bias, first_gain, first_shift, second_gain, second_shift])
    vecs = jnp.pad(vecs, ((0, 2), (0, 0)))
    _, sums, small, returned = run_layer(
        n_dp,
        n_tensor,
        undealing,
        lengths,
        vecs,
        jnp.transpose(inputs, (1, 0, 2)),
        jnp.transpose(cotangent, (1, 0, 2)),
        shard,
        biases,
    )
    returned = jnp.transpose(returned, (0, 2, 1, 3))
    small = small.reshape(SMALL, width)
    t = lax.axis_index("tensor")

    def mine(row):
        return lax.dynamic_slice(small[row], (t * group,), (group,))

    return (
        returned[0],
        returned[1],
        sums[0][:, :group],
        sums[0][:, group : 2 * group],
        sums[0][:, 2 * group : 3 * group],
        sums[0][:, 3 * group :].T,
        sums[1],
        sums[2].T,
        mine(0),
        mine(1),
        small[2],
        lax.dynamic_index_in_dim(small, 3 + t, 0, keepdims=False),
        small[7],
        small[8],
        small[9],
        small[10],
        small[11],
    )


def solution(mesh):
    tokens = P("tensor", "dp", None)
    rows, columns = P("dp", "tensor"), P("tensor", "dp")
    split, copied = P("tensor"), P()
    return jax.shard_map(
        functools.partial(shards, mesh.shape["dp"], mesh.shape["tensor"]),
        mesh=mesh,
        in_specs=(
            (tokens, tokens, copied, copied, copied)
            + (rows, rows, rows, columns, rows, columns)
            + (split, split, copied, split, copied, copied, copied, copied, copied)
        ),
        out_specs=(
            (tokens, tokens, rows, rows, rows, columns, rows, columns)
            + (split, split, copied, split, copied, copied, copied, copied, copied)
        ),
        check_vma=False,
    )
```

```python
import functools

import jax
import jax.numpy as jnp
from jax import lax
from jax.experimental import pallas as pl
from jax.experimental.pallas import tpu as pltpu
from jax.sharding import PartitionSpec as P

HEAD_DIM = 64
KINDS = 3
MESH = pl.DeviceIdType.MESH
VMEM_LIMIT = 63 << 20
BF = jnp.bfloat16
F32 = jnp.float32


def flip(index, bit):
    unit = 1 << bit
    return index + unit * (1 - 2 * lax.rem(lax.div(index, unit), 2))


def orders(bits):
    return (tuple(range(bits)), tuple(reversed(range(bits))))


def relative(chip, order, code):
    for place, bit in enumerate(order):
        if code >> place & 1:
            chip = flip(chip, bit)
    return chip


def place():
    d, t = lax.axis_index("dp"), lax.axis_index("tensor")
    return d, t, lax.div(d, 2), lax.rem(d, 2)


def greet(n_dp, n_tensor):
    d, t, _, _ = place()
    barrier = pltpu.get_barrier_semaphore()
    me = d * n_tensor + t
    count = n_dp * n_tensor

    def one(step, carry):
        other = lax.rem(me + step, count)
        pl.semaphore_signal(
            barrier,
            inc=1,
            device_id=(lax.div(other, n_tensor), lax.rem(other, n_tensor)),
            device_id_type=MESH,
        )
        return carry

    lax.fori_loop(1, count, one, 0)
    pl.semaphore_wait(barrier, count - 1)


def remote(src, dst, ssem, rsem, device):
    return pltpu.make_async_remote_copy(
        src_ref=src,
        dst_ref=dst,
        send_sem=ssem,
        recv_sem=rsem,
        device_id=device,
        device_id_type=MESH,
    )


def landed(ref, sem):
    pltpu.make_async_copy(ref, ref, sem).wait()


def send_or_keep(mine, src, dst, ssem, rsem, device):
    @pl.when(mine)
    def _():
        pltpu.make_async_copy(src, dst, rsem).start()

    @pl.when(jnp.logical_not(mine))
    def _():
        remote(src, dst, ssem, rsem, device).start()


def sent(mine, src, ssem):
    @pl.when(jnp.logical_not(mine))
    def _():
        landed(src, ssem)


LAG = 2
SMALL = 12
SLOTS = 6
DEEP = 0
PLAN = (((4, 4), (5, 5), (6, 7), (8, 9)), ((4, 5), (5, 6), (7, 8), (9, 10)))
LAST = 10
COT_ONE, COT_TWO, X_START = 4, 9, 0


def layer_kernel(
    n_dp,
    n_tensor,
    undealing,
    lengths,
    vec_ref,
    x_ref,
    cot_ref,
    shard_ref,
    bias_ref,
    full_ref,
    sum_ref,
    small_out,
    y_out,
    c_one,
    c_two,
    bias_v,
    wbuf,
    q_v,
    k_v,
    v_v,
    lts,
    rms,
    n1_v,
    n2_v,
    cot_v,
    y_v,
    acc,
    lse_v,
    lse_rows,
    rstd_v,
    mix_grad,
    delta_v,
    dqt_v,
    kt_v,
    dkv_v,
    dkv_in,
    outbox,
    from_core,
    held,
    from_chip,
    from_z,
    small_v,
    small_in,
    x_s,
    x_r,
    c1_s,
    c1_r,
    c2_s,
    c2_r,
    own_sem,
    gz_s,
    gz_r,
    gxy_s,
    gxy_r,
    sib_s,
    sib_r,
    kv_s,
    kv_r,
    bz_s,
    bz_r,
    w_sem,
    dkv_s,
    dkv_r,
    y_s,
    y_r,
    b_s,
    b_r,
    bo_s,
    bo_r,
    core_s,
    core_r,
    xy_s,
    xy_r,
    z_s,
    z_r,
    out_sem,
):
    d, t, chip, core = place()
    chips = n_dp // 2
    bits = chips.bit_length() - 1
    half_t = n_tensor // 2
    count = n_dp * n_tensor
    me = d * n_tensor + t
    rows, cols = shard_ref.shape[1:]
    half_cols = cols // 2
    group = q_v.shape[2]
    span, width = x_ref.shape[1:]
    half_width = width // 2
    tokens = 2 * span
    units = cols
    prow, pcol = c_one.shape[2:]
    n_col = width // pcol
    pieces = KINDS * n_tensor
    sibling = (d + 1 - 2 * core, t)
    length = lengths[4 * chip + t]
    mine = pl.ds(pl.multiple_of(core * tokens, tokens), tokens)
    others = pl.ds(pl.multiple_of((1 - core) * tokens, tokens), tokens)
    greet(n_dp, n_tensor)

    def block(k, tt, who, half):
        return full_ref.at[
            k,
            tt,
            pl.ds(pl.multiple_of((2 * who + core) * rows, rows), rows),
            pl.ds(half * half_cols, half_cols),
        ]

    def arriving(index):
        rest, others = index - KINDS, n_tensor - 1
        return jnp.where(
            index < KINDS,
            index * n_tensor,
            lax.div(rest, others) * n_tensor + 1 + lax.rem(rest, others),
        )

    def stripe(k, tt):
        return full_ref.at[k, tt, pl.ds(pl.multiple_of(d * rows, rows), rows)]

    def at(index):
        step = lax.rem(index, n_tensor)
        near = jnp.where(t < half_t, t, n_tensor - 1 - t)
        spot = jnp.where(step <= near, near - step, step)
        return lax.div(index, n_tensor), jnp.where(t < half_t, spot, n_tensor - 1 - spot)

    for k in range(KINDS):
        pltpu.make_async_copy(shard_ref.at[k], stripe(k, t), own_sem.at[k]).start()

    def relay(index):
        k, tt = at(index)

        @pl.when(tt != t)
        def _():
            landed(shard_ref.at[0], gz_r.at[k, tt])

        for way, wanted in ((1, (tt <= t) & (t < n_tensor - 1)), (0, (tt >= t) & (t > 0))):

            @pl.when(wanted)
            def _(way=way):
                remote(
                    stripe(k, tt),
                    stripe(k, tt),
                    gz_s.at[k, tt, way],
                    gz_r.at[k, tt],
                    (d, t + 2 * way - 1),
                ).start()

    def relayed(k, tt):
        for way, wanted in ((1, (tt <= t) & (t < n_tensor - 1)), (0, (tt >= t) & (t > 0))):

            @pl.when(wanted)
            def _(way=way):
                landed(shard_ref.at[0], gz_s.at[k, tt, way])

    def start_tokens():
        for s in range(2):
            send_or_keep(
                (lax.div(t, half_t) == core) & (2 * core + s == t),
                x_ref.at[s],
                outbox.at[0, pl.ds(pl.multiple_of(lax.rem(t, half_t) * span, span), span)],
                x_s.at[s],
                x_r.at[lax.rem(t, half_t)],
                (2 * chip + lax.div(t, half_t), 2 * core + s),
            )

    def start_biases():
        pltpu.make_async_copy(bias_ref, bias_v.at[t], bz_r.at[0]).start()
        for step in range(1, n_tensor):
            remote(
                bias_ref,
                bias_v.at[t],
                bz_s.at[step],
                bz_r.at[step],
                (d, lax.rem(t + step, n_tensor)),
            ).start()

    def piece(who):
        return cot_ref.at[
            :,
            pl.ds(pl.multiple_of(lax.div(who, n_col) * prow, prow), prow),
            pl.ds(pl.multiple_of(lax.rem(who, n_col) * pcol, pcol), pcol),
        ]

    def cot_first():
        pltpu.make_async_copy(piece(d), c_one.at[d], c1_r.at[0]).start()
        for step in range(1, n_dp):
            who = lax.rem(d + step, n_dp)
            remote(piece(who), c_one.at[d], c1_s.at[step], c1_r.at[step], (who, t)).start()

    def cot_second():
        for step in range(n_dp):
            landed(c_one.at[0], c1_r.at[step])
        count = 2 * n_dp
        for step in range(count):
            seq = lax.rem(4 * chip + step, count)
            slot = undealing[seq]
            c_two[seq] = c_one[lax.div(slot, 2), lax.rem(slot, 2)]
            goal = 2 * lax.div(seq, 4) + lax.div(t, half_t)
            send_or_keep(
                (goal == d) & (lax.rem(seq, 4) == t),
                c_two.at[seq],
                cot_v.at[
                    pl.ds(
                        pl.multiple_of(lax.rem(t, half_t) * span + lax.div(d, n_col) * prow, prow),
                        prow,
                    ),
                    pl.ds(pl.multiple_of(lax.rem(d, n_col) * pcol, pcol), pcol),
                ],
                c2_s.at[step],
                c2_r.at[lax.rem(t, half_t), d],
                (goal, lax.rem(seq, 4)),
            )

    def forward(k, tt, half, code):
        order = orders(bits)[half]
        ref = block(k, tt, relative(chip, order, code), half)
        for s in range(code.bit_length(), bits):
            target = code | 1 << s
            remote(
                ref,
                ref,
                gxy_s.at[k, tt, half],
                gxy_r.at[k, tt, half, target],
                (2 * flip(chip, order[s]) + core, t),
            ).start()
        remote(
            ref, ref, sib_s.at[k, tt, half], sib_r.at[k, tt, half, code], sibling
        ).start()

    def receive(index, codes):
        k, tt = at(arriving(index))
        for code in codes:
            for half in range(2):
                landed(block(k, tt, chip, half), gxy_r.at[k, tt, half, code])
                forward(k, tt, half, code)

    early, late = range(1, max(chips // 2, 1)), range(max(chips // 2, 1), chips)

    def comm_step(index):
        @pl.when((index + 2 >= KINDS) & (index + 2 < pieces))
        def _():
            k, tt = at(arriving(index + 2))
            for half in range(2):
                forward(k, tt, half, 0)

        @pl.when(index < pieces)
        def _():
            receive(index, early)

        @pl.when(index >= LAG)
        def _():
            receive(index - LAG, late)

        follow = index + KINDS
        others = n_tensor - 1

        @pl.when(follow < pieces)
        def _():
            relay(arriving(follow))

            @pl.when((lax.rem(index, others) == others - 1) & (follow + 1 < pieces))
            def _():
                relay(lax.div(index, others) * n_tensor + n_tensor)

    def load(index):
        k, tt = at(index)
        slot = lax.rem(index, 2)
        for half in range(2):
            for code in range(chips):
                landed(block(k, tt, chip, half), sib_r.at[k, tt, half, code])
        copy = pltpu.make_async_copy(full_ref.at[k, tt], wbuf.at[slot], w_sem.at[slot])
        copy.start()
        copy.wait()

    def project(index):
        _, tt = at(index)
        slot = lax.rem(index, 2)
        x = outbox[0]
        for c in range(3):
            out = jnp.dot(
                x, wbuf[slot, :, c * group : (c + 1) * group], preferred_element_type=F32
            )
            if c == 0:
                q_v[tt] = ((out + bias_v[tt, 0:1]) * 0.125).astype(BF)
            elif c == 1:
                k_v[tt, mine] = out.astype(BF)
            else:
                v_v[tt, mine] = (out + bias_v[tt, 1:2]).astype(BF)
        for j, ref in enumerate((k_v, v_v)):
            remote(
                ref.at[tt, mine], ref.at[tt, mine], kv_s.at[tt, j], kv_r.at[tt, j], sibling
            ).start()

    def attend(index):
        _, tt = at(index)
        slot = lax.rem(index, 2)
        for j, ref in enumerate((k_v, v_v)):
            landed(ref.at[tt, mine], kv_r.at[tt, j])
        block_rows = min(256, tokens)
        low = lax.broadcasted_iota(jnp.int32, (block_rows, 2 * HEAD_DIM), 1) < HEAD_DIM
        lanes = lax.broadcasted_iota(jnp.int32, (block_rows, lse_v.shape[1]), 1)
        live = lax.broadcasted_iota(jnp.int32, (1, 2 * tokens), 1) < length

        def pair_step(step, carry):
            pair, part = lax.div(step, tokens // block_rows), lax.rem(step, tokens // block_rows)
            wide = pl.ds(pl.multiple_of(pair * 2 * HEAD_DIM, 2 * HEAD_DIM), 2 * HEAD_DIM)
            spot = pl.ds(pl.multiple_of(part * block_rows, block_rows), block_rows)
            k_pair, v_pair = k_v[tt, :, wide], v_v[tt, :, wide]
            q_pair = q_v[tt, spot, wide]
            outs = []
            for head in range(2):
                q_one = jnp.where(low if head == 0 else jnp.logical_not(low), q_pair, 0).astype(BF)
                scores = lax.dot_general(
                    q_one, k_pair, (((1,), (1,)), ((), ())), preferred_element_type=F32
                )
                scores = jnp.where(live, scores, -1000000000.0)
                summit = jnp.max(scores, axis=-1, keepdims=True)
                raised = jnp.exp(scores - summit)
                total = jnp.sum(raised, axis=-1, keepdims=True)
                out = jnp.dot(raised.astype(BF), v_pair, preferred_element_type=F32)
                outs.append(out / total)
                number = tt * (group // HEAD_DIM) + pair * 2 + head
                lse_v[spot] = jnp.where(lanes == number, summit + jnp.log(total), lse_v[spot])
            rms[2, tt, spot, pl.ds(pl.multiple_of(3 * group + pair * 2 * HEAD_DIM, 2 * HEAD_DIM), 2 * HEAD_DIM)] = jnp.where(low, outs[0], outs[1]).astype(BF)
            return carry

        lax.fori_loop(0, (group // (2 * HEAD_DIM)) * (tokens // block_rows), pair_step, 0)
        for n in range(width // 256):
            acc[:, n * 256 : (n + 1) * 256] += lax.dot_general(
                rms[2, tt, :, 3 * group :],
                wbuf[slot, n * 256 : (n + 1) * 256, 3 * group :],
                (((1,), (1,)), ((), ())),
                preferred_element_type=F32,
            )

    chunk = 64

    def norm(which, keep):
        gain, shift = vec_ref[2 + 2 * which : 3 + 2 * which], vec_ref[3 + 2 * which : 4 + 2 * which]

        def one(step, carry):
            spot = pl.ds(pl.multiple_of(step * chunk, chunk), chunk)
            value = acc[spot]
            center = value - jnp.mean(value, axis=-1, keepdims=True)
            spread = jnp.mean(center * center, axis=-1, keepdims=True)
            inverse = lax.rsqrt(spread + 1e-05)
            unit = center * inverse
            rstd_v[which, spot] = jnp.broadcast_to(inverse, (chunk, rstd_v.shape[2]))
            keep(spot, unit, unit * gain + shift)
            return carry

        lax.fori_loop(0, tokens // chunk, one, 0)

    def keep_one(spot, unit, hidden):
        n1_v[spot] = unit.astype(BF)
        outbox[1, spot] = hidden.astype(BF)
        acc[spot] = hidden + vec_ref[1:2]

    def keep_two(spot, unit, hidden):
        n2_v[spot] = unit.astype(BF)
        y_v[spot] = hidden.astype(BF)

    def turn_rows(source, which):
        flat = jnp.transpose(source)
        for dev in range(n_dp):
            lts[which, dev % 2, (dev // 2) * rows : (dev // 2 + 1) * rows] = flat[
                dev * rows : (dev + 1) * rows
            ]

    def expand(index):
        _, tt = at(index)
        slot = lax.rem(index, 2)

        def one(n, carry):
            wide = pl.ds(pl.multiple_of(n * 256, 256), 256)
            u = jnp.dot(outbox[1], wbuf[slot, :, wide], preferred_element_type=F32)
            u = u + bias_v[tt, pl.ds(2 + n, 1)]
            bell, below = gauss(u)
            rms[0, tt, :, wide] = (u * below).astype(BF)
            rms[1, tt, :, wide] = (below + u * bell).astype(BF)
            return carry

        lax.fori_loop(0, units // 256, one, 0)

    def contract(index):
        _, tt = at(index)
        slot = lax.rem(index, 2)

        def one(n, carry):
            wide = pl.ds(pl.multiple_of(n * 256, 256), 256)
            acc[:, wide] += lax.dot_general(
                rms[0, tt], wbuf[slot, wide, :], (((1,), (1,)), ((), ())), preferred_element_type=F32
            )
            return carry

        lax.fori_loop(0, width // 256, one, 0, unroll=True)

    landed(shard_ref.at[0], own_sem.at[0])
    relay(jnp.int32(0))
    start_biases()
    for k in range(KINDS):
        if k:
            landed(shard_ref.at[0], own_sem.at[k])
        for half in range(2):
            forward(k, t, half, 0)
    def tokens_here():
        for s in range(2):
            landed(x_ref.at[s], x_r.at[s])
        for step in range(n_tensor):
            landed(bias_ref, bz_r.at[step])
        acc[...] = outbox[0].astype(F32) + vec_ref[0:1]
        turn_rows(outbox[0], 2)
        lse_v[...] = jnp.zeros_like(lse_v)

    def turn(index, carry):
        comm_step(index)
        done = index - LAG

        @pl.when(index == X_START)
        def _():
            start_tokens()

        @pl.when(done == 2)
        def _():
            tokens_here()

        @pl.when((done >= 3) & (done <= 6))
        def _():
            attend(done - 3)

        @pl.when((done >= 2) & (done <= 5))
        def _():
            load(done - 2)
            project(done - 2)

        @pl.when(index == COT_ONE)
        def _():
            cot_first()

        @pl.when(index == COT_TWO)
        def _():
            cot_second()

        @pl.when(done == 6)
        def _():
            norm(0, keep_one)
            turn_rows(outbox[1], 1)
            lse_rows[...] = jnp.transpose(lse_v[...])

        def up(step, carry):
            load(step)
            expand(step)
            return carry

        def down(step, carry):
            load(step)
            contract(step)
            return carry

        lax.fori_loop(
            jnp.where(done == 8, 6, 4), jnp.where(done == 7, 6, jnp.where(done == 8, 8, 4)), up, 0
        )
        lax.fori_loop(
            jnp.where(done == 9, 8, jnp.where(done > 9, done, 8)),
            jnp.where(done == 9, 10, jnp.where(done > 9, done + 1, 8)),
            down,
            0,
        )
        return carry

    lax.fori_loop(0, pieces + LAG, turn, 0)
    norm(1, keep_two)

    def rat(step):
        near = jnp.where(step < 2, flip(t, 0), t)
        return jnp.where((step == 1) | (step == 2), flip(near, 1), near)

    def weights(k, step, slot):
        return pltpu.make_async_copy(full_ref.at[k, rat(step)], wbuf.at[slot], w_sem.at[slot])

    def send_output(a, source):
        for q in range(2):
            send_or_keep(
                (lax.div(t, half_t) == core) & (2 * core + q == t),
                source.at[pl.ds(q * span, span)],
                y_out.at[a, lax.rem(t, half_t)],
                y_s.at[a, q],
                y_r.at[a, lax.rem(t, half_t)],
                (2 * chip + lax.div(t, half_t), 2 * core + q),
            )


    def kind_of(index):
        return KINDS - 1 - lax.div(index, n_tensor)

    def emit(index):
        order = lax.div(index, n_tensor)
        tt = rat(lax.rem(index, n_tensor))
        slot, box = lax.rem(index, SLOTS), lax.rem(index, 2)

        @pl.when(index >= 2)
        def _():
            landed(outbox.at[0], core_s.at[index - 2])

        def one(n, carry):
            wide = pl.ds(pl.multiple_of(n * group, group), group)
            left = order + jnp.where((order == 2) & (n == 3), 1, 0)
            right = rms[order, tt, :, wide]
            outbox[box, :, wide] = jnp.dot(
                lts[left, 1 - core], right, preferred_element_type=F32
            ).astype(BF)
            return carry

        lax.fori_loop(0, cols // group, one, 0, unroll=True)
        remote(
            outbox.at[box], from_core.at[lax.rem(index, 4)], core_s.at[index], core_r.at[index], sibling
        ).start()

    def spot_of(code, order):
        return pl.ds(pl.multiple_of(relative(chip, order, code) * rows, rows), rows)

    def pass_on(index, s):
        slot = lax.rem(index, SLOTS)
        for half in range(2):
            order = orders(bits)[half]
            for code in range(1 << s, 2 << s):
                remote(
                    held.at[slot, spot_of(code, order), pl.ds(half * half_cols, half_cols)],
                    from_chip.at[slot, half, code - 1],
                    xy_s.at[index, half],
                    xy_r.at[index, half, code],
                    (2 * flip(chip, order[s]) + core, t),
                ).start()

    def take_in(index, s):
        slot = lax.rem(index, SLOTS)
        for half in range(2):
            order = orders(bits)[half]
            for code in range(1 << s, 2 << s):
                landed(from_chip.at[0, 0, 0], xy_r.at[index, half, code])
                spot = spot_of(code - (1 << s), order)
                wide = pl.ds(half * half_cols, half_cols)
                held[slot, spot, wide] = (
                    held[slot, spot, wide].astype(F32)
                    + from_chip[slot, half, code - 1].astype(F32)
                ).astype(BF)

    def first(index):
        slot = lax.rem(index, SLOTS)
        @pl.when(index >= SLOTS)
        def _():
            for half in range(2):
                landed(from_chip.at[0, 0], xy_s.at[index - SLOTS, half])

            @pl.when(lax.rem(index - SLOTS, n_tensor) < n_tensor - 1)
            def _():
                landed(from_z.at[0, 0], z_s.at[index - SLOTS])

        landed(outbox.at[0], core_r.at[index])
        order = lax.div(index, n_tensor)
        tt = rat(lax.rem(index, n_tensor))

        def one(n, carry):
            wide = pl.ds(pl.multiple_of(n * group, group), group)
            left = order + jnp.where((order == 2) & (n == 3), 1, 0)
            held[slot, :, wide] = (
                jnp.dot(lts[left, core], rms[order, tt, :, wide], preferred_element_type=F32)
                + from_core[lax.rem(index, 4), :, wide].astype(F32)
            ).astype(BF)
            return carry

        lax.fori_loop(0, cols // group, one, 0, unroll=True)
        if bits:
            pass_on(index, bits - 1)

    def finish(index):
        slot, step = lax.rem(index, SLOTS), lax.rem(index, n_tensor)
        source = pl.ds(pl.multiple_of(chip * rows, rows), rows)

        k = kind_of(index)

        @pl.when(step >= 2)
        def _():
            given = 3 - step
            landed(from_z.at[0, 0], z_r.at[index - step + given])
            held[slot, source] = (
                held[slot, source].astype(F32) + from_z[k, given].astype(F32)
            ).astype(BF)

        @pl.when(step == n_tensor - 1)
        def _():
            from_z[k, step] = held[slot, source]

        @pl.when(step < n_tensor - 1)
        def _():
            remote(
                held.at[slot, source],
                from_z.at[k, step],
                z_s.at[index],
                z_r.at[index],
                (d, jnp.where(step < 2, flip(t, 0), flip(t, 1))),
            ).start()

    def advance(index):
        @pl.when(index < pieces)
        def _():
            emit(index)

        for stage in range(bits + 1):
            earlier = index - 1 - stage - (DEEP if stage else 0)

            @pl.when((earlier >= 0) & (earlier < pieces))
            def _(stage=stage, earlier=earlier):
                if stage == 0:
                    first(earlier)
                else:
                    take_in(earlier, bits - stage)
                    if stage < bits:
                        pass_on(earlier, bits - stage - 1)
                if stage == bits:
                    finish(earlier)

    def keep_small(which, row):
        for r in range(8):
            small_v[which, r : r + 1] = row[:, r * 128 : (r + 1) * 128]

    def norm_back(which, unit_ref, incoming, low_ref):
        gain = vec_ref[2 + 2 * which : 3 + 2 * which]

        def one(step, carry):
            spot = pl.ds(pl.multiple_of(step * chunk, chunk), chunk)
            e = incoming(step, spot)
            unit = unit_ref[spot].astype(F32)
            ge = e * gain
            first_mean = jnp.mean(ge, axis=-1, keepdims=True)
            second_mean = jnp.mean(ge * unit, axis=-1, keepdims=True)
            grad = (ge - first_mean - unit * second_mean) * rstd_v[which, spot, 0:1]
            acc[spot] = grad
            low = grad.astype(BF)
            low_ref[spot] = low
            return (
                carry[0] + jnp.sum(e * unit, axis=0, keepdims=True),
                carry[1] + jnp.sum(e, axis=0, keepdims=True),
                carry[2] + jnp.sum(low.astype(F32), axis=0, keepdims=True),
            )

        zero = jnp.zeros((1, width), F32)
        return lax.fori_loop(0, tokens // chunk, one, (zero, zero, zero))

    def run(index, carry):
        advance(index)
        return carry

    for q in range(half_t):
        for who in range(n_dp):
            landed(c_two.at[0], c2_r.at[q, who])
    weights(2, 0, 0).start()
    weights(1, 0, 1).start()
    send_output(0, y_v)

    def seed(step, spot):
        number = core * tokens + step * chunk + lax.broadcasted_iota(jnp.int32, (chunk, 1), 0)
        return jnp.where(number < length, cot_v[spot].astype(F32), 0.0)

    sums = norm_back(1, n2_v, seed, cot_v)
    keep_small(10, sums[0])
    keep_small(11, sums[1])
    keep_small(7, sums[2])
    turn_rows(cot_v[...], 0)
    lax.fori_loop(0, 2, run, 0)

    def mlp(step, carry):
        tt = rat(step)
        weights(2, step, 0).wait()

        def one(n, carry):
            wide = pl.ds(pl.multiple_of(n * 256, 256), 256)
            grad = jnp.dot(cot_v[...], wbuf[0, :, wide], preferred_element_type=F32)
            rms[1, tt, :, wide] = (rms[1, tt, :, wide].astype(F32) * grad).astype(BF)
            return carry

        lax.fori_loop(0, cols // 256, one, 0, unroll=True)

        @pl.when(step < n_tensor - 1)
        def _():
            weights(2, step + 1, 0).start()

        @pl.when(step == n_tensor - 1)
        def _():
            weights(0, 0, 0).start()

        total = jnp.sum(rms[1, tt].astype(F32), axis=0, keepdims=True)
        for r in range(8):
            small_v[3 + tt, r : r + 1] = total[:, r * 128 : (r + 1) * 128]
        weights(1, step, 1).wait()

        def two(n, carry):
            wide = pl.ds(pl.multiple_of(n * 256, 256), 256)
            acc[:, wide] += lax.dot_general(
                rms[1, tt], wbuf[1, wide, :], (((1,), (1,)), ((), ())), preferred_element_type=F32
            )
            return carry

        lax.fori_loop(0, width // 256, two, 0, unroll=True)

        @pl.when(step < n_tensor - 1)
        def _():
            weights(1, step + 1, 1).start()

        @pl.when(step == n_tensor - 1)
        def _():
            weights(0, 1, 1).start()

        @pl.when(lax.rem(step, 2) == 1)
        def _():
            advance(2 + lax.div(step, 2))

        return carry

    lax.fori_loop(0, n_tensor, mlp, 0)

    sums = norm_back(0, n1_v, lambda step, spot: acc[spot], n2_v)
    keep_small(8, sums[0])
    keep_small(9, sums[1])
    keep_small(2, sums[2])
    turn_rows(n2_v[...], 3)

    key_rows = min(256, 2 * tokens)
    low_lanes = lax.broadcasted_iota(jnp.int32, (tokens, 2 * HEAD_DIM), 1) < HEAD_DIM

    def prepare(step):
        tt, slot = rat(step), lax.rem(step, 2)
        weights(0, step, slot).wait()
        grad = jnp.dot(
            n2_v[...], wbuf[slot, :, 3 * group :], preferred_element_type=F32
        ).astype(BF)
        mix_grad[...] = grad
        both = grad.astype(F32) * rms[2, tt, :, 3 * group :].astype(F32)
        high = both.astype(BF)
        rest = (both - high.astype(F32)).astype(BF)
        heads = lax.broadcasted_iota(jnp.int32, (8, group), 0)
        lanes = lax.broadcasted_iota(jnp.int32, (8, group), 1)
        picks = jnp.where(lax.div(lanes, HEAD_DIM) == heads, 1.0, 0.0).astype(BF)
        dims = (((1,), (1,)), ((), ()))
        delta_v[...] = lax.dot_general(
            picks, high, dims, preferred_element_type=F32
        ) + lax.dot_general(picks, rest, dims, preferred_element_type=F32)

        @pl.when(step >= 2)
        def _():
            for j in range(2):
                landed(dkv_in.at[0, 0], dkv_s.at[step - 2, j])

    def pair_back(step, pair):
        tt, slot = rat(step), lax.rem(step, 2)
        wide = pl.ds(pl.multiple_of(pair * 2 * HEAD_DIM, 2 * HEAD_DIM), 2 * HEAD_DIM)
        q_pair, o_pair = q_v[tt, :, wide], mix_grad[:, wide]
        q_ones = [jnp.where(low_lanes, q_pair, 0).astype(BF), jnp.where(low_lanes, 0, q_pair).astype(BF)]
        o_ones = [jnp.where(low_lanes, o_pair, 0).astype(BF), jnp.where(low_lanes, 0, o_pair).astype(BF)]
        kt_v[...] = jnp.transpose(k_v[tt, :, wide])
        dqt_v[...] = jnp.zeros_like(dqt_v)
        dims = (((1,), (1,)), ((), ()))

        def block(b, carry):
            spot = pl.ds(pl.multiple_of(b * key_rows, key_rows), key_rows)
            k_part, v_part = k_v[tt, spot, wide], v_v[tt, spot, wide]
            number = b * key_rows + lax.broadcasted_iota(jnp.int32, (key_rows, 1), 0)
            live = number < length
            dv, dk = None, None
            for head in range(2):
                which = tt * (group // HEAD_DIM) + pair * 2 + head
                scores = lax.dot_general(k_part, q_ones[head], dims, preferred_element_type=F32)
                probs = jnp.where(live, jnp.exp(scores - lse_rows[pl.ds(which, 1)]), 0.0)
                prob_grad = lax.dot_general(v_part, o_ones[head], dims, preferred_element_type=F32)
                score_grad = (probs * (prob_grad - delta_v[pl.ds(pair * 2 + head, 1)])).astype(BF)
                one_v = jnp.dot(probs.astype(BF), o_ones[head], preferred_element_type=F32)
                one_k = jnp.dot(score_grad, q_ones[head], preferred_element_type=F32)
                dv = one_v if dv is None else dv + one_v
                dk = one_k if dk is None else dk + one_k
                rows_here = slice(head * HEAD_DIM, (head + 1) * HEAD_DIM)
                dqt_v[rows_here] += jnp.dot(
                    kt_v[rows_here, spot], score_grad, preferred_element_type=F32
                )
            dkv_v[slot, 0, spot, wide] = dk.astype(BF)
            dkv_v[slot, 1, spot, wide] = dv.astype(BF)
            return carry

        lax.fori_loop(0, 2 * tokens // key_rows, block, 0)
        dq = jnp.transpose(dqt_v[...].astype(BF).astype(F32)) * 0.125
        rms[2, tt, :, wide] = dq.astype(BF)
        total = jnp.sum(dq, axis=0, keepdims=True)
        small_v[0, pl.ds(tt * (group // 128) + pair, 1)] = total

    def exchange(step):
        slot = lax.rem(step, 2)
        for j in range(2):
            remote(
                dkv_v.at[slot, j, others],
                dkv_in.at[step, j],
                dkv_s.at[step, j],
                dkv_r.at[step, j],
                sibling,
            ).start()

    def collect(step):
        tt, slot = rat(step), lax.rem(step, 2)
        for j in range(2):
            landed(dkv_in.at[0, 0], dkv_r.at[step, j])
            value = (
                dkv_v[slot, j, mine].astype(F32) + dkv_in[step, j].astype(F32)
            ).astype(BF)
            rms[2, tt, :, (1 + j) * group : (2 + j) * group] = value
            if j:
                total = jnp.sum(value.astype(F32), axis=0, keepdims=True)
                for r in range(group // 128):
                    small_v[1, pl.ds(tt * (group // 128) + r, 1)] = total[:, r * 128 : (r + 1) * 128]

        def one(n, carry):
            wide = pl.ds(pl.multiple_of(n * 256, 256), 256)
            acc[:, wide] += lax.dot_general(
                rms[2, tt, :, : 3 * group],
                wbuf[slot, wide, : 3 * group],
                (((1,), (1,)), ((), ())),
                preferred_element_type=F32,
            )
            return carry

        lax.fori_loop(0, width // 256, one, 0, unroll=True)

    def attention(step, carry):
        @pl.when(step < n_tensor)
        def _():
            prepare(step)
            for pair in range(group // (2 * HEAD_DIM)):
                pair_back(step, pair)
                low, high = jnp.int32(0), jnp.int32(0)
                for s, (begin, end) in enumerate(PLAN[pair]):
                    low, high = jnp.where(step == s, begin, low), jnp.where(step == s, end, high)
                lax.fori_loop(low, high, run, 0)

            exchange(step)

        @pl.when(step >= 1)
        def _():
            collect(step - 1)

            @pl.when(step < n_tensor - 1)
            def _():
                weights(0, step + 1, lax.rem(step + 1, 2)).start()

        return carry

    lax.fori_loop(0, n_tensor + 1, attention, 0)

    cot_v[...] = acc[...].astype(BF)
    send_output(1, cot_v)
    for j in range(SMALL):
        send_or_keep(
            me == j,
            small_v.at[j],
            small_in.at[me],
            b_s.at[j],
            b_r.at[me],
            (j // n_tensor, j % n_tensor),
        )
    def drain(index, carry):
        advance(index)
        return carry

    lax.fori_loop(LAST, pieces, drain, 0)

    @pl.when(me < SMALL)
    def _():
        def arrive(step, total):
            landed(small_in.at[0], b_r.at[step])
            return total + small_in[step]

        total = lax.fori_loop(0, count, arrive, jnp.zeros(small_in.shape[1:], F32))
        small_in[0] = total
        pltpu.make_async_copy(small_in.at[0], small_out.at[me], bo_r.at[me]).start()

        def spread(step, carry):
            other = lax.rem(me + step, count)
            remote(
                small_in.at[0],
                small_out.at[me],
                bo_s.at[step],
                bo_r.at[me],
                (lax.div(other, n_tensor), lax.rem(other, n_tensor)),
            ).start()
            return carry

        lax.fori_loop(1, count, spread, 0)

    lax.fori_loop(pieces, pieces + 1 + bits + DEEP, drain, 0)

    for k in range(KINDS):
        total = from_z[k, n_tensor - 1].astype(F32)
        landed(from_z.at[0, 0], z_r.at[(KINDS - 1 - k) * n_tensor + 2])
        total = total + from_z[k, 2].astype(F32)
        acc[k * rows : (k + 1) * rows] = total
        pltpu.make_async_copy(acc.at[pl.ds(k * rows, rows)], sum_ref.at[k], out_sem.at[k]).start()
    for k in range(KINDS):
        landed(acc.at[pl.ds(0, rows)], out_sem.at[k])

    for k in range(KINDS):
        for tt in range(n_tensor):
            relayed(k, tt)
            for half in range(2):
                half_rows = full_ref.at[k, tt, pl.ds(0, width // 2), pl.ds(0, half_cols)]
                landed(half_rows, sib_s.at[k, tt, half])
                if chips > 1:
                    most = full_ref.at[k, tt, pl.ds(0, width // 2 - rows), pl.ds(0, half_cols)]
                    landed(most, gxy_s.at[k, tt, half])
    for s in range(2):
        sent((lax.div(t, half_t) == core) & (2 * core + s == t), x_ref.at[s], x_s.at[s])
    for step in range(1, n_tensor):
        landed(bias_ref, bz_s.at[step])
    for tt in range(n_tensor):
        for j in range(2):
            landed(q_v.at[tt], kv_s.at[tt, j])
    for step in range(1, n_dp):
        landed(c_one.at[0], c1_s.at[step])
    for step in range(2 * n_dp):
        seq = lax.rem(4 * chip + step, 2 * n_dp)
        goal = 2 * lax.div(seq, 4) + lax.div(t, half_t)
        sent((goal == d) & (lax.rem(seq, 4) == t), c_two.at[0], c2_s.at[step])
    for j in range(SMALL):
        landed(small_v.at[0], bo_r.at[j])
        sent(me == j, small_v.at[0], b_s.at[j])

    @pl.when(me < SMALL)
    def _():
        def gone(step, carry):
            landed(small_v.at[0], bo_s.at[step])
            return carry

        lax.fori_loop(1, count, gone, 0)

    for a in range(2):
        for q in range(2):
            sent((lax.div(t, half_t) == core) & (2 * core + q == t), x_ref.at[q], y_s.at[a, q])
            landed(x_ref.at[q], y_r.at[a, q])
    for step in range(n_tensor - 2, n_tensor):
        for j in range(2):
            landed(dkv_in.at[0, 0], dkv_s.at[step, j])
    for index in range(pieces - 2, pieces):
        landed(outbox.at[0], core_s.at[index])
    for index in range(pieces - SLOTS, pieces):
        for half in range(2):
            landed(from_chip.at[0, 0], xy_s.at[index, half])
        if index % n_tensor < n_tensor - 1:
            landed(from_z.at[0, 0], z_s.at[index])


def gauss(u):
    size = jnp.abs(u)
    bell = 0.3989422804014327 * jnp.exp(-0.5 * (u * u))
    s = 1.0 / (1.0 + 0.23164190 * size)
    tail = bell * s * (
        0.319381530 + s * (-0.356563782 + s * (1.781477937 + s * (-1.821255978 + s * 1.330274429)))
    )
    return bell, jnp.where(u < 0, tail, 1.0 - tail)


def run_layer(n_dp, n_tensor, undealing, lengths, vecs, x_in, cot_in, shard, biases):
    slots, span, width = x_in.shape
    rows, cols = shard.shape[1:]
    chips = n_dp // 2
    tokens = 2 * span
    group = cols // 4
    n_pos = min(n_dp, span // 16)
    prow, pcol = span // n_pos, width // (n_dp // n_pos)
    pieces = KINDS * n_tensor
    count = n_dp * n_tensor
    dma = pltpu.SemaphoreType.DMA
    any_space = pl.BlockSpec(memory_space=pl.ANY)
    smem = pl.BlockSpec(memory_space=pltpu.SMEM)
    vmem = pl.BlockSpec(memory_space=pltpu.VMEM)
    shapes = (
        ((KINDS, n_tensor, width, cols), BF),
        ((KINDS, rows, cols), F32),
        ((SMALL, 8, 128), F32),
        ((2, 2, span, width), BF),
    )
    return pl.pallas_call(
        functools.partial(layer_kernel, n_dp, n_tensor),
        out_shape=tuple(jax.ShapeDtypeStruct(*shape) for shape in shapes),
        in_specs=[smem, smem, vmem, any_space, any_space, vmem, vmem],
        out_specs=(any_space, any_space, any_space, any_space),
        scratch_shapes=[
            pltpu.VMEM((n_dp, slots, prow, pcol), BF),
            pltpu.VMEM((2 * n_dp, prow, pcol), BF),
            pltpu.VMEM((n_tensor,) + biases.shape, F32),
            pltpu.VMEM((2, width, cols), BF),
            pltpu.VMEM((n_tensor, tokens, group), BF),
            pltpu.VMEM((n_tensor, 2 * tokens, group), BF),
            pltpu.VMEM((n_tensor, 2 * tokens, group), BF),
            pltpu.VMEM((4, 2, width // 2, tokens), BF),
            pltpu.VMEM((KINDS, n_tensor, tokens, cols), BF),
            pltpu.VMEM((tokens, width), BF),
            pltpu.VMEM((tokens, width), BF),
            pltpu.VMEM((tokens, width), BF),
            pltpu.VMEM((tokens, width), BF),
            pltpu.VMEM((tokens, width), F32),
            pltpu.VMEM((tokens, 128), F32),
            pltpu.VMEM((128, tokens), F32),
            pltpu.VMEM((2, tokens, 128), F32),
            pltpu.VMEM((tokens, group), BF),
            pltpu.VMEM((8, tokens), F32),
            pltpu.VMEM((2 * HEAD_DIM, tokens), F32),
            pltpu.VMEM((2 * HEAD_DIM, 2 * tokens), BF),
            pltpu.VMEM((2, 2, 2 * tokens, group), BF),
            pltpu.VMEM((n_tensor, 2, tokens, group), BF),
            pltpu.VMEM((2, width // 2, cols), BF),
            pltpu.VMEM((4, width // 2, cols), BF),
            pltpu.VMEM((SLOTS, width // 2, cols), BF),
            pltpu.VMEM((SLOTS, 2, max(chips - 1, 1), rows, cols // 2), BF),
            pltpu.VMEM((KINDS, n_tensor, rows, cols), BF),
            pltpu.VMEM((SMALL, 8, 128), F32),
            pltpu.VMEM((count, 8, 128), F32),
            dma((2,)),
            dma((2,)),
            dma((n_dp,)),
            dma((n_dp,)),
            dma((2 * n_dp,)),
            dma((n_tensor // 2, n_dp)),
            dma((KINDS,)),
            dma((KINDS, n_tensor, 2)),
            dma((KINDS, n_tensor)),
            dma((KINDS, n_tensor, 2)),
            dma((KINDS, n_tensor, 2, chips)),
            dma((KINDS, n_tensor, 2)),
            dma((KINDS, n_tensor, 2, chips)),
            dma((n_tensor, 2)),
            dma((n_tensor, 2)),
            dma((n_tensor,)),
            dma((n_tensor,)),
            dma((2,)),
            dma((n_tensor, 2)),
            dma((n_tensor, 2)),
            dma((2, 2)),
            dma((2, 2)),
            dma((SMALL,)),
            dma((count,)),
            dma((count,)),
            dma((SMALL,)),
            dma((pieces,)),
            dma((pieces,)),
            dma((pieces, 2)),
            dma((pieces, 2, chips)),
            dma((pieces,)),
            dma((pieces,)),
            dma((KINDS,)),
        ],
        compiler_params=pltpu.CompilerParams(
            collective_id=0, has_side_effects=True, vmem_limit_bytes=VMEM_LIMIT
        ),
        name="encoder_layer",
    )(undealing, lengths, vecs, x_in, cot_in, shard, biases)


def shards(
    n_dp,
    n_tensor,
    inputs,
    cotangent,
    lengths,
    dealing,
    undealing,
    query_weight,
    key_weight,
    value_weight,
    output_weight,
    up_weight,
    down_weight,
    query_bias,
    value_bias,
    output_bias,
    up_bias,
    down_bias,
    first_gain,
    first_shift,
    second_gain,
    second_shift,
):
    span, slots, width = inputs.shape
    group = query_weight.shape[1]
    shard = jnp.stack(
        [
            jnp.concatenate([query_weight, key_weight, value_weight, output_weight.T], axis=1),
            up_weight,
            down_weight.T,
        ]
    ).astype(BF)
    blank = jnp.zeros((group,), F32)
    biases = jnp.concatenate([query_bias, value_bias, up_bias, blank, blank]).reshape(8, group)
    vecs = jnp.stack([output_bias, down_bias, first_gain, first_shift, second_gain, second_shift])
    vecs = jnp.pad(vecs, ((0, 2), (0, 0)))
    _, sums, small, returned = run_layer(
        n_dp,
        n_tensor,
        undealing,
        lengths,
        vecs,
        jnp.transpose(inputs, (1, 0, 2)),
        jnp.transpose(cotangent, (1, 0, 2)),
        shard,
        biases,
    )
    returned = jnp.transpose(returned, (0, 2, 1, 3))
    small = small.reshape(SMALL, width)
    t = lax.axis_index("tensor")

    def mine(row):
        return lax.dynamic_slice(small[row], (t * group,), (group,))

    return (
        returned[0],
        returned[1],
        sums[0][:, :group],
        sums[0][:, group : 2 * group],
        sums[0][:, 2 * group : 3 * group],
        sums[0][:, 3 * group :].T,
        sums[1],
        sums[2].T,
        mine(0),
        mine(1),
        small[2],
        lax.dynamic_index_in_dim(small, 3 + t, 0, keepdims=False),
        small[7],
        small[8],
        small[9],
        small[10],
        small[11],
    )


def solution(mesh):
    tokens = P("tensor", "dp", None)
    rows, columns = P("dp", "tensor"), P("tensor", "dp")
    split, copied = P("tensor"), P()
    return jax.shard_map(
        functools.partial(shards, mesh.shape["dp"], mesh.shape["tensor"]),
        mesh=mesh,
        in_specs=(
            (tokens, tokens, copied, copied, copied)
            + (rows, rows, rows, columns, rows, columns)
            + (split, split, copied, split, copied, copied, copied, copied, copied)
        ),
        out_specs=(
            (tokens, tokens, rows, rows, rows, columns, rows, columns)
            + (split, split, copied, split, copied, copied, copied, copied, copied)
        ),
        check_vma=False,
    )
```
